32 devices in a mesh: rows: 8 (over y, x, core), seq: 4 (over z).
Axes of the slice: x: 2, y: 2, z: 4, core: 2. Of those that a mesh axis runs over, the one named last changes fastest.
Arguments:
- canvas: bfloat16 [8, 2048, 512], P('rows', 'seq'), may hold values from -6 to 6
- memory: bfloat16 [8, 512, 512], P('rows', 'seq'), may hold values from -6 to 6
- cotangent: bfloat16 [8, 2048, 512], P('rows', 'seq'), may hold values from -6 to 6
- canvas_lengths: int32 [8], P('rows'), may hold values from 1844 to 2048, as said below
- canvas_segments: int32 [8, 2048], P('rows', 'seq'), may hold values from 0 to 3, as said below
- memory_segments: int32 [8, 512], P('rows', 'seq'), may hold values from 0 to 3, as said below
- memory_lengths: int32 [8], P('rows'), may hold values from 448 to 512, as said below
- self_query: bfloat16 [512, 512], replicated, may hold values from -0.25 to 0.25
- self_key: bfloat16 [512, 512], replicated, may hold values from -0.25 to 0.25
- self_value: bfloat16 [512, 512], replicated, may hold values from -0.25 to 0.25
- self_output: bfloat16 [512, 512], replicated, may hold values from -1.5 to 1.5
- self_query_bias: bfloat16 [512], replicated, may hold values from -2 to 2
- self_value_bias: bfloat16 [512], replicated, may hold values from -2 to 2
- self_output_bias: bfloat16 [512], replicated, may hold values from -2 to 2
- first_gain: bfloat16 [512], replicated, may hold values from 0.25 to 1.75
- first_bias: bfloat16 [512], replicated, may hold values from -2 to 2
- cross_query: bfloat16 [512, 512], replicated, may hold values from -0.25 to 0.25
- cross_key: bfloat16 [512, 512], replicated, may hold values from -0.25 to 0.25
- cross_value: bfloat16 [512, 512], replicated, may hold values from -0.25 to 0.25
- cross_output: bfloat16 [512, 512], replicated, may hold values from -1 to 1
- cross_query_bias: bfloat16 [512], replicated, may hold values from -2 to 2
- cross_value_bias: bfloat16 [512], replicated, may hold values from -2 to 2
- cross_output_bias: bfloat16 [512], replicated, may hold values from -2 to 2
- second_gain: bfloat16 [512], replicated, may hold values from 0.25 to 1.75
- second_bias: bfloat16 [512], replicated, may hold values from -2 to 2
- expand_weight: bfloat16 [512, 2048], replicated, may hold values from -0.25 to 0.25
- expand_bias: bfloat16 [2048], replicated, may hold values from -2 to 2
- reduce_weight: bfloat16 [2048, 512], replicated, may hold values from -0.125 to 0.125
- reduce_bias: bfloat16 [512], replicated, may hold values from -2 to 2
- third_gain: bfloat16 [512], replicated, may hold values from 0.25 to 1.75
- third_bias: bfloat16 [512], replicated, may hold values from -2 to 2
- slot_weight: bfloat16 [1024, 512], replicated, may hold values from -0.1875 to 0.1875
- slot_bias: bfloat16 [512], replicated, may hold values from -2 to 2
Outputs:
- slot_states: bfloat16 [8, 2048, 512], P('rows', 'seq')
- canvas_grad: float32 [8, 2048, 512], P('rows', 'seq')
- memory_grad: float32 [8, 512, 512], P('rows', 'seq')
- grad_self_query: float32 [512, 512], replicated
- grad_self_key: float32 [512, 512], replicated
- grad_self_value: float32 [512, 512], replicated
- grad_self_output: float32 [512, 512], replicated
- grad_self_query_bias: float32 [512], replicated
- grad_self_value_bias: float32 [512], replicated
- grad_self_output_bias: float32 [512], replicated
- grad_first_gain: float32 [512], replicated
- grad_first_bias: float32 [512], replicated
- grad_cross_query: float32 [512, 512], replicated
- grad_cross_key: float32 [512, 512], replicated
- grad_cross_value: float32 [512, 512], replicated
- grad_cross_output: float32 [512, 512], replicated
- grad_cross_query_bias: float32 [512], replicated
- grad_cross_value_bias: float32 [512], replicated
- grad_cross_output_bias: float32 [512], replicated
- grad_second_gain: float32 [512], replicated
- grad_second_bias: float32 [512], replicated
- grad_expand_weight: float32 [512, 2048], replicated
- grad_expand_bias: float32 [2048], replicated
- grad_reduce_weight: float32 [2048, 512], replicated
- grad_reduce_bias: float32 [512], replicated
- grad_third_gain: float32 [512], replicated
- grad_third_bias: float32 [512], replicated
- grad_slot_weight: float32 [1024, 512], replicated
- grad_slot_bias: float32 [512], replicated
The draws below stay inside these ranges and needn't reach their ends.
Inputs may be any that keep to these rules, and one draw needn't show every extreme that they name: `canvas_lengths`: some row is full; every canvas has live positions. `canvas_segments`: never falls along a row; each of the 4 canvases holds 256 to 1024 positions, one exactly 1024. `memory_segments`: never falls along a row; canvas k begins within 32 positions of k * 128. `memory_lengths`: some row is full; every canvas has live memory positions.
All inputs are finite; a program needn't handle non-finite values.
Results may differ from the reference program's by a relative error of at most 0.024.
Values may be sent and summed in bfloat16 or wider, within the bound.
No kernel may reach another device: no remote copies, remote signals or barrier semaphores. Data moves between devices by JAX's collectives and lax.ppermute only.
A program may use at most 192 MiB of HBM per device.

```python
import jax
import jax.numpy as jnp
from jax import lax

D = 512
H = 8
HD = 64
FF = 2048
ROW_LEN = 2048
MEM_LEN = 512
NSEG = 4
ROWS = 8


def draw_canvas_lengths(key, part):
    cuts = jax.random.randint(jax.random.fold_in(key, 1), (ROWS,), 0, ROW_LEN // 10 + 1)
    chosen = jax.random.randint(jax.random.fold_in(key, 2), (), 0, ROWS)
    lengths = ROW_LEN - cuts
    return jnp.where(jnp.arange(ROWS) == chosen, ROW_LEN, lengths).astype(jnp.int32)


def draw_canvas_segments(key, part):
    eighth = ROW_LEN // 8
    sixteenth = ROW_LEN // 16
    first_len = jax.random.randint(jax.random.fold_in(key, 11), (ROWS,), eighth, eighth + sixteenth + 1)
    second_len = jax.random.randint(jax.random.fold_in(key, 12), (ROWS,), eighth, eighth + sixteenth + 1)
    third_len = ROW_LEN // 2 - first_len - second_len
    longest_at = jax.random.randint(jax.random.fold_in(key, 13), (ROWS,), 0, 4)
    others = jnp.stack([first_len, second_len, third_len], axis=1)
    slots = jnp.arange(4, dtype=jnp.int32)[None, :]
    pick = jnp.clip(slots - (slots > longest_at[:, None]).astype(jnp.int32), 0, 2)
    taken = jnp.sum(jnp.where(pick[:, :, None] == jnp.arange(3, dtype=jnp.int32)[None, None, :], others[:, None, :], 0), axis=-1)
    sizes = jnp.where(slots == longest_at[:, None], ROW_LEN // 2, taken).astype(jnp.int32)
    ends = jnp.cumsum(sizes, axis=1).astype(jnp.int32)
    places = jnp.arange(ROW_LEN, dtype=jnp.int32)
    above = (places[None, :, None] >= ends[:, None, :3]).astype(jnp.int32)
    return jnp.sum(above, axis=-1).astype(jnp.int32)


def draw_memory_segments(key, part):
    stride = MEM_LEN // NSEG
    jitter = stride // 4
    moves = jax.random.randint(jax.random.fold_in(key, 3), (ROWS, NSEG - 1), -jitter, jitter + 1)
    starts = (jnp.arange(1, NSEG, dtype=jnp.int32) * stride)[None, :] + moves
    places = jnp.arange(MEM_LEN, dtype=jnp.int32)
    above = (places[None, :, None] >= starts[:, None, :]).astype(jnp.int32)
    return jnp.sum(above, axis=-1).astype(jnp.int32)


def draw_memory_lengths(key, part):
    stride = MEM_LEN // NSEG
    cuts = jax.random.randint(jax.random.fold_in(key, 5), (ROWS,), 0, stride // 2 + 1)
    chosen = jax.random.randint(jax.random.fold_in(key, 6), (), 0, ROWS)
    lengths = MEM_LEN - cuts
    return jnp.where(jnp.arange(ROWS) == chosen, MEM_LEN, lengths).astype(jnp.int32)


def level_of(rng, shape, split, smallest, high):
    def one(position, parts):
        steps = jax.random.uniform(jax.random.fold_in(jax.random.fold_in(rng, 6), position), (parts,), jnp.float32, smallest / len(split), high / len(split))
        return jnp.repeat(jnp.exp(steps), shape[position] // parts).reshape((-1,) + (1,) * (len(shape) - position - 1))

    level = one(*split[0])
    for cut in split[1:]:
        level = level * one(*cut)
    return level


def normal_values(key, dims, scale, reach, cuts=(), kind=jnp.bfloat16):
    factor_of = level_of(key, dims, cuts, -0.22, 0.18) if cuts else 1.0
    entries = jax.random.normal(key, dims, jnp.float32) * scale * factor_of
    return jnp.minimum(jnp.maximum(entries, -reach), reach).astype(kind)


def setup_inputs(seed: int = 0) -> dict:
    key_list = jax.random.split(jax.random.key(seed), 34)
    canvas = normal_values(key_list[0], (ROWS, ROW_LEN, D), 1.0, 6.0, ((0, 8), (1, 4)))
    memory = normal_values(key_list[1], (ROWS, MEM_LEN, D), 1.0, 6.0, ((0, 8), (1, 4)))
    cotangent = normal_values(key_list[2], (ROWS, ROW_LEN, D), 1.0, 6.0, ((0, 8), (1, 4)))
    canvas_lengths = draw_canvas_lengths(jax.random.fold_in(key_list[33], 71), 0)
    canvas_segments = draw_canvas_segments(jax.random.fold_in(key_list[33], 71), 0)
    memory_segments = draw_memory_segments(jax.random.fold_in(key_list[33], 71), 0)
    memory_lengths = draw_memory_lengths(jax.random.fold_in(key_list[33], 71), 0)
    self_query = normal_values(key_list[7], (D, D), D ** -0.5, 0.25)
    self_key = normal_values(key_list[8], (D, D), D ** -0.5, 0.25)
    self_value = normal_values(key_list[9], (D, D), D ** -0.5, 0.25)
    self_output = normal_values(key_list[10], (D, D), (D // 32) ** -0.5, 1.5)
    self_query_bias = normal_values(key_list[11], (D,), 0.3, 2.0)
    self_value_bias = normal_values(key_list[12], (D,), 0.3, 2.0)
    self_output_bias = normal_values(key_list[13], (D,), 0.3, 2.0)
    first_gain = jnp.clip(1.0 + 0.15 * jax.random.normal(key_list[14], (D,), jnp.float32), 0.25, 1.75).astype(jnp.bfloat16)
    first_bias = normal_values(key_list[15], (D,), 0.3, 2.0)
    cross_query = normal_values(key_list[16], (D, D), D ** -0.5, 0.25)
    cross_key = normal_values(key_list[17], (D, D), D ** -0.5, 0.25)
    cross_value = normal_values(key_list[18], (D, D), D ** -0.5, 0.25)
    cross_output = normal_values(key_list[19], (D, D), (D // 16) ** -0.5, 1.0)
    cross_query_bias = normal_values(key_list[20], (D,), 0.3, 2.0)
    cross_value_bias = normal_values(key_list[21], (D,), 0.3, 2.0)
    cross_output_bias = normal_values(key_list[22], (D,), 0.3, 2.0)
    second_gain = jnp.clip(1.0 + 0.15 * jax.random.normal(key_list[23], (D,), jnp.float32), 0.25, 1.75).astype(jnp.bfloat16)
    second_bias = normal_values(key_list[24], (D,), 0.3, 2.0)
    expand_weight = normal_values(key_list[25], (D, FF), D ** -0.5, 0.25)
    expand_bias = normal_values(key_list[26], (FF,), 0.3, 2.0)
    reduce_weight = normal_values(key_list[27], (FF, D), FF ** -0.5, 0.125)
    reduce_bias = normal_values(key_list[28], (D,), 0.3, 2.0)
    third_gain = jnp.clip(1.0 + 0.15 * jax.random.normal(key_list[29], (D,), jnp.float32), 0.25, 1.75).astype(jnp.bfloat16)
    third_bias = normal_values(key_list[30], (D,), 0.3, 2.0)
    slot_weight = normal_values(key_list[31], (2 * D, D), (2 * D) ** -0.5, 0.1875)
    slot_bias = normal_values(key_list[32], (D,), 0.3, 2.0)
    return dict(canvas=canvas, memory=memory, cotangent=cotangent, canvas_lengths=canvas_lengths, canvas_segments=canvas_segments, memory_segments=memory_segments, memory_lengths=memory_lengths, self_query=self_query, self_key=self_key, self_value=self_value, self_output=self_output, self_query_bias=self_query_bias, self_value_bias=self_value_bias, self_output_bias=self_output_bias, first_gain=first_gain, first_bias=first_bias, cross_query=cross_query, cross_key=cross_key, cross_value=cross_value, cross_output=cross_output, cross_query_bias=cross_query_bias, cross_value_bias=cross_value_bias, cross_output_bias=cross_output_bias, second_gain=second_gain, second_bias=second_bias, expand_weight=expand_weight, expand_bias=expand_bias, reduce_weight=reduce_weight, reduce_bias=reduce_bias, third_gain=third_gain, third_bias=third_bias, slot_weight=slot_weight, slot_bias=slot_bias)


@jax.custom_vjp
def low(v):
    return lax.optimization_barrier(v.astype(jnp.bfloat16)).astype(jnp.float32)

@jax.custom_vjp
def low_back(v):
    return v

def low_keep(v):
    return (low(v), None)

def low_pass(kept, grad):
    return (grad,)

def back_keep(v):
    return (v, None)

def back_low(kept, grad):
    return (low(grad),)
low.defvjp(low_keep, low_pass)
low_back.defvjp(back_keep, back_low)
masked_score = -30000.0
epsilon = 1e-05
gelu_scale = 0.7978845608028654
gelu_cubic = 0.044715
highest = lax.Precision.HIGHEST

def smooth_gate(inputs):
    return 0.5 * inputs * (1.0 + jnp.tanh(gelu_scale * (inputs + gelu_cubic * inputs * inputs * inputs)))

def matmul(left, right):
    return jnp.dot(left, right, precision=highest, preferred_element_type=jnp.float32)

def layer_norm(inputs, norm_gain, norm_shift):
    average = lax.optimization_barrier(jnp.mean(inputs, axis=-1, keepdims=True))
    centred = inputs - average
    variance = lax.optimization_barrier(jnp.mean(centred * centred, axis=-1, keepdims=True))
    return centred * lax.rsqrt(variance + epsilon) * norm_gain + norm_shift

def attend(queries, query_code, key_rows, values, key_code):
    length = queries.shape[0]
    block_rows = min(512, length)
    block_count = length // block_rows
    key_heads = key_rows.reshape(key_rows.shape[0], H, HD)
    value_heads = values.reshape(values.shape[0], H, HD)

    def one_block(pieces):
        query_block, code_block = pieces
        query_heads = query_block.reshape(block_rows, H, HD)
        scores = jnp.einsum('qhd,khd->hqk', query_heads, key_heads, precision=highest)
        scores = low_back(scores)
        visible = code_block[:, None] == key_code[None, :]
        masked = jnp.where(visible[None], scores, masked_score)
        summit = lax.optimization_barrier(jnp.max(masked, axis=-1, keepdims=True))
        powers = jnp.exp(masked - summit)
        chances = powers / lax.optimization_barrier(jnp.sum(powers, axis=-1, keepdims=True))
        blended = jnp.einsum('hqk,khd->qhd', low(chances), value_heads, precision=highest)
        return blended.reshape(block_rows, H * HD)
    blocks = lax.map(jax.checkpoint(one_block), (queries.reshape(block_count, block_rows, -1), query_code.reshape(block_count, block_rows)))
    return blocks.reshape(length, -1)

def row_forward(params, canvas_row, memory_row, canvas_code, key_code, memory_code, slot_valid):
    self_query, self_key, self_value, self_output, self_query_bias, self_value_bias, self_output_bias, first_gain, first_bias, cross_query, cross_key, cross_value, cross_output, cross_query_bias, cross_value_bias, cross_output_bias, second_gain, second_bias, expand_weight, expand_bias, reduce_weight, reduce_bias, third_gain, third_bias, slot_weight, slot_bias = params
    queries = low(low_back((matmul(canvas_row, self_query) + self_query_bias) * 0.125))
    key_rows = low(low_back(matmul(canvas_row, self_key)))
    values = low(low_back(matmul(canvas_row, self_value) + self_value_bias))
    blended = attend(queries, canvas_code, key_rows, values, key_code)
    attended = low_back(matmul(low(low_back(blended)), self_output) + self_output_bias)
    first = layer_norm(canvas_row + attended, first_gain, first_bias)
    first_low = low(first)
    cross_rows = low(low_back((matmul(first_low, cross_query) + cross_query_bias) * 0.125))
    memory_keys = low(low_back(matmul(memory_row, cross_key)))
    memory_values = low(low_back(matmul(memory_row, cross_value) + cross_value_bias))
    fetched = attend(cross_rows, canvas_code, memory_keys, memory_values, memory_code)
    crossed = low_back(matmul(low(low_back(fetched)), cross_output) + cross_output_bias)
    second = layer_norm(first + crossed, second_gain, second_bias)
    before = low_back(matmul(low(second), expand_weight) + expand_bias)
    hidden = low(low_back(smooth_gate(before)))
    reduced = low_back(matmul(hidden, reduce_weight) + reduce_bias)
    third = layer_norm(second + reduced, third_gain, third_bias)
    states = low(third)
    width = states.shape[1]
    following = low_back(jnp.concatenate([states[1:], jnp.zeros((1, width), jnp.float32)], axis=0))
    slots = matmul(states, slot_weight[:width]) + matmul(following, slot_weight[width:]) + slot_bias
    return slots * slot_valid[:, None]

def reference(canvas, memory, cotangent, canvas_lengths, canvas_segments, memory_segments, memory_lengths, self_query, self_key, self_value, self_output, self_query_bias, self_value_bias, self_output_bias, first_gain, first_bias, cross_query, cross_key, cross_value, cross_output, cross_query_bias, cross_value_bias, cross_output_bias, second_gain, second_bias, expand_weight, expand_bias, reduce_weight, reduce_bias, third_gain, third_bias, slot_weight, slot_bias):
    params = tuple((weight.astype(jnp.float32) for weight in (self_query, self_key, self_value, self_output, self_query_bias, self_value_bias, self_output_bias, first_gain, first_bias, cross_query, cross_key, cross_value, cross_output, cross_query_bias, cross_value_bias, cross_output_bias, second_gain, second_bias, expand_weight, expand_bias, reduce_weight, reduce_bias, third_gain, third_bias, slot_weight, slot_bias)))
    positions = jnp.arange(ROW_LEN, dtype=jnp.int32)
    memory_places = jnp.arange(MEM_LEN, dtype=jnp.int32)

    def per_row(totals, row_data):
        canvas_row, memory_row, cotangent_row, length, segments, memory_segs, memory_length = row_data
        live_mask = positions < length
        key_code = jnp.where(live_mask, segments, -1).astype(jnp.int32)
        memory_code = jnp.where(memory_places < memory_length, memory_segs, -1).astype(jnp.int32)
        next_code = jnp.concatenate([key_code[1:], jnp.full((1,), -1, jnp.int32)])
        slot_valid = jnp.where(next_code == segments, 1.0, 0.0).astype(jnp.float32)

        def row_function(weights, canvas_part, memory_part):
            return row_forward(weights, canvas_part, memory_part, segments, key_code, memory_code, slot_valid)
        slots, pullback = jax.vjp(row_function, params, canvas_row.astype(jnp.float32), memory_row.astype(jnp.float32))
        weight_grads, canvas_part_grad, memory_part_grad = pullback(cotangent_row.astype(jnp.float32))
        totals = jax.tree.map(jnp.add, totals, weight_grads)
        return (totals, (slots.astype(jnp.bfloat16), canvas_part_grad, memory_part_grad))
    starting = jax.tree.map(jnp.zeros_like, params)
    totals, outputs = lax.scan(per_row, starting, (canvas, memory, cotangent, canvas_lengths, canvas_segments, memory_segments, memory_lengths))
    slot_states, canvas_grad, memory_grad = outputs
    return (slot_states, canvas_grad, memory_grad, totals[0], totals[1], totals[2], totals[3], totals[4], totals[5], totals[6], totals[7], totals[8], totals[9], totals[10], totals[11], totals[12], totals[13], totals[14], totals[15], totals[16], totals[17], totals[18], totals[19], totals[20], totals[21], totals[22], totals[23], totals[24], totals[25])
```

```python
import functools

import jax
import jax.numpy as jnp
from jax import lax
from jax.experimental import pallas as pl
from jax.experimental.pallas import tpu as pltpu
from jax.sharding import PartitionSpec as P

H = 8
HD = 64
PAIRS = H // 2
TILE = 256
TAIL = 16
VROWS = 80
ROOM = 60 * 1024 * 1024

masked_score = -30000.0
epsilon = 1e-05
gelu_scale = 0.7978845608028654
gelu_cubic = 0.044715
safe_square = 3600.0
bf16 = jnp.bfloat16
f32 = jnp.float32


def matmul(left, right):
    return jnp.dot(left, right, preferred_element_type=f32)


def times_transposed(left, right):
    return lax.dot_general(left, right, (((1,), (1,)), ((), ())), preferred_element_type=f32)


def bfloat(values):
    return values.astype(bf16)


def widen(values):
    return values.astype(f32)


def head_rows(dtype):
    row = lax.broadcasted_iota(jnp.int32, (16, H * HD), 0)
    column = lax.broadcasted_iota(jnp.int32, (16, H * HD), 1)
    return jnp.where(column // HD == row, 1.0, 0.0).astype(dtype)


def one_head(pair_columns, side):
    lane = lax.broadcasted_iota(jnp.int32, pair_columns.shape, 1)
    wanted = lane < HD if side == 0 else lane >= HD
    return jnp.where(wanted, widen(pair_columns), 0.0).astype(bf16)


def gather_window(place, blocks, window, tails, codes, keycodes, length, semaphores, T):
    own, side, middle, middle_far, side_far = blocks
    inner = jnp.logical_or(place == 1, place == 2)
    beside = place + 1 - 2 * lax.rem(place, 2)
    across = 3 - place
    across_beside = across + 1 - 2 * lax.rem(across, 2)

    def move(block, slot, index):
        return (
            pltpu.make_async_copy(block.at[pl.ds(0, T)], window.at[slot], semaphores.at[2 * index]),
            pltpu.make_async_copy(block.at[pl.ds(T, TAIL)], tails.at[slot], semaphores.at[2 * index + 1]),
        )

    lane = lax.broadcasted_iota(jnp.int32, (1, T), 1)
    for slot in range(4):
        fill = jnp.where(slot < place, -8.0, 8.0)
        codes[slot : slot + 1, :] = jnp.full((1, T), 1.0, f32) * fill
        keycodes[slot : slot + 1, :] = jnp.full((1, T), -9.0, f32)
    always = [(own, place, 0), (side, beside, 1)]
    at_inner = [(middle, across, 2), (middle_far, across_beside, 3)]
    at_outer = [(side_far, 3 - beside, 2)]

    def run(moves):
        for m in moves:
            for c in move(*m):
                c.start()

    def finish(moves):
        for m in moves:
            for c in move(*m):
                c.wait()
        for _, slot, _ in moves:
            code = widen(tails[slot, 0:1, 0:T])
            codes[pl.ds(slot, 1), :] = code
            keycodes[pl.ds(slot, 1), :] = jnp.where(slot * T + lane < length, code, -1.0)

    run(always)

    @pl.when(inner)
    def _():
        run(at_inner)

    @pl.when(jnp.logical_not(inner))
    def _():
        run(at_outer)

    finish(always)

    @pl.when(inner)
    def _():
        finish(at_inner)

    @pl.when(jnp.logical_not(inner))
    def _():
        finish(at_outer)


def tile_range(codes, first_code, last_code):
    below = jnp.sum(jnp.where(codes[...] < first_code, 1, 0))
    through = jnp.sum(jnp.where(codes[...] <= last_code, 1, 0))
    return below // TILE, (through + TILE - 1) // TILE


def column_codes(keycodes, columns, tile, T):
    per = T // TILE
    row = keycodes[pl.ds(tile // per, 1), pl.ds(pl.multiple_of(lax.rem(tile, per) * TILE, TILE), TILE)]
    columns[pl.ds(pl.multiple_of(tile * TILE, TILE), TILE), :] = jnp.transpose(
        jnp.broadcast_to(row, (128, TILE))
    )


def self_forward_kernel(
    numbers, segments, own, side, middle, middle_far, side_far, wq, wk, wv, vectors,
    out, queries, lse,
    window, tails, codes, keycodes, columns, keys, values_t, summit, total, blend_t, semaphores,
):
    T, D = out.shape
    place, length = numbers[0], numbers[1]
    gather_window(
        place, (own, side, middle, middle_far, side_far), window, tails, codes, keycodes,
        length, semaphores, T,
    )
    per = T // TILE
    first = segments[0].astype(f32)
    last = segments[T - 1].astype(f32)
    low, high = tile_range(codes, first, last)
    ones_of_heads = head_rows(bf16)
    weights_t = jnp.transpose(wv[...])
    bias_t = as_column(vectors[BV1 : BV1 + 1, :])[:, 0:1]
    rows_q = bfloat((matmul(window[place], wq[...]) + vectors[BQ1 : BQ1 + 1, :]) * 0.125)
    queries[...] = rows_q
    query_reach = jnp.max(times_transposed(ones_of_heads, rows_q * rows_q), axis=1, keepdims=True)

    def project(tile, reach):
        start = pl.multiple_of(tile * TILE, TILE)
        x = window[tile // per, pl.ds(pl.multiple_of(lax.rem(tile, per) * TILE, TILE), TILE), :]
        k = bfloat(matmul(x, wk[...]))
        for pair in range(PAIRS):
            keys[pair, pl.ds(start, TILE), :] = k[:, 128 * pair : 128 * pair + 128]
        v_t = bfloat(times_transposed(weights_t, x) + bias_t)
        for head in range(H):
            values_t[head, 0:HD, pl.ds(start, TILE)] = v_t[HD * head : HD * head + HD]
            values_t[head, HD:VROWS, pl.ds(start, TILE)] = jnp.ones((VROWS - HD, TILE), bf16)
        column_codes(keycodes, columns, tile, T)
        return jnp.maximum(reach, times_transposed(ones_of_heads, k * k))

    key_reach = lax.fori_loop(low, high, project, jnp.zeros((16, TILE), f32))
    reach = jnp.max(query_reach * jnp.max(key_reach, axis=1, keepdims=True))
    wide = reach > safe_square
    summit[...] = jnp.zeros_like(summit)
    total[...] = jnp.zeros_like(total)
    own_codes = codes[pl.ds(place, 1), :]

    for q in range(per):
        span = slice(q * TILE, (q + 1) * TILE)
        tile_first = segments[q * TILE].astype(f32)
        tile_last = segments[(q + 1) * TILE - 1].astype(f32)
        low_q, high_q = tile_range(codes, tile_first, tile_last)
        code_row = own_codes[:, span]

        for pair in range(PAIRS):
            rows = rows_q[span, 128 * pair : 128 * pair + 128]
            sides = [one_head(rows, 0), one_head(rows, 1)]

            def visible_at(start):
                column = columns[pl.ds(start, TILE), :]
                return jnp.concatenate([column] * (TILE // 128), axis=1) == code_row

            def look(tile, _):
                start = pl.multiple_of(tile * TILE, TILE)
                k = keys[pair, pl.ds(start, TILE), :]
                visible = visible_at(start)
                for s in range(2):
                    scores = jnp.where(visible, times_transposed(k, sides[s]), masked_score)
                    head = 2 * pair + s
                    summit[head : head + 1, span] = jnp.maximum(
                        summit[head : head + 1, span], jnp.max(scores, axis=0, keepdims=True)
                    )
                return 0

            @pl.when(wide)
            def _():
                summit[2 * pair : 2 * pair + 2, span] = jnp.full((2, TILE), masked_score, f32)
                lax.fori_loop(low_q, high_q, look, 0)

            def blend(tile, _):
                start = pl.multiple_of(tile * TILE, TILE)
                k = keys[pair, pl.ds(start, TILE), :]
                visible = visible_at(start)
                for s in range(2):
                    head = 2 * pair + s
                    scores = times_transposed(k, sides[s]) - summit[head : head + 1, span]
                    powers = bfloat(jnp.where(visible, jnp.exp(scores), 0.0))
                    total[head, :, span] += matmul(values_t[head, :, pl.ds(start, TILE)], powers)
                return 0

            lax.fori_loop(low_q, high_q, blend, 0)

    for head in range(H):
        mass = total[head, HD : HD + 1, :]
        blend_t[HD * head : HD * head + HD, :] = total[head, 0:HD, :] / mass
        lse[head : head + 1, :] = summit[head : head + 1, :] + jnp.log(mass)
    out[...] = bfloat(jnp.transpose(blend_t[...]))


def self_forward(numbers, segments, blocks, weights):
    T = segments.shape[0]
    D = weights[0].shape[0]
    vmem = pl.BlockSpec(memory_space=pltpu.VMEM)
    smem = pl.BlockSpec(memory_space=pltpu.SMEM)
    hbm = pl.BlockSpec(memory_space=pl.ANY)
    return pl.pallas_call(
        self_forward_kernel,
        out_shape=[
            jax.ShapeDtypeStruct((T, D), bf16),
            jax.ShapeDtypeStruct((T, D), bf16),
            jax.ShapeDtypeStruct((H, T), f32),
        ],
        in_specs=[smem, smem] + [hbm] * 5 + [vmem] * 4,
        out_specs=[vmem] * 3,
        scratch_shapes=[
            pltpu.VMEM((4, T, D), bf16),
            pltpu.VMEM((4, TAIL, D), bf16),
            pltpu.VMEM((4, T), f32),
            pltpu.VMEM((4, T), f32),
            pltpu.VMEM((4 * T, 128), f32),
            pltpu.VMEM((PAIRS, 4 * T, 128), bf16),
            pltpu.VMEM((H, VROWS, 4 * T), bf16),
            pltpu.VMEM((H, T), f32),
            pltpu.VMEM((H, VROWS, T), f32),
            pltpu.VMEM((D, T), f32),
            pltpu.SemaphoreType.DMA((8,)),
        ],
        compiler_params=pltpu.CompilerParams(vmem_limit_bytes=ROOM),
        name="self_forward",
    )(numbers, segments, *blocks, *weights)


def self_backward_kernel(
    numbers, segments, own, side, middle, middle_far, side_far, wq, wk, wv, vectors,
    queries, blended, upstream, lse, entering, sums_one, sums_two,
    canvas_out, first_out, middle_out, side_out, sent, kept,
    window, tails, codes, keycodes, columns, keys, keys_t, values, grad_keys, grad_values,
    query_t, grad_k, grad_v, semaphores,
):
    T, D = queries.shape
    place, length = numbers[0], numbers[1]
    gather_window(
        place, (own, side, middle, middle_far, side_far), window, tails, codes, keycodes,
        length, semaphores, T,
    )
    per = T // TILE
    low, high = tile_range(codes, segments[0].astype(f32), segments[T - 1].astype(f32))
    weights_t = jnp.transpose(wk[...])

    def project(tile, _):
        start = pl.multiple_of(tile * TILE, TILE)
        x = window[tile // per, pl.ds(pl.multiple_of(lax.rem(tile, per) * TILE, TILE), TILE), :]
        k = bfloat(matmul(x, wk[...]))
        v = bfloat(matmul(x, wv[...]) + vectors[BV1 : BV1 + 1, :])
        for pair in range(PAIRS):
            keys[pair, pl.ds(start, TILE), :] = k[:, 128 * pair : 128 * pair + 128]
            values[pair, pl.ds(start, TILE), :] = v[:, 128 * pair : 128 * pair + 128]
            grad_keys[pair, pl.ds(start, TILE), :] = jnp.zeros((TILE, 128), f32)
            grad_values[pair, pl.ds(start, TILE), :] = jnp.zeros((TILE, 128), f32)
        keys_t[:, pl.ds(start, TILE)] = bfloat(times_transposed(weights_t, x))
        column_codes(keycodes, columns, tile, T)
        return 0

    lax.fori_loop(low, high, project, 0)
    own_codes = codes[pl.ds(place, 1), :]
    products = widen(upstream[...]) * widen(blended[...])
    coarse = bfloat(products)
    fine = bfloat(products - widen(coarse))
    ones_of_heads = head_rows(bf16)
    corrections = times_transposed(ones_of_heads, coarse) + times_transposed(ones_of_heads, fine)
    query_t[...] = jnp.zeros_like(query_t)

    for q in range(per):
        span = slice(q * TILE, (q + 1) * TILE)
        tile_first = segments[q * TILE].astype(f32)
        tile_last = segments[(q + 1) * TILE - 1].astype(f32)
        low_q, high_q = tile_range(codes, tile_first, tile_last)
        code_row = own_codes[:, span]
        for pair in range(PAIRS):
            lanes = slice(128 * pair, 128 * pair + 128)
            q_sides = [one_head(queries[span, lanes], s) for s in range(2)]
            u_sides = [one_head(upstream[span, lanes], s) for s in range(2)]

            def step(tile, _):
                start = pl.multiple_of(tile * TILE, TILE)
                k = keys[pair, pl.ds(start, TILE), :]
                v = values[pair, pl.ds(start, TILE), :]
                column = columns[pl.ds(start, TILE), :]
                visible = jnp.concatenate([column] * (TILE // 128), axis=1) == code_row
                key_add = None
                value_add = None
                for s in range(2):
                    head = 2 * pair + s
                    scores = times_transposed(k, q_sides[s]) - lse[head : head + 1, span]
                    chances = jnp.where(visible, jnp.exp(scores), 0.0)
                    chance_grad = times_transposed(v, u_sides[s]) - corrections[head : head + 1, span]
                    score_grad = bfloat(chances * chance_grad)
                    to_values = matmul(bfloat(chances), u_sides[s])
                    to_keys = matmul(score_grad, q_sides[s])
                    value_add = to_values if s == 0 else value_add + to_values
                    key_add = to_keys if s == 0 else key_add + to_keys
                    rows = slice(HD * head, HD * head + HD)
                    query_t[rows, span] += matmul(keys_t[rows, pl.ds(start, TILE)], score_grad)
                grad_keys[pair, pl.ds(start, TILE), :] += key_add
                grad_values[pair, pl.ds(start, TILE), :] += value_add
                return 0

            lax.fori_loop(low_q, high_q, step, 0)

    query_rows = bfloat(jnp.transpose(query_t[...])) * 0.125
    canvas_out[...] = entering[...] + times_transposed(query_rows, wq[...])
    own_t = jnp.transpose(window[place])
    half = kept.shape[0]
    half_side = numbers[3]
    put_block(bfloat(matmul(own_t, query_rows)), 0, half, half_side, sent, kept)
    grad_k[...] = jnp.zeros_like(grad_k)
    grad_v[...] = jnp.zeros_like(grad_v)
    first_out[...] = jnp.zeros_like(first_out)
    middle_out[...] = jnp.zeros_like(middle_out)
    side_out[...] = jnp.zeros_like(side_out)
    inner = jnp.logical_or(place == 1, place == 2)
    beside = place + 1 - 2 * lax.rem(place, 2)
    across = 3 - place
    far = jnp.where(inner, across + 1 - 2 * lax.rem(across, 2), 3 - beside)

    def fold(tile, value_sum):
        start = pl.multiple_of(tile * TILE, TILE)
        block = tile // per
        inside = pl.ds(pl.multiple_of(lax.rem(tile, per) * TILE, TILE), TILE)
        gk = jnp.concatenate([bfloat(grad_keys[pair, pl.ds(start, TILE), :]) for pair in range(PAIRS)], axis=1)
        gv = jnp.concatenate([bfloat(grad_values[pair, pl.ds(start, TILE), :]) for pair in range(PAIRS)], axis=1)
        x_t = jnp.transpose(window[block, inside, :])
        grad_k[...] += matmul(x_t, gk)
        grad_v[...] += matmul(x_t, gv)
        part = times_transposed(gk, wk[...]) + times_transposed(gv, wv[...])

        @pl.when(block == place)
        def _():
            canvas_out[inside, :] += part

        @pl.when(block == far)
        def _():
            first_out[inside, :] = bfloat(part)

        @pl.when(jnp.logical_and(inner, block == across))
        def _():
            middle_out[inside, :] = bfloat(part)

        @pl.when(block == beside)
        def _():
            side_out[inside, :] = bfloat(part)

        return value_sum + summed(gv)

    value_sum = lax.fori_loop(low, high, fold, jnp.zeros((1, D), f32))
    put_block(bfloat(grad_k[...]), D, half, half_side, sent, kept)
    put_block(bfloat(grad_v[...]), 2 * D, half, half_side, sent, kept)
    vector_sums = jnp.concatenate(
        [sums_one[...], sums_two[...], summed(query_rows), value_sum, jnp.zeros((6, D), f32)], axis=0
    )
    put_block(bfloat(vector_sums), 3 * D, half, half_side, sent, kept)
    spare = 2 * half - 3 * D - 32
    put_block(jnp.zeros((spare, D), bf16), 3 * D + 32, half, half_side, sent, kept)


def self_backward(numbers, segments, blocks, weights, queries, blended, upstream, lse, entering, sums_one, sums_two):
    T, D = queries.shape
    vmem = pl.BlockSpec(memory_space=pltpu.VMEM)
    smem = pl.BlockSpec(memory_space=pltpu.SMEM)
    hbm = pl.BlockSpec(memory_space=pl.ANY)
    part = jax.ShapeDtypeStruct((T, D), bf16)
    grad = jax.ShapeDtypeStruct((3 * D // 2 + D // 4, D), bf16)
    return pl.pallas_call(
        self_backward_kernel,
        out_shape=[jax.ShapeDtypeStruct((T, D), f32), part, part, part, grad, grad],
        in_specs=[smem, smem] + [hbm] * 5 + [vmem] * 11,
        out_specs=[vmem] * 6,
        scratch_shapes=[
            pltpu.VMEM((4, T, D), bf16),
            pltpu.VMEM((4, TAIL, D), bf16),
            pltpu.VMEM((4, T), f32),
            pltpu.VMEM((4, T), f32),
            pltpu.VMEM((4 * T, 128), f32),
            pltpu.VMEM((PAIRS, 4 * T, 128), bf16),
            pltpu.VMEM((D, 4 * T), bf16),
            pltpu.VMEM((PAIRS, 4 * T, 128), bf16),
            pltpu.VMEM((PAIRS, 4 * T, 128), f32),
            pltpu.VMEM((PAIRS, 4 * T, 128), f32),
            pltpu.VMEM((D, T), f32),
            pltpu.VMEM((D, D), f32),
            pltpu.VMEM((D, D), f32),
            pltpu.SemaphoreType.DMA((8,)),
        ],
        compiler_params=pltpu.CompilerParams(vmem_limit_bytes=ROOM),
        name="self_backward",
    )(numbers, segments, *blocks, *weights, queries, blended, upstream, lse, entering, sums_one, sums_two)


BQ1, BV1, BO1, G1, B1, BQ2, BV2, BO2, G2, B2, BR, G3, B3, BS, BE = range(15)


def smooth_gate(inputs):
    square = inputs * inputs
    bent = jnp.tanh(gelu_scale * inputs * (1.0 + gelu_cubic * square))
    half = 0.5 * (1.0 + bent)
    slope = half + 0.5 * inputs * (1.0 - bent * bent) * (
        gelu_scale * (1.0 + 3.0 * gelu_cubic * square)
    )
    return inputs * half, slope


def norm_forward(inputs):
    average = jnp.mean(inputs, axis=-1, keepdims=True)
    centred = inputs - average
    scaling = lax.rsqrt(jnp.mean(centred * centred, axis=-1, keepdims=True) + epsilon)
    return centred * scaling, scaling


def norm_backward(upstream, gain, normal, scaling):
    scaled = upstream * gain
    return scaling * (
        scaled
        - jnp.mean(scaled, axis=-1, keepdims=True)
        - normal * jnp.mean(scaled * normal, axis=-1, keepdims=True)
    )


def summed(values):
    return jnp.sum(widen(values), axis=0, keepdims=True)


def as_column(row):
    return jnp.transpose(jnp.broadcast_to(row, (128, row.shape[1])))


def memory_rows(gathered, memory, columns, memory_length):
    count, size, width = gathered.shape
    here = size - TAIL
    lane = lax.broadcasted_iota(jnp.int32, (1, here), 1)
    for b in range(count):
        span = slice(b * here, (b + 1) * here)
        memory[span, :] = gathered[b, 0:here, :]
        code = widen(gathered[b, here : here + 1, 0:here])
        columns[span, :] = as_column(jnp.where(b * here + lane < memory_length, code, -1.0))


def put_block(block, start, half, side, sent, kept):
    size = block.shape[0]
    for part in range(2):
        low, high = max(start, part * half), min(start + size, (part + 1) * half)
        if low >= high:
            continue
        rows = block[low - start : high - start]
        at = slice(low - part * half, high - part * half)

        @pl.when(side == part)
        def _():
            kept[at, :] = rows

        @pl.when(side != part)
        def _():
            sent[at, :] = rows


def forward_kernel(
    numbers, segments, canvas, blended, cotangent, gathered, vectors, side, middle,
    wo_h, cq_h, ck_h, cv_h, co_h, we_h, wr_h, ws_h,
    slots_out, last_out, first_state, normal_out, scaling_out, low_out, query_out, fetched_out,
    lse, second_out, sent, kept, sums,
    wo, cq, ck, cv, co, we, wr, ws, tails, memory, columns, keys, values_t, summit, total,
    blend_t, hidden, slope, second, low2, semaphores,
):
    T, D = canvas.shape
    M = memory.shape[0]
    FF = we.shape[1]
    place, length, memory_length, half_side = numbers[0], numbers[1], numbers[2], numbers[3]
    loads = [
        pltpu.make_async_copy(a, b, semaphores.at[i])
        for i, (a, b) in enumerate(
            [
                (side.at[pl.ds(T, TAIL)], tails.at[0]),
                (middle.at[pl.ds(T, TAIL)], tails.at[1]),
                (wo_h, wo), (ck_h, ck), (cv_h, cv), (cq_h, cq), (co_h, co),
                (we_h, we), (wr_h, wr), (ws_h, ws),
            ]
        )
    ]
    for load in loads:
        load.start()

    def vector(index):
        return vectors[index : index + 1, :]

    sums[...] = jnp.zeros_like(sums)
    code_row = segments[...].astype(f32)

    memory_rows(gathered, memory, columns, memory_length)
    loads[3].wait()
    k = bfloat(matmul(memory[...], ck[...]))
    for pair in range(PAIRS):
        keys[pair] = k[:, 128 * pair : 128 * pair + 128]
    loads[4].wait()
    bias_t = as_column(vector(BV2))[:, 0:1]
    v_t = bfloat(times_transposed(jnp.transpose(cv[...]), memory[...]) + bias_t)
    for head in range(H):
        values_t[head, 0:HD, :] = v_t[HD * head : HD * head + HD]
        values_t[head, HD:VROWS, :] = jnp.ones((VROWS - HD, M), bf16)

    loads[2].wait()
    first_in = widen(canvas[...]) + matmul(blended[...], wo[...]) + vector(BO1)
    normal, scaling = norm_forward(first_in)
    normal_out[...] = normal
    scaling_out[...] = jnp.broadcast_to(scaling, (T, 128))
    first = normal * vector(G1) + vector(B1)
    low = bfloat(first)
    low_out[...] = low
    loads[5].wait()
    query_out[...] = bfloat((matmul(low, cq[...]) + vector(BQ2)) * 0.125)

    ones_of_heads = head_rows(bf16)
    q_all = query_out[...]
    reach = jnp.max(
        jnp.max(times_transposed(ones_of_heads, q_all * q_all), axis=1, keepdims=True)
        * jnp.max(times_transposed(ones_of_heads, k * k), axis=1, keepdims=True)
    )
    wide = reach > safe_square
    summit[...] = jnp.zeros_like(summit)
    total[...] = jnp.zeros_like(total)

    def cross(pair, _):
        lanes = pl.ds(pl.multiple_of(128 * pair, 128), 128)
        for q in range(T // TILE):
            span = slice(q * TILE, (q + 1) * TILE)
            rows = query_out[span, lanes]
            for s in range(2):
                head = 2 * pair + s
                q_side = one_head(rows, s)

                def scores_at(tile):
                    at = slice(tile * TILE, (tile + 1) * TILE)
                    column = columns[at, :]
                    visible = jnp.concatenate([column] * (TILE // 128), axis=1) == code_row[:, span]
                    return at, visible, times_transposed(keys[pair, at, :], q_side)

                @pl.when(wide)
                def _():
                    top = jnp.full((1, TILE), masked_score, f32)
                    for tile in range(M // TILE):
                        _, visible, scores = scores_at(tile)
                        scores = jnp.where(visible, scores, masked_score)
                        top = jnp.maximum(top, jnp.max(scores, axis=0, keepdims=True))
                    summit[pl.ds(head, 1), span] = top

                top = summit[pl.ds(head, 1), span]
                gained = jnp.zeros((VROWS, TILE), f32)
                for tile in range(M // TILE):
                    at, visible, scores = scores_at(tile)
                    powers = bfloat(jnp.where(visible, jnp.exp(scores - top), 0.0))
                    gained += matmul(values_t[head, :, at], powers)
                total[head, :, span] = gained
        return 0

    lax.fori_loop(0, PAIRS, cross, 0)
    for head in range(H):
        mass = total[head, HD : HD + 1, :]
        blend_t[HD * head : HD * head + HD, :] = total[head, 0:HD, :] / mass
        lse[head : head + 1, :] = summit[head : head + 1, :] + jnp.log(mass)
    fetched = bfloat(jnp.transpose(blend_t[...]))
    fetched_out[...] = fetched

    loads[6].wait()
    second_in = first + matmul(fetched, co[...]) + vector(BO2)
    normal2, scaling2 = norm_forward(second_in)
    second[...] = normal2 * vector(G2) + vector(B2)
    low2[...] = bfloat(second[...])
    loads[7].wait()
    loads[8].wait()
    third_in = second[...] + vector(BR)
    for c in range(FF // D):
        lanes = slice(c * D, (c + 1) * D)
        before = matmul(low2[...], we[:, lanes]) + vector(BE + c)
        gate, bend = smooth_gate(before)
        gate = bfloat(gate)
        hidden[:, lanes] = gate
        slope[:, lanes] = bend
        third_in += matmul(gate, wr[lanes, :])
    normal3, scaling3 = norm_forward(third_in)
    states = bfloat(normal3 * vector(G3) + vector(B3))
    first_state[...] = states[0:TAIL]

    loads[0].wait()
    loads[1].wait()
    loads[9].wait()
    inner = jnp.logical_or(place == 1, place == 2)
    beside_tail, across_tail = widen(tails[0]), widen(tails[1])
    after_code = jnp.where(place == 1, across_tail[0:1, 0:1], beside_tail[0:1, 0:1])
    before_code = jnp.where(place == 2, across_tail[0:1, T - 1 : T], beside_tail[0:1, T - 1 : T])
    before_row = jnp.where(place == 2, across_tail[1:2, :], beside_tail[1:2, :])
    lane = lax.broadcasted_iota(jnp.int32, (8, T), 1)
    codes8 = jnp.broadcast_to(code_row, (8, T))
    live = jnp.where(place * T + lane < length, codes8, -1.0)
    next_code = jnp.where(lane == T - 1, after_code, pltpu.roll(live, T - 1, 1))
    valid8 = jnp.where(
        jnp.logical_and(next_code == codes8, place * T + lane + 1 < length), 1.0, 0.0
    )
    valid = as_column(valid8[0:1, :])[:, 0:1]
    last_valid = jnp.where(
        jnp.logical_and(before_code == code_row[:, 0:1], jnp.logical_and(place > 0, place * T < length)),
        1.0, 0.0,
    )
    row = lax.broadcasted_iota(jnp.int32, (T, D), 0)
    following = bfloat(jnp.where(row == T - 1, 0.0, pltpu.roll(widen(states), T - 1, 0)))
    raw = matmul(states, ws[0:D, :]) + vector(BS) + matmul(following, ws[D : 2 * D, :])
    slots_out[...] = bfloat(raw * valid)
    last_out[...] = jnp.concatenate(
        [raw[T - 1 : T], jnp.broadcast_to(valid[T - 1 : T], (1, D)), jnp.zeros((6, D), f32)], axis=0
    )
    masked = widen(cotangent[...]) * valid
    shifted = jnp.where(row == 0, before_row * last_valid, pltpu.roll(masked, 1, 0))
    masked_low, shifted_low = bfloat(masked), bfloat(shifted)
    upstream = times_transposed(masked_low, ws[0:D, :]) + widen(
        bfloat(times_transposed(shifted_low, ws[D : 2 * D, :]))
    )
    half = D + FF
    states_t = jnp.transpose(states)
    put_block(bfloat(matmul(states_t, masked_low)), 0, half, half_side, sent, kept)
    put_block(bfloat(matmul(states_t, shifted_low)), D, half, half_side, sent, kept)
    sums[0:1, :] = summed(masked)

    third_grad = norm_backward(upstream, vector(G3), normal3, scaling3)
    sums[1:2, :] = summed(upstream * normal3)
    sums[2:3, :] = summed(upstream)
    third_low = bfloat(third_grad)
    sums[3:4, :] = summed(third_low)
    low2_t = jnp.transpose(low2[...])
    second_up = third_grad
    for c in range(FF // D):
        lanes = slice(c * D, (c + 1) * D)
        put_block(
            bfloat(matmul(jnp.transpose(hidden[:, lanes]), third_low)),
            2 * D + FF + c * D, half, half_side, sent, kept,
        )
        hidden_grad = bfloat(times_transposed(third_low, wr[lanes, :]))
        before_grad = bfloat(widen(hidden_grad) * slope[:, lanes])
        put_block(bfloat(matmul(low2_t, before_grad)), 2 * D + c * D, half, half_side, sent, kept)
        sums[4 + c : 5 + c, :] = summed(before_grad)
        second_up += times_transposed(before_grad, we[:, lanes])
    second_out[...] = norm_backward(second_up, vector(G2), normal2, scaling2)
    sums[8:9, :] = summed(second_up * normal2)
    sums[9:10, :] = summed(second_up)


def backward_kernel(
    numbers, segments, blended, gathered, vectors, normal, scaling, low, query, fetched, lse, second_grad, first_state,
    wo_h, cq_h, ck_h, cv_h, co_h,
    first_grad_out, upstream_out, memory_out, sent, kept, sums,
    wo, cq, ck, cv, co, memory, columns, keys, keys_t, values, grad_keys, grad_values, query_t,
    upstream2, semaphores,
):
    T, D = low.shape
    M = memory.shape[0]
    memory_length, half_side = numbers[2], numbers[3]
    loads = [
        pltpu.make_async_copy(a, b, semaphores.at[i])
        for i, (a, b) in enumerate([(co_h, co), (ck_h, ck), (cv_h, cv), (cq_h, cq), (wo_h, wo)])
    ]
    for load in loads:
        load.start()

    def vector(index):
        return vectors[index : index + 1, :]

    sums[...] = jnp.zeros_like(sums)
    code_row = segments[...].astype(f32)
    memory_rows(gathered, memory, columns, memory_length)
    loads[0].wait()
    low_grad = bfloat(second_grad[...])
    upstream2[...] = bfloat(times_transposed(low_grad, co[...]))
    loads[1].wait()
    loads[2].wait()
    k = bfloat(matmul(memory[...], ck[...]))
    v = bfloat(matmul(memory[...], cv[...]) + vector(BV2))
    for pair in range(PAIRS):
        keys[pair] = k[:, 128 * pair : 128 * pair + 128]
        values[pair] = v[:, 128 * pair : 128 * pair + 128]
    keys_t[...] = jnp.transpose(k)
    products = widen(upstream2[...]) * widen(fetched[...])
    coarse = bfloat(products)
    fine = bfloat(products - widen(coarse))
    ones_of_heads = head_rows(bf16)
    corrections = (
        times_transposed(ones_of_heads, coarse) + times_transposed(ones_of_heads, fine)
    )[0:H]
    lse_plus = lse[...]

    def one_tile(pair, q, tile):
        span = slice(q * TILE, (q + 1) * TILE)
        at = slice(tile * TILE, (tile + 1) * TILE)
        lanes = slice(128 * pair, 128 * pair + 128)
        column = columns[at, :]
        visible = jnp.concatenate([column] * (TILE // 128), axis=1) == code_row[:, span]
        key_add = value_add = None
        for s in range(2):
            head = 2 * pair + s
            q_side = one_head(query[span, lanes], s)
            u_side = one_head(upstream2[span, lanes], s)
            scores = times_transposed(keys[pair, at, :], q_side) - lse_plus[head : head + 1, span]
            chances = jnp.where(visible, jnp.exp(scores), 0.0)
            chance_grad = (
                times_transposed(values[pair, at, :], u_side) - corrections[head : head + 1, span]
            )
            score_grad = bfloat(chances * chance_grad)
            to_values = matmul(bfloat(chances), u_side)
            to_keys = matmul(score_grad, q_side)
            value_add = to_values if s == 0 else value_add + to_values
            key_add = to_keys if s == 0 else key_add + to_keys
            rows = slice(HD * head, HD * head + HD)
            gained = matmul(keys_t[rows, at], score_grad)
            if tile == 0:
                query_t[rows, span] = gained
            else:
                query_t[rows, span] += gained
        if q == 0:
            grad_keys[at, lanes] = key_add
            grad_values[at, lanes] = value_add
        else:
            grad_keys[at, lanes] += key_add
            grad_values[at, lanes] += value_add

    for pair in range(PAIRS):
        for q in range(T // TILE):
            for tile in range(M // TILE):
                one_tile(pair, q, tile)

    query_rows = bfloat(jnp.transpose(query_t[...])) * 0.125
    loads[3].wait()
    first_up = second_grad[...] + times_transposed(query_rows, cq[...])
    first_grad = norm_backward(first_up, vector(G1), normal[...], scaling[:, 0:1])
    first_grad_out[...] = first_grad
    first_low = bfloat(first_grad)
    loads[4].wait()
    upstream_out[...] = bfloat(times_transposed(first_low, wo[...]))
    gk, gv = bfloat(grad_keys[...]), bfloat(grad_values[...])
    part = bfloat(times_transposed(gk, ck[...]) + times_transposed(gv, cv[...]))
    count, size, _ = memory_out.shape
    here = size - TAIL
    for b in range(count):
        memory_out[b, 0:here, :] = part[b * here : (b + 1) * here]
        memory_out[b, here:size, :] = jnp.where(
            numbers[0] == b + 1, widen(first_state[...]), 0.0
        ).astype(bf16)
    memory_t = jnp.transpose(memory[...])
    put_block(bfloat(matmul(jnp.transpose(low[...]), query_rows)), 0, 5 * D // 2, half_side, sent, kept)
    put_block(bfloat(matmul(memory_t, gk)), D, 5 * D // 2, half_side, sent, kept)
    put_block(bfloat(matmul(memory_t, gv)), 2 * D, 5 * D // 2, half_side, sent, kept)
    put_block(bfloat(matmul(jnp.transpose(fetched[...]), low_grad)), 3 * D, 5 * D // 2, half_side, sent, kept)
    put_block(bfloat(matmul(jnp.transpose(blended[...]), first_low)), 4 * D, 5 * D // 2, half_side, sent, kept)
    sums[0:1, :] = summed(low_grad)
    sums[1:2, :] = summed(query_rows)
    sums[2:3, :] = summed(gv)
    sums[3:4, :] = summed(first_up * normal[...])
    sums[4:5, :] = summed(first_up)
    sums[5:6, :] = summed(first_low)


VMEM_BLOCK = pl.BlockSpec(memory_space=pltpu.VMEM)
SMEM_BLOCK = pl.BlockSpec(memory_space=pltpu.SMEM)
HBM_BLOCK = pl.BlockSpec(memory_space=pl.ANY)


def middle_forward(numbers, segments, canvas, blended, cotangent, gathered, vectors, side, middle, weights):
    T, D = canvas.shape
    wo, cq, ck, cv, co, we, wr, ws = weights
    FF = we.shape[1]
    M = gathered.shape[0] * (gathered.shape[1] - TAIL)
    rows = (2 * D + 2 * FF) // 2
    shape = jax.ShapeDtypeStruct
    return pl.pallas_call(
        forward_kernel,
        out_shape=[
            shape((T, D), bf16), shape((8, D), f32), shape((TAIL, D), bf16),
            shape((T, D), f32), shape((T, 128), f32), shape((T, D), bf16), shape((T, D), bf16),
            shape((T, D), bf16), shape((H, T), f32), shape((T, D), f32),
            shape((rows, D), bf16), shape((rows, D), bf16), shape((16, D), f32),
        ],
        in_specs=[SMEM_BLOCK] + [VMEM_BLOCK] * 6 + [HBM_BLOCK] * 10,
        out_specs=[VMEM_BLOCK] * 13,
        scratch_shapes=[pltpu.VMEM(w.shape, bf16) for w in weights] + [
            pltpu.VMEM((2, TAIL, D), bf16),
            pltpu.VMEM((M, D), bf16),
            pltpu.VMEM((M, 128), f32),
            pltpu.VMEM((PAIRS, M, 128), bf16),
            pltpu.VMEM((H, VROWS, M), bf16),
            pltpu.VMEM((H, T), f32),
            pltpu.VMEM((H, VROWS, T), f32),
            pltpu.VMEM((D, T), f32),
            pltpu.VMEM((T, FF), bf16),
            pltpu.VMEM((T, FF), f32),
            pltpu.VMEM((T, D), f32),
            pltpu.VMEM((T, D), bf16),
            pltpu.SemaphoreType.DMA((10,)),
        ],
        compiler_params=pltpu.CompilerParams(vmem_limit_bytes=ROOM),
        name="middle_forward",
    )(numbers, segments, canvas, blended, cotangent, gathered, vectors, side, middle, *weights)


def middle_backward(numbers, segments, blended, gathered, vectors, saved, weights):
    T, D = blended.shape
    M = gathered.shape[0] * (gathered.shape[1] - TAIL)
    rows = 5 * D // 2
    shape = jax.ShapeDtypeStruct
    return pl.pallas_call(
        backward_kernel,
        out_shape=[
            shape((T, D), f32), shape((T, D), bf16), shape(gathered.shape, bf16),
            shape((rows, D), bf16), shape((rows, D), bf16), shape((8, D), f32),
        ],
        in_specs=[SMEM_BLOCK] + [VMEM_BLOCK] * 12 + [HBM_BLOCK] * 5,
        out_specs=[VMEM_BLOCK] * 6,
        scratch_shapes=[pltpu.VMEM(w.shape, bf16) for w in weights] + [
            pltpu.VMEM((M, D), bf16),
            pltpu.VMEM((M, 128), f32),
            pltpu.VMEM((PAIRS, M, 128), bf16),
            pltpu.VMEM((D, M), bf16),
            pltpu.VMEM((PAIRS, M, 128), bf16),
            pltpu.VMEM((M, D), f32),
            pltpu.VMEM((M, D), f32),
            pltpu.VMEM((D, T), f32),
            pltpu.VMEM((T, D), bf16),
            pltpu.SemaphoreType.DMA((5,)),
        ],
        compiler_params=pltpu.CompilerParams(vmem_limit_bytes=ROOM),
        name="middle_backward",
    )(numbers, segments, blended, gathered, vectors, *saved, *weights)


SIDE = [(0, 1), (1, 0), (2, 3), (3, 2)]
MIDDLE = [(1, 2), (2, 1)]
OUTWARD = [(1, 0), (2, 3)]
INWARD = [(0, 1), (3, 2)]


def row_window(payload):
    side = lax.ppermute(payload, "seq", SIDE)
    middle = lax.ppermute(payload, "seq", MIDDLE)
    middle_far = lax.ppermute(side, "seq", MIDDLE)
    side_far = lax.ppermute(middle, "seq", OUTWARD)
    return payload, side, middle, middle_far, side_far


def routes():
    bits = [("rows", 1 << b) for b in range((lax.axis_size("rows") - 1).bit_length())]
    along = [("seq", 1 << b) for b in range((lax.axis_size("seq") - 1).bit_length())]
    return bits[0], bits[1:], bits[:0:-1], along


def swap(block, step):
    axis, bit = step
    return lax.ppermute(block, axis, [(i, i ^ bit) for i in range(lax.axis_size(axis))])


def side_of(step):
    axis, bit = step
    return jnp.where((lax.axis_index(axis) & bit) != 0, 1, 0)


def halves(terms, step):
    side = side_of(step)
    half = terms[0].shape[0] // 2

    def part(which):
        pieces = [widen(lax.dynamic_slice_in_dim(t, which * half, half)) for t in terms]
        return bfloat(sum(pieces[1:], pieces[0]))

    return part(1 - side), part(side)


def doubled(block, step):
    came = swap(block, step)
    side = side_of(step) == 1
    return jnp.where(side, came, block), jnp.where(side, block, came)


def sum_over_devices(sent, kept):
    first, up, down, along = routes()
    came = swap(sent, first)
    half = kept.shape[0] // 2
    lanes = []
    for way, at in ((up, 0), (down, half)):
        terms = [kept[at : at + half], came[at : at + half]]
        for step in way:
            goes, stays = halves(terms, step)
            terms = [stays, swap(goes, step)]
        lanes.append(terms)
    both = None
    for number, step in enumerate(along):
        if number == 0:
            parts = [halves(terms, step) for terms in lanes]
            goes = jnp.concatenate([p[0] for p in parts], axis=0)
            stays = jnp.concatenate([p[1] for p in parts], axis=0)
            cut = parts[0][0].shape[0]
            both = [stays, swap(goes, step)]
        else:
            goes, stays = halves(both, step)
            both = [stays, swap(goes, step)]
    mine = bfloat(widen(both[0]) + widen(both[1]))
    for step in along[:0:-1]:
        mine = jnp.concatenate(doubled(mine, step), axis=0)
    low, high = doubled(mine, along[0])
    whole = []
    for way, at in ((up, 0), (down, cut)):
        block = jnp.concatenate([low[at : at + cut], high[at : at + cut]], axis=0)
        for step in way[::-1]:
            block = jnp.concatenate(doubled(block, step), axis=0)
        whole.append(block)
    return doubled(jnp.concatenate(whole, axis=0), first)


def rows_from(summed_halves, start, count):
    low, high = summed_halves
    half = low.shape[0]
    pieces = []
    if start < half:
        pieces.append(low[start : min(start + count, half)])
    if start + count > half:
        pieces.append(high[max(start - half, 0) : start + count - half])
    return widen(pieces[0] if len(pieces) == 1 else jnp.concatenate(pieces, axis=0))


def shards(
    canvas,
    memory,
    cotangent,
    canvas_lengths,
    canvas_segments,
    memory_segments,
    memory_lengths,
    self_query,
    self_key,
    self_value,
    self_output,
    self_query_bias,
    self_value_bias,
    self_output_bias,
    first_gain,
    first_bias,
    cross_query,
    cross_key,
    cross_value,
    cross_output,
    cross_query_bias,
    cross_value_bias,
    cross_output_bias,
    second_gain,
    second_bias,
    expand_weight,
    expand_bias,
    reduce_weight,
    reduce_bias,
    third_gain,
    third_bias,
    slot_weight,
    slot_bias,
):
    place = lax.axis_index("seq")
    tokens_here = canvas.shape[1]
    memory_here = memory.shape[1]
    width = canvas.shape[2]
    wide = expand_weight.shape[1]
    segments = canvas_segments[0]
    first_step = routes()[0]

    def code_row(codes):
        return jnp.pad(bfloat(widen(codes)), ((0, 0), (0, width - codes.shape[1])))

    payload = jnp.concatenate(
        [canvas[0], code_row(canvas_segments), cotangent[0, -1:], jnp.zeros((TAIL - 2, width), bf16)],
        axis=0,
    )
    blocks = row_window(payload)
    memory_payload = jnp.concatenate(
        [memory[0], code_row(memory_segments), jnp.zeros((TAIL - 1, width), bf16)], axis=0
    )
    gathered = lax.all_gather(memory_payload, "seq", axis=0)
    vectors = jnp.stack(
        [
            self_query_bias, self_value_bias, self_output_bias, first_gain, first_bias,
            cross_query_bias, cross_value_bias, cross_output_bias, second_gain, second_bias,
            reduce_bias, third_gain, third_bias, slot_bias,
        ]
    )
    vectors = widen(jnp.concatenate([vectors, expand_bias.reshape(-1, width)], axis=0))
    numbers = jnp.stack(
        [place, canvas_lengths[0], memory_lengths[0], side_of(first_step)]
    ).astype(jnp.int32)

    blended, queries, masses = self_forward(
        numbers, segments, blocks, (self_query, self_key, self_value, vectors)
    )
    (
        slots, last_slot, first_state, normal, scaling, low, cross_rows, fetched, cross_masses,
        second_grad, early_sent, early_kept, early_sums,
    ) = middle_forward(
        numbers, canvas_segments, canvas[0], blended, cotangent[0], gathered, vectors, blocks[1], blocks[2],
        (self_output, cross_query, cross_key, cross_value, cross_output, expand_weight, reduce_weight, slot_weight),
    )
    early = sum_over_devices(early_sent, early_kept)
    first_grad, blended_grad, memory_part, later_sent, later_kept, later_sums = middle_backward(
        numbers, canvas_segments, blended, gathered, vectors,
        (normal, scaling, low, cross_rows, fetched, cross_masses, second_grad, first_state),
        (self_output, cross_query, cross_key, cross_value, cross_output),
    )
    later = sum_over_devices(later_sent, later_kept)
    memory_grad = lax.psum_scatter(memory_part, "seq", scatter_dimension=0)
    canvas_base, far_part, middle_part, side_part, last_sent, last_kept = self_backward(
        numbers, segments, blocks, (self_query, self_key, self_value, vectors),
        queries, blended, blended_grad, masses, first_grad, early_sums, later_sums,
    )
    from_side = lax.ppermute(far_part, "seq", INWARD)
    from_middle = lax.ppermute(far_part, "seq", MIDDLE)
    last = sum_over_devices(last_sent, last_kept)
    onward = lax.ppermute(bfloat(widen(middle_part) + widen(from_side)), "seq", MIDDLE)
    outward = lax.ppermute(bfloat(widen(side_part) + widen(from_middle)), "seq", SIDE)
    canvas_grad = canvas_base + widen(onward) + widen(outward)

    next_state = memory_grad[memory_here : memory_here + 1]
    last_row = (last_slot[0:1] + matmul(next_state, slot_weight[width:])) * last_slot[1:2]
    slots = lax.dynamic_update_slice(slots, bfloat(last_row), (tokens_here - 1, 0))

    grad_slot = rows_from(early, 0, 2 * width)
    grad_expand = jnp.concatenate(
        [rows_from(early, 2 * width + c, width) for c in range(0, wide, width)], axis=1
    )
    grad_reduce = rows_from(early, 2 * width + wide, wide)
    cross_grads = [rows_from(later, c * width, width) for c in range(5)]
    self_grads = [rows_from(last, c * width, width) for c in range(3)]
    sums = rows_from(last, 3 * width, 32)
    return (
        slots[None],
        canvas_grad[None],
        widen(memory_grad[:memory_here])[None],
        self_grads[0],
        self_grads[1],
        self_grads[2],
        cross_grads[4],
        sums[24],
        sums[25],
        sums[21],
        sums[19],
        sums[20],
        cross_grads[0],
        cross_grads[1],
        cross_grads[2],
        cross_grads[3],
        sums[17],
        sums[18],
        sums[16],
        sums[8],
        sums[9],
        grad_expand,
        sums[4:8].reshape(-1),
        grad_reduce,
        sums[3],
        sums[1],
        sums[2],
        grad_slot,
        sums[0],
    )


def solution(mesh):
    placed = (
        P("rows", "seq", None),
        P("rows", "seq", None),
        P("rows", "seq", None),
        P("rows"),
        P("rows", "seq"),
        P("rows", "seq"),
        P("rows"),
        P(),
        P(),
        P(),
        P(),
        P(),
        P(),
        P(),
        P(),
        P(),
        P(),
        P(),
        P(),
        P(),
        P(),
        P(),
        P(),
        P(),
        P(),
        P(),
        P(),
        P(),
        P(),
        P(),
        P(),
        P(),
        P(),
    )
    return jax.shard_map(
        shards,
        mesh=mesh,
        in_specs=placed,
        out_specs=(
            P("rows", "seq", None),
            P("rows", "seq", None),
            P("rows", "seq", None),
            P(),
            P(),
            P(),
            P(),
            P(),
            P(),
            P(),
            P(),
            P(),
            P(),
            P(),
            P(),
            P(),
            P(),
            P(),
            P(),
            P(),
            P(),
            P(),
            P(),
            P(),
            P(),
            P(),
            P(),
            P(),
            P(),
        ),
        check_vma=False,
    )
```

```python
import functools

import jax
import jax.numpy as jnp
from jax import lax
from jax.experimental import pallas as pl
from jax.experimental.pallas import tpu as pltpu
from jax.sharding import PartitionSpec as P

H = 8
HD = 64
PAIRS = H // 2
TILE = 256
TAIL = 16
LAST_SPLIT = 2
LATER_SPLIT = 0
TURNS = "EM1SMSEMSESMEMSSESMceSMsm"
VROWS = 80
ROOM = 58 * 1024 * 1024

masked_score = -30000.0
epsilon = 1e-05
gelu_scale = 0.7978845608028654
gelu_cubic = 0.044715
safe_square = 3600.0
bf16 = jnp.bfloat16
f32 = jnp.float32


def cost(microseconds):
    return pl.CostEstimate(flops=int(microseconds * 1.1e9), bytes_accessed=0, transcendentals=0)


def matmul(left, right):
    return jnp.dot(left, right, preferred_element_type=f32)


def times_transposed(left, right):
    return lax.dot_general(left, right, (((1,), (1,)), ((), ())), preferred_element_type=f32)


def bfloat(values):
    return values.astype(bf16)


def widen(values):
    return values.astype(f32)


def head_rows(dtype):
    row = lax.broadcasted_iota(jnp.int32, (16, H * HD), 0)
    column = lax.broadcasted_iota(jnp.int32, (16, H * HD), 1)
    return jnp.where(column // HD == row, 1.0, 0.0).astype(dtype)


def one_head(pair_columns, side):
    lane = lax.broadcasted_iota(jnp.int32, pair_columns.shape, 1)
    wanted = lane < HD if side == 0 else lane >= HD
    return jnp.where(wanted, widen(pair_columns), 0.0).astype(bf16)


def neighbours(place):
    inner = jnp.logical_or(place == 1, place == 2)
    beside = place + 1 - 2 * lax.rem(place, 2)
    across = 3 - place
    far = jnp.where(inner, across + 1 - 2 * lax.rem(across, 2), 3 - beside)
    return inner, beside, across, far


def window_moves(place, blocks, window, tails, semaphores):
    own, side, middle, middle_far, side_far = blocks
    inner, beside, across, far = neighbours(place)
    outer = jnp.logical_not(inner)
    T = window.shape[1]

    def move(block, slot, index):
        return (
            pltpu.make_async_copy(block.at[pl.ds(0, T)], window.at[slot], semaphores.at[2 * index]),
            pltpu.make_async_copy(
                block.at[pl.ds(T, TAIL)], tails.at[slot], semaphores.at[2 * index + 1]
            ),
        )

    def near(act):
        for copy in move(own, place, 0) + move(side, beside, 1):
            act(copy)

        @pl.when(inner)
        def _():
            for copy in move(middle, across, 2):
                act(copy)

    def distant(act):
        @pl.when(inner)
        def _():
            for copy in move(middle_far, far, 3):
                act(copy)

        @pl.when(outer)
        def _():
            for copy in move(side_far, far, 3):
                act(copy)

    return near, distant


def is_outer(place):
    return jnp.logical_or(place == 0, place == 3)


def present_tiles(place, per, with_far):
    reach = 2 if with_far else 1
    return jnp.maximum(place - reach, 0) * per, jnp.minimum(place + reach + 1, 4) * per


def masked_chances(lse):
    return jnp.exp(masked_score - lse)


def masked_terms(lse, upstream):
    chances = jnp.concatenate([masked_chances(lse), jnp.zeros((8, lse.shape[1]), f32)], axis=0)
    terms = matmul(bfloat(chances), upstream)
    return jnp.sum(jnp.where(head_rows(f32) > 0.0, terms, 0.0), axis=0, keepdims=True)


def start(copy):
    copy.start()


def wait(copy):
    copy.wait()


def no_codes(codes, keycodes, pivot):
    T = codes.shape[1]
    for slot in range(4):
        codes[slot : slot + 1, :] = jnp.full((1, T), 1.0, f32) * jnp.where(slot < pivot, -8.0, 8.0)
        keycodes[slot : slot + 1, :] = jnp.full((1, T), -9.0, f32)


def read_codes(codes, keycodes, tails, slot, length):
    T = codes.shape[1]
    lane = lax.broadcasted_iota(jnp.int32, (1, T), 1)
    code = widen(tails[slot, 0:1, 0:T])
    codes[pl.ds(slot, 1), :] = code
    keycodes[pl.ds(slot, 1), :] = jnp.where(slot * T + lane < length, code, -1.0)


def near_codes(codes, keycodes, tails, place, length):
    inner, beside, across, _ = neighbours(place)
    read_codes(codes, keycodes, tails, place, length)
    read_codes(codes, keycodes, tails, beside, length)

    @pl.when(inner)
    def _():
        read_codes(codes, keycodes, tails, across, length)


def tile_range(codes, first_code, last_code):
    below = jnp.sum(jnp.where(codes[...] < first_code, 1, 0))
    through = jnp.sum(jnp.where(codes[...] <= last_code, 1, 0))
    return below // TILE, (through + TILE - 1) // TILE


def as_column(row):
    return jnp.transpose(jnp.broadcast_to(row, (128, row.shape[1])))


def column_codes(keycodes, columns, tile, T):
    per = T // TILE
    row = keycodes[pl.ds(tile // per, 1), pl.ds(pl.multiple_of(lax.rem(tile, per) * TILE, TILE), TILE)]
    columns[pl.ds(pl.multiple_of(tile * TILE, TILE), TILE), :] = as_column(row)


def tile_rows(window, tile):
    per = window.shape[1] // TILE
    return window[tile // per, pl.ds(pl.multiple_of(lax.rem(tile, per) * TILE, TILE), TILE), :]


def split_heads(rows, sides):
    for head in range(H):
        sides[head] = one_head(rows[:, 128 * (head // 2) : 128 * (head // 2) + 128], head % 2)


def visible_in(columns, at, code_row):
    column = columns[at, :]
    return jnp.concatenate([column] * (code_row.shape[1] // 128), axis=1) == code_row


def look_at(at, keys, q_sides, columns, code_row, summit):
    visible = visible_in(columns, at, code_row)
    for head in range(H):
        scores = times_transposed(keys[head // 2, at, :], q_sides[head])
        scores = jnp.where(visible, scores, masked_score)
        summit[head : head + 1, :] = jnp.maximum(
            summit[head : head + 1, :], jnp.max(scores, axis=0, keepdims=True)
        )


def blend_at(at, keys, values_t, q_sides, columns, code_row, summit, total):
    visible = visible_in(columns, at, code_row)
    for head in range(H):
        scores = jnp.where(visible, times_transposed(keys[head // 2, at, :], q_sides[head]), masked_score)
        powers = bfloat(jnp.exp(scores - summit[head : head + 1, :]))
        total[head] += matmul(values_t[head, :, at], powers)


def normalise(total, summit, lse, blend_t):
    for head in range(H):
        mass = total[head, HD : HD + 1, :]
        blend_t[HD * head : HD * head + HD, :] = total[head, 0:HD, :] / mass
        lse[head : head + 1, :] = summit[head : head + 1, :] + jnp.log(mass)
    return bfloat(jnp.transpose(blend_t[...]))


def row_corrections(upstream, blended):
    products = widen(upstream) * widen(blended)
    coarse = bfloat(products)
    fine = bfloat(products - widen(coarse))
    ones_of_heads = head_rows(bf16)
    both = times_transposed(ones_of_heads, coarse) + times_transposed(ones_of_heads, fine)
    return both[0:H]


def step_back(at, keys, keys_t, values, q_sides, u_sides, columns, code_row, lse, fixes, query_t, grad_keys, grad_values):
    visible = visible_in(columns, at, code_row)
    for pair in range(PAIRS):
        k = keys[pair, at, :]
        v = values[pair, at, :]
        key_add = value_add = None
        for head in (2 * pair, 2 * pair + 1):
            q_side, u_side = q_sides[head], u_sides[head]
            scores = jnp.where(visible, times_transposed(k, q_side), masked_score)
            chances = jnp.exp(scores - lse[head : head + 1, :])
            chance_grad = times_transposed(v, u_side) - fixes[head : head + 1, :]
            score_grad = bfloat(jnp.where(visible, chances * chance_grad, 0.0))
            to_values = matmul(bfloat(chances), u_side)
            to_keys = matmul(score_grad, q_side)
            value_add = to_values if value_add is None else value_add + to_values
            key_add = to_keys if key_add is None else key_add + to_keys
            rows = slice(HD * head, HD * head + HD)
            query_t[rows, :] += matmul(keys_t[rows, at], score_grad)
        grad_keys[pair, at, :] = key_add
        grad_values[pair, at, :] = value_add


def tile_at(tile):
    return pl.ds(pl.multiple_of(tile * TILE, TILE), TILE)


def project_forward(tile, window, keycodes, columns, keys, values_t, wk, weights_t, bias_t):
    x = tile_rows(window, tile)
    at = tile_at(tile)
    k = bfloat(matmul(x, wk[...]))
    for pair in range(PAIRS):
        keys[pair, at, :] = k[:, 128 * pair : 128 * pair + 128]
    v_t = bfloat(times_transposed(weights_t, x) + bias_t)
    for head in range(H):
        values_t[head, 0:HD, at] = v_t[HD * head : HD * head + HD]
        values_t[head, HD:VROWS, at] = jnp.ones((VROWS - HD, TILE), bf16)
    column_codes(keycodes, columns, tile, window.shape[1])
    return times_transposed(head_rows(bf16), k * k)


def self_near_kernel(
    ready, done, numbers, own, side, middle, segments, vectors, wv, wq, wk,
    queries, total, reach_out,
    window, tails, codes, keycodes, columns, keys, values_t, zeros, q_sides, semaphores,
):
    T, D = queries.shape
    place, length = numbers[0], numbers[1]
    near, _ = window_moves(place, (own, side, middle, middle, side), window, tails, semaphores)
    near(start)
    no_codes(codes, keycodes, place)
    ready()
    weights_t = jnp.transpose(wv[...])
    bias_t = as_column(vectors[BV1 : BV1 + 1, :])[:, 0:1]
    near(wait)
    near_codes(codes, keycodes, tails, place, length)
    low, high = tile_range(codes, numbers[4].astype(f32), numbers[5].astype(f32))
    rows_q = bfloat((matmul(window[place], wq[...]) + vectors[BQ1 : BQ1 + 1, :]) * 0.125)
    queries[...] = rows_q
    done(0)
    split_heads(rows_q, q_sides)

    def project(tile, reach):
        return jnp.maximum(
            reach, project_forward(tile, window, keycodes, columns, keys, values_t, wk, weights_t, bias_t)
        )

    key_reach = lax.fori_loop(low, high, project, jnp.zeros((16, TILE), f32))
    reach_out[...] = jnp.broadcast_to(jnp.max(key_reach, axis=1, keepdims=True), (16, 128))
    zeros[...] = jnp.zeros_like(zeros)
    total[...] = jnp.zeros_like(total)
    code_row = segments[...].astype(f32)

    def blend(tile, _):
        blend_at(tile_at(tile), keys, values_t, q_sides, columns, code_row, zeros, total)
        return 0

    lax.fori_loop(low, high, blend, 0)


def self_far_kernel(
    ready, done, numbers, own, side, middle, middle_far, side_far,
    wk, wv, segments, vectors, queries, near_reach, opposite, near_total,
    out, lse,
    window, tails, codes, keycodes, columns, keys, values_t, summit, total, blend_t, q_sides, semaphores,
):
    T, D = out.shape
    place, length = numbers[0], numbers[1]
    _, _, _, far = neighbours(place)
    near, distant = window_moves(
        place, (own, side, middle, middle_far, side_far), window, tails, semaphores
    )
    distant(start)
    no_codes(codes, keycodes, far)
    ready()
    weights_t = jnp.transpose(wv[...])
    bias_t = as_column(vectors[BV1 : BV1 + 1, :])[:, 0:1]
    ones_of_heads = head_rows(bf16)
    rows_q = queries[...]
    split_heads(rows_q, q_sides)
    query_reach = jnp.max(times_transposed(ones_of_heads, rows_q * rows_q), axis=1, keepdims=True)
    first, last = numbers[4].astype(f32), numbers[5].astype(f32)
    distant(wait)
    read_codes(codes, keycodes, tails, far, length)
    low, high = tile_range(codes, first, last)

    def project(tile, reach):
        return jnp.maximum(
            reach, project_forward(tile, window, keycodes, columns, keys, values_t, wk, weights_t, bias_t)
        )

    key_reach = lax.fori_loop(low, high, project, jnp.zeros((16, TILE), f32))
    key_reach = jnp.maximum(jnp.max(key_reach, axis=1, keepdims=True), near_reach[:, 0:1])
    wide = jnp.max(query_reach * key_reach) > safe_square
    summit[...] = jnp.zeros_like(summit)
    total[...] = near_total[...]
    code_row = segments[...].astype(f32)

    per = T // TILE
    low_here, high_here = present_tiles(place, per, True)

    @pl.when(wide)
    def _():
        near(start)
        near(wait)
        near_codes(codes, keycodes, tails, place, length)
        lax.fori_loop(low_here, high_here, project, jnp.zeros((16, TILE), f32))
        total[...] = jnp.zeros_like(total)
        summit[...] = jnp.full(summit.shape, masked_score, f32)

        def look(tile, _):
            look_at(tile_at(tile), keys, q_sides, columns, code_row, summit)
            return 0

        lax.fori_loop(low_here, high_here, look, 0)

        @pl.when(is_outer(place))
        def _():
            sums = times_transposed(weights_t, opposite[...])
            column = sums[:, 2:3] + sums[:, 3:4] + T * bias_t
            for head in range(H):
                part = jnp.concatenate(
                    [column[HD * head : HD * head + HD], jnp.full((VROWS - HD, 1), T, f32)], axis=0
                )
                total[head] = part * jnp.exp(masked_score - summit[head : head + 1, :])

    def blend(tile, _):
        blend_at(tile_at(tile), keys, values_t, q_sides, columns, code_row, summit, total)
        return 0

    lax.fori_loop(
        jnp.where(wide, low_here, low), jnp.where(wide, high_here, high), blend, 0
    )
    out[...] = normalise(total, summit, lse, blend_t)


def project_backward(tile, window, keycodes, columns, keys, keys_t, values, wk, wv, bias, weights_t):
    x = tile_rows(window, tile)
    at = tile_at(tile)
    k = bfloat(matmul(x, wk[...]))
    v = bfloat(matmul(x, wv[...]) + bias)
    for pair in range(PAIRS):
        keys[pair, at, :] = k[:, 128 * pair : 128 * pair + 128]
        values[pair, at, :] = v[:, 128 * pair : 128 * pair + 128]
    keys_t[:, at] = bfloat(times_transposed(weights_t, x))
    column_codes(keycodes, columns, tile, window.shape[1])


def tile_grads(at, grad_keys, grad_values):
    gk = jnp.concatenate([bfloat(grad_keys[pair, at, :]) for pair in range(PAIRS)], axis=1)
    gv = jnp.concatenate([bfloat(grad_values[pair, at, :]) for pair in range(PAIRS)], axis=1)
    return gk, gv


def back_far_kernel(
    ready, done, numbers, middle_far, side_far,
    segments, vectors, wk, wv, queries, upstream, blended, lse, opposite,
    part_out, grad_k, grad_v, value_sum, query_t,
    window, tails, codes, keycodes, columns, keys, keys_t, values, grad_keys, grad_values,
    q_sides, u_sides, fixes, semaphores,
):
    T, D = queries.shape
    place, length = numbers[0], numbers[1]
    _, _, _, far = neighbours(place)
    _, distant = window_moves(
        place, (side_far, side_far, side_far, middle_far, side_far), window, tails, semaphores
    )
    distant(start)
    ready()
    no_codes(codes, keycodes, far)
    part_out[...] = jnp.zeros_like(part_out)
    query_t[...] = jnp.zeros_like(query_t)
    grad_k[...] = jnp.zeros_like(grad_k)
    grad_v[...] = jnp.zeros_like(grad_v)
    value_sum[...] = jnp.zeros_like(value_sum)
    distant(wait)
    read_codes(codes, keycodes, tails, far, length)
    low, high = tile_range(codes, numbers[4].astype(f32), numbers[5].astype(f32))
    code_row = segments[...].astype(f32)
    per = T // TILE
    deep = jnp.max(masked_chances(lse[...])) > 0.0
    low = jnp.where(deep, far * per, low)
    high = jnp.where(deep, far * per + per, high)

    @pl.when(jnp.logical_and(deep, is_outer(place)))
    def _():
        terms = masked_terms(lse[...], upstream[...])
        terms_8 = jnp.broadcast_to(terms, (TAIL, D))
        row = lax.broadcasted_iota(jnp.int32, (TAIL, D), 0)
        rows = jnp.where(jnp.logical_or(row == 2, row == 3), widen(opposite[...]), 0.0)
        grad_v[...] += matmul(jnp.transpose(rows), jnp.where(row < 4, terms_8, 0.0))
        value_sum[0:1, :] += T * terms

    @pl.when(high > low)
    def _():
        weights_t = jnp.transpose(wk[...])
        split_heads(queries[...], q_sides)
        split_heads(upstream[...], u_sides)
        fixes[...] = row_corrections(upstream[...], blended[...])

        def step(tile, _):
            project_backward(
                tile, window, keycodes, columns, keys, keys_t, values, wk, wv,
                vectors[BV1 : BV1 + 1, :], weights_t,
            )
            at = tile_at(tile)
            step_back(
                at, keys, keys_t, values, q_sides, u_sides, columns, code_row, lse, fixes, query_t,
                grad_keys, grad_values,
            )
            gk, gv = tile_grads(at, grad_keys, grad_values)
            x_t = jnp.transpose(tile_rows(window, tile))
            grad_k[...] += matmul(x_t, gk)
            grad_v[...] += matmul(x_t, gv)
            value_sum[0:1, :] += summed(gv)
            inside = pl.ds(pl.multiple_of(lax.rem(tile, T // TILE) * TILE, TILE), TILE)
            part_out[inside, :] = bfloat(times_transposed(gk, wk[...]) + times_transposed(gv, wv[...]))
            return 0

        lax.fori_loop(low, high, step, 0)


def back_near_kernel(
    ready, done, numbers, own, side, middle,
    segments, vectors, wk, wv, queries, upstream, blended, lse, far_query_t,
    wq, entering, far_k, far_v, far_sum, sums_one, sums_two,
    canvas_out, middle_out, side_out, sent, kept,
    window, tails, codes, keycodes, columns, keys, keys_t, values, grad_keys, grad_values,
    q_sides, u_sides, fixes, query_t, grad_k, grad_v, semaphores,
):
    T, D = queries.shape
    place, length = numbers[0], numbers[1]
    per = T // TILE
    near, _ = window_moves(place, (own, side, middle, middle, side), window, tails, semaphores)
    near(start)
    no_codes(codes, keycodes, place)
    ready(9)
    weights_t = jnp.transpose(wk[...])
    split_heads(queries[...], q_sides)
    split_heads(upstream[...], u_sides)
    fixes[...] = row_corrections(upstream[...], blended[...])
    query_t[...] = far_query_t[...]
    middle_out[...] = jnp.zeros_like(middle_out)
    side_out[...] = jnp.zeros_like(side_out)
    near(wait)
    near_codes(codes, keycodes, tails, place, length)
    low, high = tile_range(codes, numbers[4].astype(f32), numbers[5].astype(f32))
    code_row = segments[...].astype(f32)
    deep = jnp.max(masked_chances(lse[...])) > 0.0
    low_here, high_here = present_tiles(place, per, False)
    low, high = jnp.where(deep, low_here, low), jnp.where(deep, high_here, high)

    def step(tile, _):
        project_backward(
            tile, window, keycodes, columns, keys, keys_t, values, wk, wv,
            vectors[BV1 : BV1 + 1, :], weights_t,
        )
        step_back(
            tile_at(tile), keys, keys_t, values, q_sides, u_sides, columns, code_row, lse, fixes, query_t,
            grad_keys, grad_values,
        )
        return 0

    lax.fori_loop(low, high, step, 0)
    ready()
    grad_k[...] = far_k[...]
    grad_v[...] = far_v[...]
    query_rows = bfloat(jnp.transpose(query_t[...])) * 0.125
    canvas_out[...] = entering[...] + times_transposed(query_rows, wq[...])
    half = kept.shape[0]
    half_side = numbers[3]
    put_block(bfloat(matmul(jnp.transpose(window[place]), query_rows)), 0, half, half_side, sent, kept)
    inner, beside, across, _ = neighbours(place)

    def fold(tile, value_sum):
        block = tile // per
        inside = pl.ds(pl.multiple_of(lax.rem(tile, per) * TILE, TILE), TILE)
        gk, gv = tile_grads(tile_at(tile), grad_keys, grad_values)
        x_t = jnp.transpose(tile_rows(window, tile))
        grad_k[...] += matmul(x_t, gk)
        grad_v[...] += matmul(x_t, gv)
        part = times_transposed(gk, wk[...]) + times_transposed(gv, wv[...])

        @pl.when(block == place)
        def _():
            canvas_out[inside, :] += part

        @pl.when(jnp.logical_and(inner, block == across))
        def _():
            middle_out[inside, :] = bfloat(part)

        @pl.when(block == beside)
        def _():
            side_out[inside, :] = bfloat(part)

        return value_sum + summed(gv)

    value_sum = lax.fori_loop(low, high, fold, far_sum[0:1, :])
    done(0, 1, 2)
    put_block(bfloat(grad_k[...]), D, half, half_side, sent, kept)
    put_block(bfloat(grad_v[...]), 2 * D, half, half_side, sent, kept)
    vector_sums = jnp.concatenate(
        [sums_one[...], sums_two[...], summed(query_rows), value_sum, jnp.zeros((6, D), f32)], axis=0
    )
    put_block(bfloat(vector_sums), 3 * D, half, half_side, sent, kept)
    spare = 2 * half - 3 * D - 32
    put_block(jnp.zeros((spare, D), bf16), 3 * D + 32, half, half_side, sent, kept)


VMEM_BLOCK = pl.BlockSpec(memory_space=pltpu.VMEM)
SMEM_BLOCK = pl.BlockSpec(memory_space=pltpu.SMEM)
ANY_BLOCK = pl.BlockSpec(memory_space=pl.ANY)
HBM_BLOCK = pl.BlockSpec(memory_space=pltpu.HBM)


class Numbers:
    def __init__(self, numbers, length, memory_length, segments):
        T = segments.shape[1]
        self.refs = [
            (numbers, (0,)), (length, (0,)), (memory_length, (0,)), (numbers, (1,)),
            (segments, (0, 0)), (segments, (0, T - 1)),
        ]

    def __getitem__(self, index):
        ref, at = self.refs[index]
        return ref[at]


def run_kernel(kernel, name, microseconds, out_shapes, small, far, near, scratch, ties=(), out_far=0):
    kept = out_shapes[: len(out_shapes) - out_far]
    counts = [len(small), len(far), len(near), len(ties), len(kept), out_far, len(scratch), len(near), len(kept), 1]

    def body(*refs):
        parts, at = [], 0
        for count in counts:
            parts.append(refs[at : at + count])
            at += count
        small_refs, far_refs, held, _, outs, own_outs, scratch_refs, copies, results, (semaphores,) = parts
        loads = [
            pltpu.make_async_copy(a, b, semaphores.at[n]) for n, (a, b) in enumerate(zip(held, copies))
        ]
        leaving = {
            n: pltpu.make_async_copy(a, b, semaphores.at[len(loads) + n])
            for n, (a, b) in enumerate(zip(results, outs))
        }
        left = []
        for load in loads:
            load.start()
        waiting = list(loads)

        def ready(count=len(loads)):
            for load in waiting[:count]:
                load.wait()
            del waiting[:count]

        def done(*numbers):
            for n in numbers:
                copy = leaving.pop(n)
                copy.start()
                left.append(copy)

        kernel(ready, done, Numbers(*small_refs), *far_refs, *copies, *results, *own_outs, *scratch_refs)
        ready()
        done(*list(leaving))
        for copy in left:
            copy.wait()

    return pl.pallas_call(
        body,
        out_shape=[jax.ShapeDtypeStruct(shape, kind) for shape, kind in out_shapes],
        in_specs=[SMEM_BLOCK] * len(small)
        + [HBM_BLOCK] * (len(far) + len(near))
        + [ANY_BLOCK] * len(ties),
        out_specs=[HBM_BLOCK] * len(out_shapes),
        scratch_shapes=[
            *scratch,
            *[pltpu.VMEM(w.shape, w.dtype) for w in near],
            *[pltpu.VMEM(shape, kind) for shape, kind in kept],
            pltpu.SemaphoreType.DMA((len(near) + len(kept),)),
        ],
        compiler_params=pltpu.CompilerParams(vmem_limit_bytes=ROOM),
        cost_estimate=cost(microseconds),
        name=name,
    )(*small, *far, *near, *ties)


def window_scratch(T, D):
    return [
        pltpu.VMEM((4, T, D), bf16),
        pltpu.VMEM((4, TAIL, D), bf16),
        pltpu.VMEM((4, T), f32),
        pltpu.VMEM((4, T), f32),
        pltpu.VMEM((4 * T, 128), f32),
    ]


def self_near(numbers, segments, blocks, weights, vectors, ties=()):
    T, D = segments.shape[1], vectors.shape[1]
    wq, wk, wv = weights
    return run_kernel(
        self_near_kernel, "self_near", 13,
        [((T, D), bf16), ((H, VROWS, T), f32), ((16, 128), f32)],
        numbers, blocks[:3], [segments, vectors, wv, wq, wk],
        window_scratch(T, D)
        + [
            pltpu.VMEM((PAIRS, 4 * T, 128), bf16),
            pltpu.VMEM((H, VROWS, 4 * T), bf16),
            pltpu.VMEM((H, T), f32),
            pltpu.VMEM((H, T, 128), bf16),
            pltpu.SemaphoreType.DMA((8,)),
        ],
        ties,
    )


def self_far(numbers, segments, blocks, weights, vectors, queries, total, reach, opposite, ties=()):
    T, D = queries.shape
    return run_kernel(
        self_far_kernel, "self_far", 7,
        [((T, D), bf16), ((H, T), f32)],
        numbers, blocks, [*weights[1:], segments, vectors, queries, reach, opposite, total],
        window_scratch(T, D)
        + [
            pltpu.VMEM((PAIRS, 4 * T, 128), bf16),
            pltpu.VMEM((H, VROWS, 4 * T), bf16),
            pltpu.VMEM((H, T), f32),
            pltpu.VMEM((H, VROWS, T), f32),
            pltpu.VMEM((D, T), f32),
            pltpu.VMEM((H, T, 128), bf16),
            pltpu.SemaphoreType.DMA((8,)),
        ],
        ties,
    )


def backward_scratch(T, D):
    return window_scratch(T, D) + [
        pltpu.VMEM((PAIRS, 4 * T, 128), bf16),
        pltpu.VMEM((D, 4 * T), bf16),
        pltpu.VMEM((PAIRS, 4 * T, 128), bf16),
        pltpu.VMEM((PAIRS, 4 * T, 128), f32),
        pltpu.VMEM((PAIRS, 4 * T, 128), f32),
        pltpu.VMEM((H, T, 128), bf16),
        pltpu.VMEM((H, T, 128), bf16),
        pltpu.VMEM((H, T), f32),
    ]


def back_far(numbers, segments, blocks, weights, vectors, queries, blended, upstream, lse, opposite, ties=()):
    T, D = queries.shape
    return run_kernel(
        back_far_kernel, "back_far", 8,
        [((T, D), bf16), ((D, D), f32), ((D, D), f32), ((8, D), f32), ((D, T), f32)],
        numbers, blocks[3:],
        [segments, vectors, *weights[1:], queries, upstream, blended, lse, opposite],
        backward_scratch(T, D) + [pltpu.SemaphoreType.DMA((8,))],
        ties,
    )


def back_near(numbers, segments, blocks, weights, vectors, queries, blended, upstream, lse, entering, sums, far, ties=()):
    T, D = queries.shape
    wq, wk, wv = weights
    far_k, far_v, far_sum, far_query_t = far
    rows = 3 * D // 2 + D // 4
    return run_kernel(
        back_near_kernel, "back_near", 22,
        [((T, D), f32), ((T, D), bf16), ((T, D), bf16), ((rows, D), bf16), ((rows, D), bf16)],
        numbers, blocks[:3],
        [
            segments, vectors, wk, wv, queries, upstream, blended, lse, far_query_t,
            wq, entering, far_k, far_v, far_sum, *sums,
        ],
        backward_scratch(T, D)
        + [
            pltpu.VMEM((D, T), f32),
            pltpu.VMEM((D, D), f32),
            pltpu.VMEM((D, D), f32),
            pltpu.SemaphoreType.DMA((8,)),
        ],
        ties,
    )


def pack_kernel(ready, done, numbers, canvas, cotangent, *refs):
    *small, wide, segments, memory_segments, memory, vectors, payload, last, extras, held, semaphores = refs
    T, D = canvas.shape
    here = memory.shape[0]
    arrive = pltpu.make_async_copy(canvas, held, semaphores.at[0])
    arrive.start()
    rows = pltpu.make_async_copy(held, payload.at[pl.ds(0, T)], semaphores.at[3])
    copy = pltpu.make_async_copy(cotangent.at[pl.ds(T - TAIL, TAIL)], last, semaphores.at[1])
    copy.start()
    arrive.wait()
    rows.start()
    ready()

    def padded(row):
        if row.shape[1] == D:
            return row
        return jnp.concatenate([row, jnp.zeros((1, D - row.shape[1]), f32)], axis=1)

    row = lax.broadcasted_iota(jnp.int32, (TAIL, D), 0)
    copy.wait()
    codes = jnp.broadcast_to(padded(segments[...].astype(f32)), (TAIL, D))
    carried = jnp.broadcast_to(widen(last[...])[TAIL - 1 : TAIL], (TAIL, D))
    row_sum = jnp.broadcast_to(summed(held[...]), (TAIL, D))
    rest_of_sum = row_sum - widen(bfloat(row_sum))
    extras[0:TAIL, :] = bfloat(
        jnp.where(
            row == 0, codes,
            jnp.where(row == 1, carried, jnp.where(row == 2, row_sum, jnp.where(row == 3, rest_of_sum, 0.0))),
        )
    )
    extras[TAIL : TAIL + here, :] = memory[...]
    codes = jnp.broadcast_to(padded(memory_segments[...].astype(f32)), (TAIL, D))
    extras[TAIL + here : 2 * TAIL + here, :] = bfloat(jnp.where(row == 0, codes, 0.0))
    rest = pltpu.make_async_copy(extras, payload.at[pl.ds(T, 2 * TAIL + here)], semaphores.at[2])
    rest.start()
    for index, vector in enumerate(small):
        vectors[index : index + 1, :] = widen(vector[...])[None, :]
    values = widen(wide[...])
    for c in range(values.shape[0] // D):
        vectors[len(small) + c : len(small) + c + 1, :] = values[c * D : c * D + D][None, :]
    rows.wait()
    rest.wait()


def pack(numbers, small, wide, segments, memory_segments, memory, canvas, cotangent):
    T, D = canvas.shape
    size = 2 * TAIL + memory.shape[0]
    return run_kernel(
        pack_kernel, "pack", 2,
        [((len(small) + wide.shape[0] // D, D), f32), ((T + size, D), bf16)],
        numbers, [canvas, cotangent], [*small, wide, segments, memory_segments, memory],
        [pltpu.VMEM((TAIL, D), bf16), pltpu.VMEM((size, D), bf16), pltpu.VMEM((T, D), bf16), pltpu.SemaphoreType.DMA((4,))],
        (), 1,
    )


BQ1, BV1, BO1, G1, B1, BQ2, BV2, BO2, G2, B2, BR, G3, B3, BS, BE = range(15)


def smooth_gate(inputs):
    square = inputs * inputs
    bent = jnp.tanh(gelu_scale * inputs * (1.0 + gelu_cubic * square))
    half = 0.5 * (1.0 + bent)
    slope = half + 0.5 * inputs * (1.0 - bent * bent) * (
        gelu_scale * (1.0 + 3.0 * gelu_cubic * square)
    )
    return inputs * half, slope


def norm_forward(inputs):
    average = jnp.mean(inputs, axis=-1, keepdims=True)
    centred = inputs - average
    scaling = lax.rsqrt(jnp.mean(centred * centred, axis=-1, keepdims=True) + epsilon)
    return centred * scaling, scaling


def norm_backward(upstream, gain, normal, scaling):
    scaled = upstream * gain
    return scaling * (
        scaled
        - jnp.mean(scaled, axis=-1, keepdims=True)
        - normal * jnp.mean(scaled * normal, axis=-1, keepdims=True)
    )


def summed(values):
    return jnp.sum(widen(values), axis=0, keepdims=True)


def memory_moves(place, blocks, last_memory, gathered, semaphores, first):
    own, side, middle, middle_far, side_far = blocks
    size = gathered.shape[1]
    begin = own.shape[0] - size
    inner, beside, across, far = neighbours(place)

    def move(block, slot, index):
        return pltpu.make_async_copy(
            block.at[pl.ds(begin, size)], gathered.at[slot], semaphores.at[first + index]
        )

    def run(act):
        for copy in (move(own, place, 0), move(side, beside, 1)):
            act(copy)

        @pl.when(inner)
        def _():
            for copy in (move(middle, across, 2), move(middle_far, far, 3)):
                act(copy)

        @pl.when(jnp.logical_not(inner))
        def _():
            last = pltpu.make_async_copy(last_memory, gathered.at[3 - place], semaphores.at[first + 3])
            for copy in (move(side_far, far, 2), last):
                act(copy)

    return run


def memory_rows(gathered, memory, columns, memory_length):
    count, size, width = gathered.shape
    here = size - TAIL
    lane = lax.broadcasted_iota(jnp.int32, (1, here), 1)
    for b in range(count):
        span = slice(b * here, (b + 1) * here)
        memory[span, :] = gathered[b, 0:here, :]
        code = widen(gathered[b, here : here + 1, 0:here])
        columns[span, :] = as_column(jnp.where(b * here + lane < memory_length, code, -1.0))


def put_block(block, start, half, side, sent, kept):
    size = block.shape[0]
    for part in range(2):
        low, high = max(start, part * half), min(start + size, (part + 1) * half)
        if low >= high:
            continue
        rows = block[low - start : high - start]
        at = slice(low - part * half, high - part * half)

        @pl.when(side == part)
        def _():
            kept[at, :] = rows

        @pl.when(side != part)
        def _():
            sent[at, :] = rows


def forward_kernel(
    ready, done, numbers, own, side, middle, middle_far, side_far, last_memory,
    segments, vectors, ck, cv, canvas, blended, wo, cq, co, we, wr, ws, cotangent,
    slots_out, last_out, first_state, normal_out, scaling_out, low_out, query_out, fetched_out,
    lse, second_out, sums, gathered, sent, kept,
    tails, memory, columns, keys, values_t, summit, total,
    blend_t, q_sides, hidden, slope, second, low2, early, semaphores,
):
    T, D = canvas.shape
    M = memory.shape[0]
    FF = we.shape[1]
    place, length, memory_length = numbers[0], numbers[1], numbers[2]
    edges = [
        pltpu.make_async_copy(side.at[pl.ds(T, TAIL)], tails.at[0], semaphores.at[0]),
        pltpu.make_async_copy(middle.at[pl.ds(T, TAIL)], tails.at[1], semaphores.at[1]),
    ]
    bring = memory_moves(
        place, (own, side, middle, middle_far, side_far), last_memory, gathered, semaphores, 2
    )
    bring(start)
    for copy in edges:
        copy.start()
    leaving = []

    half = sent.shape[0]
    half_side = numbers[3]

    def leave(block, index):
        early[pl.ds(index * D, D), :] = block
        part, start_row = divmod(index * D, half)
        source = early.at[pl.ds(index * D, D)]
        rows = pl.ds(start_row, D)

        @pl.when(half_side == part)
        def _():
            pltpu.make_async_copy(source, kept.at[rows], semaphores.at[6 + index]).start()

        @pl.when(half_side != part)
        def _():
            pltpu.make_async_copy(source, sent.at[rows], semaphores.at[6 + index]).start()

        leaving.append(pltpu.make_async_copy(source, kept.at[rows], semaphores.at[6 + index]))

    def vector(index):
        return vectors[index : index + 1, :]

    sums[...] = jnp.zeros_like(sums)
    ready(2)
    code_row = segments[...].astype(f32)

    bring(wait)
    memory_rows(gathered, memory, columns, memory_length)
    done(11)
    ready(2)
    k = bfloat(matmul(memory[...], ck[...]))
    for pair in range(PAIRS):
        keys[pair] = k[:, 128 * pair : 128 * pair + 128]
    bias_t = as_column(vector(BV2))[:, 0:1]
    v_t = bfloat(times_transposed(jnp.transpose(cv[...]), memory[...]) + bias_t)
    for head in range(H):
        values_t[head, 0:HD, :] = v_t[HD * head : HD * head + HD]
        values_t[head, HD:VROWS, :] = jnp.ones((VROWS - HD, M), bf16)

    ready(3)
    first_in = widen(canvas[...]) + matmul(blended[...], wo[...]) + vector(BO1)
    normal, scaling = norm_forward(first_in)
    normal_out[...] = normal
    scaling_out[...] = jnp.broadcast_to(scaling, (T, 128))
    done(3, 4)
    first = normal * vector(G1) + vector(B1)
    low = bfloat(first)
    low_out[...] = low
    ready(1)
    query_out[...] = bfloat((matmul(low, cq[...]) + vector(BQ2)) * 0.125)
    done(5, 6)

    ones_of_heads = head_rows(bf16)
    q_all = query_out[...]
    reach = jnp.max(
        jnp.max(times_transposed(ones_of_heads, q_all * q_all), axis=1, keepdims=True)
        * jnp.max(times_transposed(ones_of_heads, k * k), axis=1, keepdims=True)
    )
    wide = reach > safe_square
    summit[...] = jnp.zeros_like(summit)
    total[...] = jnp.zeros_like(total)
    split_heads(q_all, q_sides)
    tiles = [slice(t, t + TILE) for t in range(0, M, TILE)]

    @pl.when(wide)
    def _():
        summit[...] = jnp.full(summit.shape, masked_score, f32)
        for at in tiles:
            look_at(at, keys, q_sides, columns, code_row, summit)

    for at in tiles:
        blend_at(at, keys, values_t, q_sides, columns, code_row, summit, total)
    fetched = normalise(total, summit, lse, blend_t)
    fetched_out[...] = fetched
    done(7, 8)

    ready(1)
    second_in = first + matmul(fetched, co[...]) + vector(BO2)
    normal2, scaling2 = norm_forward(second_in)
    second[...] = normal2 * vector(G2) + vector(B2)
    low2[...] = bfloat(second[...])
    ready(2)
    third_in = second[...] + vector(BR)
    for c in range(FF // D):
        lanes = slice(c * D, (c + 1) * D)
        before = matmul(low2[...], we[:, lanes]) + vector(BE + c)
        gate, bend = smooth_gate(before)
        gate = bfloat(gate)
        hidden[:, lanes] = gate
        slope[:, lanes] = bend
        third_in += matmul(gate, wr[lanes, :])
    normal3, scaling3 = norm_forward(third_in)
    states = bfloat(normal3 * vector(G3) + vector(B3))
    first_state[...] = states[0:TAIL]

    for copy in edges:
        copy.wait()
    ready()
    inner = jnp.logical_or(place == 1, place == 2)
    beside_tail, across_tail = widen(tails[0]), widen(tails[1])
    after_code = jnp.where(place == 1, across_tail[0:1, 0:1], beside_tail[0:1, 0:1])
    before_code = jnp.where(place == 2, across_tail[0:1, T - 1 : T], beside_tail[0:1, T - 1 : T])
    before_row = jnp.where(place == 2, across_tail[1:2, :], beside_tail[1:2, :])
    lane = lax.broadcasted_iota(jnp.int32, (8, T), 1)
    codes8 = jnp.broadcast_to(code_row, (8, T))
    live = jnp.where(place * T + lane < length, codes8, -1.0)
    next_code = jnp.where(lane == T - 1, after_code, pltpu.roll(live, T - 1, 1))
    valid8 = jnp.where(
        jnp.logical_and(next_code == codes8, place * T + lane + 1 < length), 1.0, 0.0
    )
    valid = as_column(valid8[0:1, :])[:, 0:1]
    last_valid = jnp.where(
        jnp.logical_and(before_code == code_row[:, 0:1], jnp.logical_and(place > 0, place * T < length)),
        1.0, 0.0,
    )
    row = lax.broadcasted_iota(jnp.int32, (T, D), 0)
    following = bfloat(jnp.where(row == T - 1, 0.0, pltpu.roll(widen(states), T - 1, 0)))
    raw = matmul(states, ws[0:D, :]) + vector(BS) + matmul(following, ws[D : 2 * D, :])
    slots_out[...] = bfloat(raw * valid)
    last_out[...] = jnp.concatenate(
        [raw[T - 1 : T], jnp.broadcast_to(valid[T - 1 : T], (1, D)), jnp.zeros((6, D), f32)], axis=0
    )
    done(0, 1, 2)
    masked = widen(cotangent[...]) * valid
    shifted = jnp.where(row == 0, before_row * last_valid, pltpu.roll(masked, 1, 0))
    masked_low, shifted_low = bfloat(masked), bfloat(shifted)
    upstream = times_transposed(masked_low, ws[0:D, :]) + widen(
        bfloat(times_transposed(shifted_low, ws[D : 2 * D, :]))
    )
    states_t = jnp.transpose(states)
    leave(bfloat(matmul(states_t, masked_low)), 0)
    leave(bfloat(matmul(states_t, shifted_low)), 1)
    sums[0:1, :] = summed(masked)

    third_grad = norm_backward(upstream, vector(G3), normal3, scaling3)
    sums[1:2, :] = summed(upstream * normal3)
    sums[2:3, :] = summed(upstream)
    third_low = bfloat(third_grad)
    sums[3:4, :] = summed(third_low)
    low2_t = jnp.transpose(low2[...])
    second_up = third_grad
    for c in range(FF // D):
        lanes = slice(c * D, (c + 1) * D)
        leave(bfloat(matmul(jnp.transpose(hidden[:, lanes]), third_low)), 2 + FF // D + c)
        hidden_grad = bfloat(times_transposed(third_low, wr[lanes, :]))
        before_grad = bfloat(widen(hidden_grad) * slope[:, lanes])
        leave(bfloat(matmul(low2_t, before_grad)), 2 + c)
        sums[4 + c : 5 + c, :] = summed(before_grad)
        second_up += times_transposed(before_grad, we[:, lanes])
    second_out[...] = norm_backward(second_up, vector(G2), normal2, scaling2)
    sums[8:9, :] = summed(second_up * normal2)
    sums[9:10, :] = summed(second_up)
    for copy in leaving:
        copy.wait()


def backward_kernel(
    ready, done, numbers,
    second_grad, co, segments, vectors, gathered, query, ck, cv, fetched, lse, cq, normal, scaling, wo, low,
    blended, first_state, wv, self_lse,
    first_grad_out, upstream_out, memory_out, sent, kept, sums,
    memory, columns, keys, keys_t, values, grad_keys, grad_values, query_t, upstream2, q_sides, u_sides, fixes,
):
    T, D = low.shape
    M = memory.shape[0]
    half_side = numbers[3]
    sums[...] = jnp.zeros_like(sums)
    ready(2)
    low_grad = bfloat(second_grad[...])
    upstream2[...] = bfloat(times_transposed(low_grad, co[...]))
    ready(4)
    code_row = segments[...].astype(f32)
    gain = vectors[G1 : G1 + 1, :]
    memory_rows(gathered, memory, columns, numbers[2])
    split_heads(query[...], q_sides)
    ready(2)
    k = bfloat(matmul(memory[...], ck[...]))
    v = bfloat(matmul(memory[...], cv[...]) + vectors[BV2 : BV2 + 1, :])
    for pair in range(PAIRS):
        keys[pair] = k[:, 128 * pair : 128 * pair + 128]
        values[pair] = v[:, 128 * pair : 128 * pair + 128]
    keys_t[...] = jnp.transpose(k)
    ready(2)
    fixes[...] = row_corrections(upstream2[...], fetched[...])
    split_heads(upstream2[...], u_sides)
    query_t[...] = jnp.zeros_like(query_t)
    for tile in range(M // TILE):
        step_back(
            slice(tile * TILE, (tile + 1) * TILE), keys, keys_t, values, q_sides, u_sides, columns,
            code_row, lse, fixes, query_t, grad_keys, grad_values,
        )
    query_rows = bfloat(jnp.transpose(query_t[...])) * 0.125
    ready()
    first_up = second_grad[...] + times_transposed(query_rows, cq[...])
    first_grad = norm_backward(first_up, gain, normal[...], scaling[:, 0:1])
    first_grad_out[...] = first_grad
    first_low = bfloat(first_grad)
    upstream_out[...] = bfloat(times_transposed(first_low, wo[...]))
    done(0, 1)
    gk, gv = tile_grads(slice(0, M), grad_keys, grad_values)
    part = bfloat(times_transposed(gk, ck[...]) + times_transposed(gv, cv[...]))
    count, size, _ = memory_out.shape
    here = size - TAIL
    place = numbers[0]
    tail = lax.broadcasted_iota(jnp.int32, (TAIL, D), 0)
    terms = jnp.broadcast_to(masked_terms(self_lse[...], upstream_out[...]), (TAIL, D))
    opposite_row = times_transposed(bfloat(terms), wv[...])
    for b in range(count):
        memory_out[b, 0:here, :] = part[b * here : (b + 1) * here]
        rows = jnp.where(jnp.logical_and(tail == 0, place == b + 1), widen(first_state[...]), 0.0)
        rows += jnp.where(
            jnp.logical_and(tail == 1, jnp.logical_and(is_outer(place), place == 3 - b)), opposite_row, 0.0
        )
        memory_out[b, here:size, :] = bfloat(rows)
    done(2)
    half = 5 * D // 2
    memory_t = jnp.transpose(memory[...])
    put_block(bfloat(matmul(jnp.transpose(low[...]), query_rows)), 0, half, half_side, sent, kept)
    put_block(bfloat(matmul(memory_t, gk)), D, half, half_side, sent, kept)
    put_block(bfloat(matmul(memory_t, gv)), 2 * D, half, half_side, sent, kept)
    put_block(bfloat(matmul(jnp.transpose(fetched[...]), low_grad)), 3 * D, half, half_side, sent, kept)
    put_block(bfloat(matmul(jnp.transpose(blended[...]), first_low)), 4 * D, half, half_side, sent, kept)
    sums[0:1, :] = summed(low_grad)
    sums[1:2, :] = summed(query_rows)
    sums[2:3, :] = summed(gv)
    sums[3:4, :] = summed(first_up * normal[...])
    sums[4:5, :] = summed(first_up)
    sums[5:6, :] = summed(first_low)


def middle_forward(numbers, segments, canvas, blended, cotangent, vectors, blocks, last_memory, weights, ties=()):
    T, D = canvas.shape
    wo, ck, cv, cq, co, we, wr, ws = weights
    FF = we.shape[1]
    here = last_memory.shape[0] - TAIL
    M = 4 * here
    rows = 2 * D + 2 * FF
    return run_kernel(
        forward_kernel, "middle_forward", 24,
        [
            ((T, D), bf16), ((8, D), f32), ((TAIL, D), bf16), ((T, D), f32), ((T, 128), f32), ((T, D), bf16),
            ((T, D), bf16), ((T, D), bf16), ((H, T), f32), ((T, D), f32),
            ((16, D), f32), ((4, here + TAIL, D), bf16), ((rows // 2, D), bf16), ((rows // 2, D), bf16),
        ],
        numbers, [*blocks, last_memory],
        [segments, vectors, ck, cv, canvas, blended, wo, cq, co, we, wr, ws, cotangent],
        [
            pltpu.VMEM((2, TAIL, D), bf16),
            pltpu.VMEM((M, D), bf16),
            pltpu.VMEM((M, 128), f32),
            pltpu.VMEM((PAIRS, M, 128), bf16),
            pltpu.VMEM((H, VROWS, M), bf16),
            pltpu.VMEM((H, T), f32),
            pltpu.VMEM((H, VROWS, T), f32),
            pltpu.VMEM((D, T), f32),
            pltpu.VMEM((H, T, 128), bf16),
            pltpu.VMEM((T, FF), bf16),
            pltpu.VMEM((T, FF), f32),
            pltpu.VMEM((T, D), f32),
            pltpu.VMEM((T, D), bf16),
            pltpu.VMEM((rows, D), bf16),
            pltpu.SemaphoreType.DMA((6 + rows // D,)),
        ],
        ties, 2,
    )


def middle_backward(numbers, segments, blended, gathered, vectors, saved, weights, ties=()):
    T, D = blended.shape
    M = gathered.shape[0] * (gathered.shape[1] - TAIL)
    rows = 5 * D // 2
    normal, scaling, low, query, fetched, lse, second_grad, first_state, self_lse = saved
    wo, cq, ck, cv, co, wv = weights
    return run_kernel(
        backward_kernel, "middle_backward", 16,
        [
            ((T, D), f32), ((T, D), bf16), (gathered.shape, bf16),
            ((rows, D), bf16), ((rows, D), bf16), ((8, D), f32),
        ],
        numbers, [],
        [
            second_grad, co, segments, vectors, gathered, query, ck, cv, fetched, lse,
            cq, normal, scaling, wo, low, blended, first_state, wv, self_lse,
        ],
        [
            pltpu.VMEM((M, D), bf16),
            pltpu.VMEM((M, 128), f32),
            pltpu.VMEM((PAIRS, M, 128), bf16),
            pltpu.VMEM((D, M), bf16),
            pltpu.VMEM((PAIRS, M, 128), bf16),
            pltpu.VMEM((PAIRS, M, 128), f32),
            pltpu.VMEM((PAIRS, M, 128), f32),
            pltpu.VMEM((D, T), f32),
            pltpu.VMEM((T, D), bf16),
            pltpu.VMEM((H, T, 128), bf16),
            pltpu.VMEM((H, T, 128), bf16),
            pltpu.VMEM((H, T), f32),
        ],
        ties,
    )


def pieces(start, count, half):
    found = []
    for part in range(2):
        low, high = max(start, part * half), min(start + count, (part + 1) * half)
        if low < high:
            found.append((part, low - part * half, low - start, high - low))
    return found


def unpack_kernel(layout, ready, done, numbers, mine, came, *outs):
    half, D = mine.shape
    half_side = numbers[3]
    ready()
    for number, (out, starts) in enumerate(zip(outs, layout)):
        count = out.shape[0]
        for column, start_row in enumerate(starts):
            lanes = slice(column * D, (column + 1) * D)
            for part, there, here, rows in pieces(start_row, count, half):
                step = min(rows, 512)
                for at in range(0, rows, step):
                    size = min(step, rows - at)
                    source = slice(there + at, there + at + size)
                    target = slice(here + at, here + at + size)

                    @pl.when(half_side == part)
                    def _():
                        out[target, lanes] = widen(mine[source, :])

                    @pl.when(half_side != part)
                    def _():
                        out[target, lanes] = widen(came[source, :])

        done(number)


def unpack(numbers, name, mine, came, layout, ties=()):
    D = mine.shape[1]
    return run_kernel(
        functools.partial(unpack_kernel, [starts for _, starts in layout]), name, 4,
        [((count, D * len(starts)), f32) for count, starts in layout],
        numbers, [], [mine, came], [], ties,
    )


def finish_kernel(
    ready, done, numbers, memory_stays, memory_came, last_slot, slots, bottom, base, onward, outward,
    memory_grad, slots_out, canvas_grad,
):
    T, D = slots.shape
    here = memory_grad.shape[0]
    ready(4)
    summed_rows = widen(memory_stays[...]) + widen(memory_came[...])
    memory_grad[...] = summed_rows[0:here]
    done(0)
    next_state = bfloat(summed_rows[here : here + TAIL])
    ready(1)
    last_row = (last_slot[0:1, :] + matmul(next_state, bottom[...])[0:1]) * last_slot[1:2, :]
    row = lax.broadcasted_iota(jnp.int32, (TAIL, D), 0)
    slots_out[0 : T - TAIL, :] = slots[0 : T - TAIL, :]
    slots_out[T - TAIL : T, :] = bfloat(
        jnp.where(row == TAIL - 1, last_row, widen(slots[T - TAIL : T, :]))
    )
    done(1)
    ready()
    canvas_grad[...] = base[...] + summed_rows[here + 1 : here + 2] + widen(onward[...]) + widen(outward[...])


def finish(numbers, memory_stays, memory_came, last_slot, slots, bottom, base, onward, outward, ties=()):
    T, D = slots.shape
    return run_kernel(
        finish_kernel, "finish", 3,
        [((memory_stays.shape[0] - TAIL, D), f32), ((T, D), bf16), ((T, D), f32)],
        numbers, [], [memory_stays, memory_came, last_slot, slots, bottom, base, onward, outward], [], ties,
    )


SIDE = [(0, 1), (1, 0), (2, 3), (3, 2)]
MIDDLE = [(1, 2), (2, 1)]
OUTWARD = [(1, 0), (2, 3)]
INWARD = [(0, 1), (3, 2)]


def routes():
    bits = [("rows", 1 << b) for b in range((lax.axis_size("rows") - 1).bit_length())]
    along = [("seq", 1 << b) for b in range((lax.axis_size("seq") - 1).bit_length())]
    return bits[0], bits[1:], bits[:0:-1], along


def swap(block, step):
    axis, bit = step
    return lax.ppermute(block, axis, [(i, i ^ bit) for i in range(lax.axis_size(axis))])


def side_of(step):
    axis, bit = step
    return jnp.where((lax.axis_index(axis) & bit) != 0, 1, 0)


def halves(terms, step):
    side = side_of(step)
    half = terms[0].shape[0] // 2

    def part(which):
        pieces = [widen(lax.dynamic_slice_in_dim(t, which * half, half)) for t in terms]
        return bfloat(sum(pieces[1:], pieces[0]))

    return part(1 - side), part(side)


def ordered(block, came, step):
    side = side_of(step) == 1
    return jnp.where(side, came, block), jnp.where(side, block, came)


class Order:
    def __init__(self):
        self.last = []

    def made(self, *values):
        self.last = list(values)

    def after(self, *values):
        if not self.last:
            return values
        values, _ = lax.optimization_barrier((values, tuple(self.last)))
        return values


class Summing:
    def __init__(self, order, sent, kept, split):
        self.order = order
        self.split = split
        self.steps = self.run(sent, kept)
        self.whole = None
        next(self.steps)

    def step(self):
        if self.whole is not None:
            return
        try:
            self.order.made(*next(self.steps))
        except StopIteration as end:
            self.whole = end.value

    def finish(self):
        while self.whole is None:
            self.step()
        return self.whole

    def take(self, blocks):
        return self.order.after(*blocks)

    def run(self, sent, kept):
        first, up, down, along = routes()
        came = swap(sent, first)
        yield [sent]
        (came,) = self.take([came])
        size = kept.shape[0]
        if self.split == 2:
            ways = [(up, 0, size // 2), (down, size // 2, size // 2)]
        else:
            ways = [(down if self.split else up, 0, size)]
        lanes = [[kept[at : at + n], came[at : at + n]] for _, at, n in ways]
        for number in range(len(up)):
            parts = [halves(terms, way[number]) for terms, (way, _, _) in zip(lanes, ways)]
            came = [swap(goes, way[number]) for (goes, _), (way, _, _) in zip(parts, ways)]
            yield [goes for goes, _ in parts]
            came = self.take(came)
            lanes = [[stays, block] for (_, stays), block in zip(parts, came)]
        parts = [halves(terms, along[0]) for terms in lanes]
        cut = parts[0][0].shape[0]
        goes = jnp.concatenate([p[0] for p in parts], axis=0)
        stays = jnp.concatenate([p[1] for p in parts], axis=0)
        came = swap(goes, along[0])
        yield [goes]
        (came,) = self.take([came])
        mine = bfloat(widen(stays) + widen(came))
        for step in along[1:]:
            came = swap(mine, step)
            yield [mine]
            (came,) = self.take([came])
            mine = bfloat(widen(mine) + widen(came))
        came = swap(mine, along[0])
        yield [mine]
        (came,) = self.take([came])
        low, high = ordered(mine, came, along[0])
        lanes = [
            jnp.concatenate([low[n * cut : n * cut + cut], high[n * cut : n * cut + cut]], axis=0)
            for n in range(len(ways))
        ]
        for number in range(len(up) - 1, -1, -1):
            came = [swap(block, way[number]) for block, (way, _, _) in zip(lanes, ways)]
            yield lanes
            came = self.take(came)
            lanes = [
                jnp.concatenate(ordered(block, other, way[number]), axis=0)
                for block, other, (way, _, _) in zip(lanes, came, ways)
            ]
        block = lanes[0] if len(lanes) == 1 else jnp.concatenate(lanes, axis=0)
        came = swap(block, first)
        yield [block]
        return block, came


def entry_halves(block, step, bit):
    count = block.shape[0]
    grouped = block.reshape(count // (2 * bit), 2, bit, *block.shape[1:])
    side = side_of(step)
    take = lambda which: lax.dynamic_index_in_dim(grouped, which, 1, False).reshape(
        count // 2, *block.shape[1:]
    )
    return take(1 - side), take(side)


def shards(
    canvas,
    memory,
    cotangent,
    canvas_lengths,
    canvas_segments,
    memory_segments,
    memory_lengths,
    self_query,
    self_key,
    self_value,
    self_output,
    self_query_bias,
    self_value_bias,
    self_output_bias,
    first_gain,
    first_bias,
    cross_query,
    cross_key,
    cross_value,
    cross_output,
    cross_query_bias,
    cross_value_bias,
    cross_output_bias,
    second_gain,
    second_bias,
    expand_weight,
    expand_bias,
    reduce_weight,
    reduce_bias,
    third_gain,
    third_bias,
    slot_weight,
    slot_bias,
):
    place = lax.axis_index("seq")
    tokens_here = canvas.shape[1]
    width = canvas.shape[2]
    wide = expand_weight.shape[1]
    row = canvas[0]
    numbers = [
        jnp.stack([place, side_of(routes()[0])]).astype(jnp.int32),
        canvas_lengths, memory_lengths, canvas_segments,
    ]
    vectors, payload = pack(
        numbers,
        (
            self_query_bias, self_value_bias, self_output_bias, first_gain, first_bias,
            cross_query_bias, cross_value_bias, cross_output_bias, second_gain, second_bias,
            reduce_bias, third_gain, third_bias, slot_bias,
        ),
        expand_bias, canvas_segments, memory_segments, memory[0], row, cotangent[0],
    )
    side, middle = lax.ppermute(payload, "seq", SIDE), lax.ppermute(payload, "seq", MIDDLE)
    opposite = lax.ppermute(payload[tokens_here : tokens_here + TAIL], "seq", [(0, 3), (3, 0)])
    blocks = (
        payload, side, middle, lax.ppermute(side, "seq", MIDDLE), lax.ppermute(middle, "seq", OUTWARD)
    )
    last_memory = lax.ppermute(blocks[3][tokens_here + TAIL :], "seq", OUTWARD)
    projections = (self_query, self_key, self_value)

    queries, total, reach = self_near(numbers, canvas_segments, blocks, projections, vectors)
    blended, masses = self_far(
        numbers, canvas_segments, blocks, projections, vectors, queries, total, reach, opposite
    )
    (
        slots, last_slot, first_state, normal, scaling, low, cross_rows, fetched, cross_masses,
        second_grad, early_sums, gathered, early_sent, early_kept,
    ) = middle_forward(
        numbers, canvas_segments, row, blended, cotangent[0], vectors, blocks, last_memory,
        (self_output, cross_key, cross_value, cross_query, cross_output, expand_weight, reduce_weight, slot_weight),
    )
    order = Order()
    early = Summing(order, early_sent, early_kept, 2)
    early.step()
    first_grad, blended_grad, memory_part, later_sent, later_kept, later_sums = middle_backward(
        numbers, canvas_segments, blended, gathered, vectors,
        (normal, scaling, low, cross_rows, fetched, cross_masses, second_grad, first_state, masses),
        (self_output, cross_query, cross_key, cross_value, cross_output, self_value), order.last,
    )
    order.made(later_sums)
    early.step()
    later = Summing(order, later_sent, later_kept, LATER_SPLIT)
    far_part, *far = back_far(
        numbers, canvas_segments, blocks, projections, vectors, queries, blended, blended_grad, masses,
        opposite, order.last,
    )
    order.made(far[2])
    from_side = lax.ppermute(far_part, "seq", INWARD)
    from_middle = lax.ppermute(far_part, "seq", MIDDLE)
    near_step, far_step = routes()[3]
    memory_goes, memory_stays = entry_halves(memory_part, near_step, 1)
    memory_came = swap(memory_goes, near_step)
    early.step()
    (memory_came,) = order.after(memory_came)
    half_sum = bfloat(widen(memory_stays) + widen(memory_came))
    memory_goes, memory_stays = entry_halves(half_sum, far_step, 1)
    memory_came = swap(memory_goes, far_step)
    order.made(*order.last, memory_goes)
    later.step()
    canvas_base, middle_part, side_part, last_sent, last_kept = back_near(
        numbers, canvas_segments, blocks, projections, vectors, queries, blended, blended_grad, masses,
        first_grad, (early_sums, later_sums), far, order.last,
    )
    order.made(last_sent)
    last = Summing(order, last_sent, last_kept, LAST_SPLIT)
    finals = {}
    turns = {"E": early, "M": later, "S": last}
    for turn in TURNS:
        if turn in turns:
            turns[turn].step()
        elif turn == "1":
            from_side, from_middle = order.after(from_side, from_middle)
            middle_part = bfloat(widen(middle_part) + widen(from_side))
            side_part = bfloat(widen(side_part) + widen(from_middle))
            onward = lax.ppermute(middle_part, "seq", MIDDLE)
            outward = lax.ppermute(side_part, "seq", SIDE)
            order.made(middle_part, side_part)
        elif turn == "s":
            *self_grads, sums = unpack(
                numbers, "last_out", *last.finish(),
                [(width, [c * width]) for c in range(3)] + [(32, [3 * width])], order.last,
            )
            order.made(sums)
        elif turn == "e":
            count = 2 * width
            grad_slot, grad_expand, grad_reduce = unpack(
                numbers, "early_out", *early.finish(),
                [
                    (count, [0]),
                    (width, list(range(count, count + wide, width))),
                    (wide, [count + wide]),
                ],
                order.last,
            )
            order.made(grad_slot)
        elif turn == "m":
            cross_grads = unpack(
                numbers, "later_out", *later.finish(),
                [(width, [c * width]) for c in range(5)], order.last,
            )
            order.made(cross_grads[0])
        elif turn == "c":
            memory_grad, slots, canvas_grad = finish(
                numbers, memory_stays[0], memory_came[0], last_slot, slots, slot_weight[width:],
                canvas_base, onward, outward, order.last,
            )
            order.made(memory_grad)
    return (
        slots[None],
        canvas_grad[None],
        memory_grad[None],
        self_grads[0],
        self_grads[1],
        self_grads[2],
        cross_grads[4],
        sums[24],
        sums[25],
        sums[21],
        sums[19],
        sums[20],
        cross_grads[0],
        cross_grads[1],
        cross_grads[2],
        cross_grads[3],
        sums[17],
        sums[18],
        sums[16],
        sums[8],
        sums[9],
        grad_expand,
        sums[4:8].reshape(-1),
        grad_reduce,
        sums[3],
        sums[1],
        sums[2],
        grad_slot,
        sums[0],
    )


def solution(mesh):
    placed = (
        P("rows", "seq", None),
        P("rows", "seq", None),
        P("rows", "seq", None),
        P("rows"),
        P("rows", "seq"),
        P("rows", "seq"),
        P("rows"),
        P(),
        P(),
        P(),
        P(),
        P(),
        P(),
        P(),
        P(),
        P(),
        P(),
        P(),
        P(),
        P(),
        P(),
        P(),
        P(),
        P(),
        P(),
        P(),
        P(),
        P(),
        P(),
        P(),
        P(),
        P(),
        P(),
    )
    return jax.shard_map(
        shards,
        mesh=mesh,
        in_specs=placed,
        out_specs=(
            P("rows", "seq", None),
            P("rows", "seq", None),
            P("rows", "seq", None),
            P(),
            P(),
            P(),
            P(),
            P(),
            P(),
            P(),
            P(),
            P(),
            P(),
            P(),
            P(),
            P(),
            P(),
            P(),
            P(),
            P(),
            P(),
            P(),
            P(),
            P(),
            P(),
            P(),
            P(),
            P(),
            P(),
        ),
        check_vma=False,
    )
```

```python
import functools

import jax
import jax.numpy as jnp
from jax import lax
from jax.experimental import pallas as pl
from jax.experimental.pallas import tpu as pltpu
from jax.sharding import PartitionSpec as P

H = 8
HD = 64
PAIRS = H // 2
TILE = 256
TAIL = 16
LAST_SPLIT = 2
LATER_SPLIT = 0
TURNS = "EM1SMSEMSESMEMSSESMceSMsm"
VROWS = 80
ROOM = 58 * 1024 * 1024

masked_score = -30000.0
epsilon = 1e-05
gelu_scale = 0.7978845608028654
gelu_cubic = 0.044715
safe_square = 3600.0
bf16 = jnp.bfloat16
f32 = jnp.float32


def cost(microseconds):
    return pl.CostEstimate(flops=int(microseconds * 1.1e9), bytes_accessed=0, transcendentals=0)


def matmul(left, right):
    return jnp.dot(left, right, preferred_element_type=f32)


def times_transposed(left, right):
    return lax.dot_general(left, right, (((1,), (1,)), ((), ())), preferred_element_type=f32)


def bfloat(values):
    return values.astype(bf16)


def widen(values):
    return values.astype(f32)


def head_rows(dtype):
    row = lax.broadcasted_iota(jnp.int32, (16, H * HD), 0)
    column = lax.broadcasted_iota(jnp.int32, (16, H * HD), 1)
    return jnp.where(column // HD == row, 1.0, 0.0).astype(dtype)


def one_head(pair_columns, side):
    lane = lax.broadcasted_iota(jnp.int32, pair_columns.shape, 1)
    wanted = lane < HD if side == 0 else lane >= HD
    return jnp.where(wanted, widen(pair_columns), 0.0).astype(bf16)


def neighbours(place):
    inner = jnp.logical_or(place == 1, place == 2)
    beside = place + 1 - 2 * lax.rem(place, 2)
    across = 3 - place
    far = jnp.where(inner, across + 1 - 2 * lax.rem(across, 2), 3 - beside)
    return inner, beside, across, far


def window_moves(place, blocks, window, tails, semaphores):
    own, side, middle, middle_far, side_far = blocks
    inner, beside, across, far = neighbours(place)
    outer = jnp.logical_not(inner)
    T = window.shape[1]

    def move(block, slot, index):
        return (
            pltpu.make_async_copy(block.at[pl.ds(0, T)], window.at[slot], semaphores.at[2 * index]),
            pltpu.make_async_copy(
                block.at[pl.ds(T, TAIL)], tails.at[slot], semaphores.at[2 * index + 1]
            ),
        )

    def near(act):
        for copy in move(own, place, 0) + move(side, beside, 1):
            act(copy)

        @pl.when(inner)
        def _():
            for copy in move(middle, across, 2):
                act(copy)

    def distant(act):
        @pl.when(inner)
        def _():
            for copy in move(middle_far, far, 3):
                act(copy)

        @pl.when(outer)
        def _():
            for copy in move(side_far, far, 3):
                act(copy)

    return near, distant


def is_outer(place):
    return jnp.logical_or(place == 0, place == 3)


def present_tiles(place, per, with_far):
    reach = 2 if with_far else 1
    return jnp.maximum(place - reach, 0) * per, jnp.minimum(place + reach + 1, 4) * per


def masked_chances(lse):
    return jnp.exp(masked_score - lse)


def masked_terms(lse, upstream):
    chances = jnp.concatenate([masked_chances(lse), jnp.zeros((8, lse.shape[1]), f32)], axis=0)
    terms = matmul(bfloat(chances), upstream)
    return jnp.sum(jnp.where(head_rows(f32) > 0.0, terms, 0.0), axis=0, keepdims=True)


def start(copy):
    copy.start()


def wait(copy):
    copy.wait()


def no_codes(codes, keycodes, pivot):
    T = codes.shape[1]
    for slot in range(4):
        codes[slot : slot + 1, :] = jnp.full((1, T), 1.0, f32) * jnp.where(slot < pivot, -8.0, 8.0)
        keycodes[slot : slot + 1, :] = jnp.full((1, T), -9.0, f32)


def read_codes(codes, keycodes, tails, slot, length):
    T = codes.shape[1]
    lane = lax.broadcasted_iota(jnp.int32, (1, T), 1)
    code = widen(tails[slot, 0:1, 0:T])
    codes[pl.ds(slot, 1), :] = code
    keycodes[pl.ds(slot, 1), :] = jnp.where(slot * T + lane < length, code, -1.0)


def near_codes(codes, keycodes, tails, place, length):
    inner, beside, across, _ = neighbours(place)
    read_codes(codes, keycodes, tails, place, length)
    read_codes(codes, keycodes, tails, beside, length)

    @pl.when(inner)
    def _():
        read_codes(codes, keycodes, tails, across, length)


def tile_range(codes, first_code, last_code):
    below = jnp.sum(jnp.where(codes[...] < first_code, 1, 0))
    through = jnp.sum(jnp.where(codes[...] <= last_code, 1, 0))
    return below // TILE, (through + TILE - 1) // TILE


def as_column(row):
    return jnp.transpose(jnp.broadcast_to(row, (128, row.shape[1])))


def column_codes(keycodes, columns, tile, T):
    per = T // TILE
    row = keycodes[pl.ds(tile // per, 1), pl.ds(pl.multiple_of(lax.rem(tile, per) * TILE, TILE), TILE)]
    columns[pl.ds(pl.multiple_of(tile * TILE, TILE), TILE), :] = as_column(row)


def tile_rows(window, tile):
    per = window.shape[1] // TILE
    return window[tile // per, pl.ds(pl.multiple_of(lax.rem(tile, per) * TILE, TILE), TILE), :]


def split_heads(rows, sides):
    for head in range(H):
        sides[head] = one_head(rows[:, 128 * (head // 2) : 128 * (head // 2) + 128], head % 2)


def visible_in(columns, at, code_row):
    column = columns[at, :]
    return jnp.concatenate([column] * (code_row.shape[1] // 128), axis=1) == code_row


def look_at(at, keys, q_sides, columns, code_row, summit):
    visible = visible_in(columns, at, code_row)
    for head in range(H):
        scores = times_transposed(keys[head // 2, at, :], q_sides[head])
        scores = jnp.where(visible, scores, masked_score)
        summit[head : head + 1, :] = jnp.maximum(
            summit[head : head + 1, :], jnp.max(scores, axis=0, keepdims=True)
        )


def blend_at(at, keys, values_t, q_sides, columns, code_row, summit, total):
    visible = visible_in(columns, at, code_row)
    for head in range(H):
        scores = jnp.where(visible, times_transposed(keys[head // 2, at, :], q_sides[head]), masked_score)
        powers = bfloat(jnp.exp(scores - summit[head : head + 1, :]))
        total[head] += matmul(values_t[head, :, at], powers)


def normalise(total, summit, lse, blend_t):
    for head in range(H):
        mass = total[head, HD : HD + 1, :]
        blend_t[HD * head : HD * head + HD, :] = total[head, 0:HD, :] / mass
        lse[head : head + 1, :] = summit[head : head + 1, :] + jnp.log(mass)
    return bfloat(jnp.transpose(blend_t[...]))


def row_corrections(upstream, blended):
    products = widen(upstream) * widen(blended)
    coarse = bfloat(products)
    fine = bfloat(products - widen(coarse))
    ones_of_heads = head_rows(bf16)
    both = times_transposed(ones_of_heads, coarse) + times_transposed(ones_of_heads, fine)
    return both[0:H]


def step_back(at, keys, keys_t, values, q_sides, u_sides, columns, code_row, lse, fixes, query_t, grad_keys, grad_values):
    visible = visible_in(columns, at, code_row)
    for pair in range(PAIRS):
        k = keys[pair, at, :]
        v = values[pair, at, :]
        key_add = value_add = None
        for head in (2 * pair, 2 * pair + 1):
            q_side, u_side = q_sides[head], u_sides[head]
            scores = jnp.where(visible, times_transposed(k, q_side), masked_score)
            chances = jnp.exp(scores - lse[head : head + 1, :])
            chance_grad = times_transposed(v, u_side) - fixes[head : head + 1, :]
            score_grad = bfloat(jnp.where(visible, chances * chance_grad, 0.0))
            to_values = matmul(bfloat(chances), u_side)
            to_keys = matmul(score_grad, q_side)
            value_add = to_values if value_add is None else value_add + to_values
            key_add = to_keys if key_add is None else key_add + to_keys
            rows = slice(HD * head, HD * head + HD)
            query_t[rows, :] += matmul(keys_t[rows, at], score_grad)
        grad_keys[pair, at, :] = key_add
        grad_values[pair, at, :] = value_add


def tile_at(tile):
    return pl.ds(pl.multiple_of(tile * TILE, TILE), TILE)


def project_forward(tile, window, keycodes, columns, keys, values_t, wk, weights_t, bias_t):
    x = tile_rows(window, tile)
    at = tile_at(tile)
    k = bfloat(matmul(x, wk[...]))
    for pair in range(PAIRS):
        keys[pair, at, :] = k[:, 128 * pair : 128 * pair + 128]
    v_t = bfloat(times_transposed(weights_t, x) + bias_t)
    for head in range(H):
        values_t[head, 0:HD, at] = v_t[HD * head : HD * head + HD]
        values_t[head, HD:VROWS, at] = jnp.ones((VROWS - HD, TILE), bf16)
    column_codes(keycodes, columns, tile, window.shape[1])
    return times_transposed(head_rows(bf16), k * k)


def self_near_kernel(
    ready, done, numbers, own, side, middle, segments, vectors, wv, wq, wk,
    queries, total, reach_out,
    window, tails, codes, keycodes, columns, keys, values_t, zeros, q_sides, semaphores,
):
    T, D = queries.shape
    place, length = numbers[0], numbers[1]
    near, _ = window_moves(place, (own, side, middle, middle, side), window, tails, semaphores)
    near(start)
    no_codes(codes, keycodes, place)
    ready()
    weights_t = jnp.transpose(wv[...])
    bias_t = as_column(vectors[BV1 : BV1 + 1, :])[:, 0:1]
    near(wait)
    near_codes(codes, keycodes, tails, place, length)
    low, high = tile_range(codes, numbers[4].astype(f32), numbers[5].astype(f32))
    rows_q = bfloat((matmul(window[place], wq[...]) + vectors[BQ1 : BQ1 + 1, :]) * 0.125)
    queries[...] = rows_q
    done(0)
    split_heads(rows_q, q_sides)

    def project(tile, reach):
        return jnp.maximum(
            reach, project_forward(tile, window, keycodes, columns, keys, values_t, wk, weights_t, bias_t)
        )

    key_reach = lax.fori_loop(low, high, project, jnp.zeros((16, TILE), f32))
    reach_out[...] = jnp.broadcast_to(jnp.max(key_reach, axis=1, keepdims=True), (16, 128))
    zeros[...] = jnp.zeros_like(zeros)
    total[...] = jnp.zeros_like(total)
    code_row = segments[...].astype(f32)

    def blend(tile, _):
        blend_at(tile_at(tile), keys, values_t, q_sides, columns, code_row, zeros, total)
        return 0

    lax.fori_loop(low, high, blend, 0)


def self_far_kernel(
    ready, done, numbers, own, side, middle, middle_far, side_far,
    wk, wv, segments, vectors, queries, near_reach, opposite, near_total,
    out, lse,
    window, tails, codes, keycodes, columns, keys, values_t, summit, total, blend_t, q_sides, semaphores,
):
    T, D = out.shape
    place, length = numbers[0], numbers[1]
    _, _, _, far = neighbours(place)
    near, distant = window_moves(
        place, (own, side, middle, middle_far, side_far), window, tails, semaphores
    )
    distant(start)
    no_codes(codes, keycodes, far)
    ready()
    weights_t = jnp.transpose(wv[...])
    bias_t = as_column(vectors[BV1 : BV1 + 1, :])[:, 0:1]
    ones_of_heads = head_rows(bf16)
    rows_q = queries[...]
    split_heads(rows_q, q_sides)
    query_reach = jnp.max(times_transposed(ones_of_heads, rows_q * rows_q), axis=1, keepdims=True)
    first, last = numbers[4].astype(f32), numbers[5].astype(f32)
    distant(wait)
    read_codes(codes, keycodes, tails, far, length)
    low, high = tile_range(codes, first, last)

    def project(tile, reach):
        return jnp.maximum(
            reach, project_forward(tile, window, keycodes, columns, keys, values_t, wk, weights_t, bias_t)
        )

    key_reach = lax.fori_loop(low, high, project, jnp.zeros((16, TILE), f32))
    key_reach = jnp.maximum(jnp.max(key_reach, axis=1, keepdims=True), near_reach[:, 0:1])
    wide = jnp.max(query_reach * key_reach) > safe_square
    summit[...] = jnp.zeros_like(summit)
    total[...] = near_total[...]
    code_row = segments[...].astype(f32)

    per = T // TILE
    low_here, high_here = present_tiles(place, per, True)

    @pl.when(wide)
    def _():
        near(start)
        near(wait)
        near_codes(codes, keycodes, tails, place, length)
        lax.fori_loop(low_here, high_here, project, jnp.zeros((16, TILE), f32))
        total[...] = jnp.zeros_like(total)
        summit[...] = jnp.full(summit.shape, masked_score, f32)

        def look(tile, _):
            look_at(tile_at(tile), keys, q_sides, columns, code_row, summit)
            return 0

        lax.fori_loop(low_here, high_here, look, 0)

        @pl.when(is_outer(place))
        def _():
            sums = times_transposed(weights_t, opposite[...])
            column = sums[:, 2:3] + sums[:, 3:4] + T * bias_t
            for head in range(H):
                part = jnp.concatenate(
                    [column[HD * head : HD * head + HD], jnp.full((VROWS - HD, 1), T, f32)], axis=0
                )
                total[head] = part * jnp.exp(masked_score - summit[head : head + 1, :])

    def blend(tile, _):
        blend_at(tile_at(tile), keys, values_t, q_sides, columns, code_row, summit, total)
        return 0

    lax.fori_loop(
        jnp.where(wide, low_here, low), jnp.where(wide, high_here, high), blend, 0
    )
    out[...] = normalise(total, summit, lse, blend_t)


def project_backward(tile, window, keycodes, columns, keys, keys_t, values, wk, wv, bias, weights_t):
    x = tile_rows(window, tile)
    at = tile_at(tile)
    k = bfloat(matmul(x, wk[...]))
    v = bfloat(matmul(x, wv[...]) + bias)
    for pair in range(PAIRS):
        keys[pair, at, :] = k[:, 128 * pair : 128 * pair + 128]
        values[pair, at, :] = v[:, 128 * pair : 128 * pair + 128]
    keys_t[:, at] = bfloat(times_transposed(weights_t, x))
    column_codes(keycodes, columns, tile, window.shape[1])


def tile_grads(at, grad_keys, grad_values):
    gk = jnp.concatenate([bfloat(grad_keys[pair, at, :]) for pair in range(PAIRS)], axis=1)
    gv = jnp.concatenate([bfloat(grad_values[pair, at, :]) for pair in range(PAIRS)], axis=1)
    return gk, gv


def back_far_kernel(
    ready, done, numbers, middle_far, side_far,
    segments, vectors, wk, wv, queries, upstream, blended, lse, opposite,
    part_out, grad_k, grad_v, value_sum, query_t,
    window, tails, codes, keycodes, columns, keys, keys_t, values, grad_keys, grad_values,
    q_sides, u_sides, fixes, semaphores,
):
    T, D = queries.shape
    place, length = numbers[0], numbers[1]
    _, _, _, far = neighbours(place)
    _, distant = window_moves(
        place, (side_far, side_far, side_far, middle_far, side_far), window, tails, semaphores
    )
    distant(start)
    ready()
    no_codes(codes, keycodes, far)
    part_out[...] = jnp.zeros_like(part_out)
    query_t[...] = jnp.zeros_like(query_t)
    grad_k[...] = jnp.zeros_like(grad_k)
    grad_v[...] = jnp.zeros_like(grad_v)
    value_sum[...] = jnp.zeros_like(value_sum)
    distant(wait)
    read_codes(codes, keycodes, tails, far, length)
    low, high = tile_range(codes, numbers[4].astype(f32), numbers[5].astype(f32))
    code_row = segments[...].astype(f32)
    per = T // TILE
    deep = jnp.max(masked_chances(lse[...])) > 0.0
    low = jnp.where(deep, far * per, low)
    high = jnp.where(deep, far * per + per, high)

    @pl.when(jnp.logical_and(deep, is_outer(place)))
    def _():
        terms = masked_terms(lse[...], upstream[...])
        terms_8 = jnp.broadcast_to(terms, (TAIL, D))
        row = lax.broadcasted_iota(jnp.int32, (TAIL, D), 0)
        rows = jnp.where(jnp.logical_or(row == 2, row == 3), widen(opposite[...]), 0.0)
        grad_v[...] += matmul(jnp.transpose(rows), jnp.where(row < 4, terms_8, 0.0))
        value_sum[0:1, :] += T * terms

    @pl.when(high > low)
    def _():
        weights_t = jnp.transpose(wk[...])
        split_heads(queries[...], q_sides)
        split_heads(upstream[...], u_sides)
        fixes[...] = row_corrections(upstream[...], blended[...])

        def step(tile, _):
            project_backward(
                tile, window, keycodes, columns, keys, keys_t, values, wk, wv,
                vectors[BV1 : BV1 + 1, :], weights_t,
            )
            at = tile_at(tile)
            step_back(
                at, keys, keys_t, values, q_sides, u_sides, columns, code_row, lse, fixes, query_t,
                grad_keys, grad_values,
            )
            gk, gv = tile_grads(at, grad_keys, grad_values)
            x_t = jnp.transpose(tile_rows(window, tile))
            grad_k[...] += matmul(x_t, gk)
            grad_v[...] += matmul(x_t, gv)
            value_sum[0:1, :] += summed(gv)
            inside = pl.ds(pl.multiple_of(lax.rem(tile, T // TILE) * TILE, TILE), TILE)
            part_out[inside, :] = bfloat(times_transposed(gk, wk[...]) + times_transposed(gv, wv[...]))
            return 0

        lax.fori_loop(low, high, step, 0)


def back_near_kernel(
    ready, done, numbers, own, side, middle,
    segments, vectors, wk, wv, queries, upstream, blended, lse, far_query_t,
    wq, entering, far_k, far_v, far_sum, sums_one, sums_two,
    canvas_out, middle_out, side_out, sent, kept,
    window, tails, codes, keycodes, columns, keys, keys_t, values, grad_keys, grad_values,
    q_sides, u_sides, fixes, query_t, grad_k, grad_v, late, semaphores,
):
    T, D = queries.shape
    place, length = numbers[0], numbers[1]
    per = T // TILE
    near, _ = window_moves(place, (own, side, middle, middle, side), window, tails, semaphores)
    near(start)
    no_codes(codes, keycodes, place)
    ready(9)
    weights_t = jnp.transpose(wk[...])
    split_heads(queries[...], q_sides)
    split_heads(upstream[...], u_sides)
    fixes[...] = row_corrections(upstream[...], blended[...])
    query_t[...] = far_query_t[...]
    middle_out[...] = jnp.zeros_like(middle_out)
    side_out[...] = jnp.zeros_like(side_out)
    near(wait)
    near_codes(codes, keycodes, tails, place, length)
    low, high = tile_range(codes, numbers[4].astype(f32), numbers[5].astype(f32))
    code_row = segments[...].astype(f32)
    deep = jnp.max(masked_chances(lse[...])) > 0.0
    low_here, high_here = present_tiles(place, per, False)
    low, high = jnp.where(deep, low_here, low), jnp.where(deep, high_here, high)

    def step(tile, _):
        project_backward(
            tile, window, keycodes, columns, keys, keys_t, values, wk, wv,
            vectors[BV1 : BV1 + 1, :], weights_t,
        )
        step_back(
            tile_at(tile), keys, keys_t, values, q_sides, u_sides, columns, code_row, lse, fixes, query_t,
            grad_keys, grad_values,
        )
        return 0

    lax.fori_loop(low, high, step, 0)
    ready()
    grad_k[...] = far_k[...]
    grad_v[...] = far_v[...]
    query_rows = bfloat(jnp.transpose(query_t[...])) * 0.125
    canvas_out[...] = entering[...] + times_transposed(query_rows, wq[...])
    half = kept.shape[0]
    half_side = numbers[3]
    late[0:D, :] = bfloat(matmul(jnp.transpose(window[place]), query_rows))
    inner, beside, across, _ = neighbours(place)

    def fold(tile, value_sum):
        block = tile // per
        inside = pl.ds(pl.multiple_of(lax.rem(tile, per) * TILE, TILE), TILE)
        gk, gv = tile_grads(tile_at(tile), grad_keys, grad_values)
        x_t = jnp.transpose(tile_rows(window, tile))
        grad_k[...] += matmul(x_t, gk)
        grad_v[...] += matmul(x_t, gv)
        part = times_transposed(gk, wk[...]) + times_transposed(gv, wv[...])

        @pl.when(block == place)
        def _():
            canvas_out[inside, :] += part

        @pl.when(jnp.logical_and(inner, block == across))
        def _():
            middle_out[inside, :] = bfloat(part)

        @pl.when(block == beside)
        def _():
            side_out[inside, :] = bfloat(part)

        return value_sum + summed(gv)

    value_sum = lax.fori_loop(low, high, fold, far_sum[0:1, :])
    done(0, 1, 2)
    late[D : 2 * D, :] = bfloat(grad_k[...])
    late[2 * D : 3 * D, :] = bfloat(grad_v[...])
    vector_sums = jnp.concatenate(
        [sums_one[...], sums_two[...], summed(query_rows), value_sum, jnp.zeros((6, D), f32)], axis=0
    )
    late[3 * D : 3 * D + 32, :] = bfloat(vector_sums)
    late[3 * D + 32 : 2 * half, :] = jnp.zeros((2 * half - 3 * D - 32, D), bf16)
    for copy in [ship(late, n * half, half, sent, kept, half_side, semaphores.at[8 + n]) for n in range(2)]:
        copy.wait()


VMEM_BLOCK = pl.BlockSpec(memory_space=pltpu.VMEM)
SMEM_BLOCK = pl.BlockSpec(memory_space=pltpu.SMEM)
ANY_BLOCK = pl.BlockSpec(memory_space=pl.ANY)
HBM_BLOCK = pl.BlockSpec(memory_space=pltpu.HBM)


class Numbers:
    def __init__(self, numbers, length, memory_length, segments):
        T = segments.shape[1]
        self.refs = [
            (numbers, (0,)), (length, (0,)), (memory_length, (0,)), (numbers, (1,)),
            (segments, (0, 0)), (segments, (0, T - 1)),
        ]

    def __getitem__(self, index):
        ref, at = self.refs[index]
        return ref[at]


def run_kernel(kernel, name, microseconds, out_shapes, small, far, near, scratch, ties=(), out_far=0, anywhere=False):
    kept = out_shapes[: len(out_shapes) - out_far]
    counts = [len(small), len(far), len(near), len(ties), len(kept), out_far, len(scratch), len(near), len(kept), 1]

    def body(*refs):
        parts, at = [], 0
        for count in counts:
            parts.append(refs[at : at + count])
            at += count
        small_refs, far_refs, held, _, outs, own_outs, scratch_refs, copies, results, (semaphores,) = parts
        loads = [
            pltpu.make_async_copy(a, b, semaphores.at[n]) for n, (a, b) in enumerate(zip(held, copies))
        ]
        leaving = {
            n: pltpu.make_async_copy(a, b, semaphores.at[len(loads) + n])
            for n, (a, b) in enumerate(zip(results, outs))
        }
        left = []
        for load in loads:
            load.start()
        waiting = list(loads)

        def ready(count=len(loads)):
            for load in waiting[:count]:
                load.wait()
            del waiting[:count]

        def done(*numbers):
            for n in numbers:
                copy = leaving.pop(n)
                copy.start()
                left.append(copy)

        kernel(ready, done, Numbers(*small_refs), *far_refs, *copies, *results, *own_outs, *scratch_refs)
        ready()
        done(*list(leaving))
        for copy in left:
            copy.wait()

    return pl.pallas_call(
        body,
        out_shape=[jax.ShapeDtypeStruct(shape, kind) for shape, kind in out_shapes],
        in_specs=[SMEM_BLOCK] * len(small)
        + [HBM_BLOCK] * len(far)
        + [ANY_BLOCK if anywhere else HBM_BLOCK] * len(near)
        + [ANY_BLOCK] * len(ties),
        out_specs=[HBM_BLOCK] * len(out_shapes),
        scratch_shapes=[
            *scratch,
            *[pltpu.VMEM(w.shape, w.dtype) for w in near],
            *[pltpu.VMEM(shape, kind) for shape, kind in kept],
            pltpu.SemaphoreType.DMA((len(near) + len(kept),)),
        ],
        compiler_params=pltpu.CompilerParams(vmem_limit_bytes=ROOM),
        cost_estimate=cost(microseconds),
        name=name,
    )(*small, *far, *near, *ties)


def window_scratch(T, D):
    return [
        pltpu.VMEM((4, T, D), bf16),
        pltpu.VMEM((4, TAIL, D), bf16),
        pltpu.VMEM((4, T), f32),
        pltpu.VMEM((4, T), f32),
        pltpu.VMEM((4 * T, 128), f32),
    ]


def self_near(numbers, segments, blocks, weights, vectors, ties=()):
    T, D = segments.shape[1], vectors.shape[1]
    wq, wk, wv = weights
    return run_kernel(
        self_near_kernel, "self_near", 13,
        [((T, D), bf16), ((H, VROWS, T), f32), ((16, 128), f32)],
        numbers, blocks[:3], [segments, vectors, wv, wq, wk],
        window_scratch(T, D)
        + [
            pltpu.VMEM((PAIRS, 4 * T, 128), bf16),
            pltpu.VMEM((H, VROWS, 4 * T), bf16),
            pltpu.VMEM((H, T), f32),
            pltpu.VMEM((H, T, 128), bf16),
            pltpu.SemaphoreType.DMA((8,)),
        ],
        ties,
    )


def self_far(numbers, segments, blocks, weights, vectors, queries, total, reach, opposite, ties=()):
    T, D = queries.shape
    return run_kernel(
        self_far_kernel, "self_far", 7,
        [((T, D), bf16), ((H, T), f32)],
        numbers, blocks, [*weights[1:], segments, vectors, queries, reach, opposite, total],
        window_scratch(T, D)
        + [
            pltpu.VMEM((PAIRS, 4 * T, 128), bf16),
            pltpu.VMEM((H, VROWS, 4 * T), bf16),
            pltpu.VMEM((H, T), f32),
            pltpu.VMEM((H, VROWS, T), f32),
            pltpu.VMEM((D, T), f32),
            pltpu.VMEM((H, T, 128), bf16),
            pltpu.SemaphoreType.DMA((8,)),
        ],
        ties,
    )


def backward_scratch(T, D):
    return window_scratch(T, D) + [
        pltpu.VMEM((PAIRS, 4 * T, 128), bf16),
        pltpu.VMEM((D, 4 * T), bf16),
        pltpu.VMEM((PAIRS, 4 * T, 128), bf16),
        pltpu.VMEM((PAIRS, 4 * T, 128), f32),
        pltpu.VMEM((PAIRS, 4 * T, 128), f32),
        pltpu.VMEM((H, T, 128), bf16),
        pltpu.VMEM((H, T, 128), bf16),
        pltpu.VMEM((H, T), f32),
    ]


def back_far(numbers, segments, blocks, weights, vectors, queries, blended, upstream, lse, opposite, ties=()):
    T, D = queries.shape
    return run_kernel(
        back_far_kernel, "back_far", 8,
        [((T, D), bf16), ((D, D), f32), ((D, D), f32), ((8, D), f32), ((D, T), f32)],
        numbers, blocks[3:],
        [segments, vectors, *weights[1:], queries, upstream, blended, lse, opposite],
        backward_scratch(T, D) + [pltpu.SemaphoreType.DMA((8,))],
        ties,
    )


def back_near(numbers, segments, blocks, weights, vectors, queries, blended, upstream, lse, entering, sums, far, ties=()):
    T, D = queries.shape
    wq, wk, wv = weights
    far_k, far_v, far_sum, far_query_t = far
    rows = 3 * D // 2 + D // 4
    return run_kernel(
        back_near_kernel, "back_near", 22,
        [((T, D), f32), ((T, D), bf16), ((T, D), bf16), ((rows, D), bf16), ((rows, D), bf16)],
        numbers, blocks[:3],
        [
            segments, vectors, wk, wv, queries, upstream, blended, lse, far_query_t,
            wq, entering, far_k, far_v, far_sum, *sums,
        ],
        backward_scratch(T, D)
        + [
            pltpu.VMEM((D, T), f32),
            pltpu.VMEM((D, D), f32),
            pltpu.VMEM((D, D), f32),
            pltpu.VMEM((2 * rows, D), bf16),
            pltpu.SemaphoreType.DMA((10,)),
        ],
        ties, 2,
    )


def pack_kernel(ready, done, numbers, canvas, cotangent, *refs):
    *small, wide, segments, memory_segments, memory, vectors, payload, last, extras, held, semaphores = refs
    T, D = canvas.shape
    here = memory.shape[0]
    arrive = pltpu.make_async_copy(canvas, held, semaphores.at[0])
    arrive.start()
    rows = pltpu.make_async_copy(held, payload.at[pl.ds(0, T)], semaphores.at[3])
    copy = pltpu.make_async_copy(cotangent.at[pl.ds(T - TAIL, TAIL)], last, semaphores.at[1])
    copy.start()
    arrive.wait()
    rows.start()
    ready()

    def padded(row):
        if row.shape[1] == D:
            return row
        return jnp.concatenate([row, jnp.zeros((1, D - row.shape[1]), f32)], axis=1)

    row = lax.broadcasted_iota(jnp.int32, (TAIL, D), 0)
    copy.wait()
    codes = jnp.broadcast_to(padded(segments[...].astype(f32)), (TAIL, D))
    carried = jnp.broadcast_to(widen(last[...])[TAIL - 1 : TAIL], (TAIL, D))
    row_sum = jnp.broadcast_to(summed(held[...]), (TAIL, D))
    rest_of_sum = row_sum - widen(bfloat(row_sum))
    extras[0:TAIL, :] = bfloat(
        jnp.where(
            row == 0, codes,
            jnp.where(row == 1, carried, jnp.where(row == 2, row_sum, jnp.where(row == 3, rest_of_sum, 0.0))),
        )
    )
    extras[TAIL : TAIL + here, :] = memory[...]
    codes = jnp.broadcast_to(padded(memory_segments[...].astype(f32)), (TAIL, D))
    extras[TAIL + here : 2 * TAIL + here, :] = bfloat(jnp.where(row == 0, codes, 0.0))
    rest = pltpu.make_async_copy(extras, payload.at[pl.ds(T, 2 * TAIL + here)], semaphores.at[2])
    rest.start()
    for index, vector in enumerate(small):
        vectors[index : index + 1, :] = widen(vector[...])[None, :]
    values = widen(wide[...])
    for c in range(values.shape[0] // D):
        vectors[len(small) + c : len(small) + c + 1, :] = values[c * D : c * D + D][None, :]
    rows.wait()
    rest.wait()


def pack(numbers, small, wide, segments, memory_segments, memory, canvas, cotangent):
    T, D = canvas.shape
    size = 2 * TAIL + memory.shape[0]
    return run_kernel(
        pack_kernel, "pack", 2,
        [((len(small) + wide.shape[0] // D, D), f32), ((T + size, D), bf16)],
        numbers, [canvas, cotangent], [*small, wide, segments, memory_segments, memory],
        [pltpu.VMEM((TAIL, D), bf16), pltpu.VMEM((size, D), bf16), pltpu.VMEM((T, D), bf16), pltpu.SemaphoreType.DMA((4,))],
        (), 1,
    )


BQ1, BV1, BO1, G1, B1, BQ2, BV2, BO2, G2, B2, BR, G3, B3, BS, BE = range(15)


def smooth_gate(inputs):
    square = inputs * inputs
    bent = jnp.tanh(gelu_scale * inputs * (1.0 + gelu_cubic * square))
    half = 0.5 * (1.0 + bent)
    slope = half + 0.5 * inputs * (1.0 - bent * bent) * (
        gelu_scale * (1.0 + 3.0 * gelu_cubic * square)
    )
    return inputs * half, slope


def norm_forward(inputs):
    average = jnp.mean(inputs, axis=-1, keepdims=True)
    centred = inputs - average
    scaling = lax.rsqrt(jnp.mean(centred * centred, axis=-1, keepdims=True) + epsilon)
    return centred * scaling, scaling


def norm_backward(upstream, gain, normal, scaling):
    scaled = upstream * gain
    return scaling * (
        scaled
        - jnp.mean(scaled, axis=-1, keepdims=True)
        - normal * jnp.mean(scaled * normal, axis=-1, keepdims=True)
    )


def summed(values):
    return jnp.sum(widen(values), axis=0, keepdims=True)


def memory_moves(place, blocks, last_memory, gathered, semaphores, first):
    own, side, middle, middle_far, side_far = blocks
    size = gathered.shape[1]
    begin = own.shape[0] - size
    inner, beside, across, far = neighbours(place)

    def move(block, slot, index):
        return pltpu.make_async_copy(
            block.at[pl.ds(begin, size)], gathered.at[slot], semaphores.at[first + index]
        )

    def run(act):
        for copy in (move(own, place, 0), move(side, beside, 1)):
            act(copy)

        @pl.when(inner)
        def _():
            for copy in (move(middle, across, 2), move(middle_far, far, 3)):
                act(copy)

        @pl.when(jnp.logical_not(inner))
        def _():
            last = pltpu.make_async_copy(last_memory, gathered.at[3 - place], semaphores.at[first + 3])
            for copy in (move(side_far, far, 2), last):
                act(copy)

    return run


def memory_rows(gathered, memory, columns, memory_length):
    count, size, width = gathered.shape
    here = size - TAIL
    lane = lax.broadcasted_iota(jnp.int32, (1, here), 1)
    for b in range(count):
        span = slice(b * here, (b + 1) * here)
        memory[span, :] = gathered[b, 0:here, :]
        code = widen(gathered[b, here : here + 1, 0:here])
        columns[span, :] = as_column(jnp.where(b * here + lane < memory_length, code, -1.0))


def ship(buffer, first, count, sent, kept, side, semaphore):
    half = kept.shape[0]
    part, at = divmod(first, half)
    source = buffer.at[pl.ds(first, count)]

    @pl.when(side == part)
    def _():
        pltpu.make_async_copy(source, kept.at[pl.ds(at, count)], semaphore).start()

    @pl.when(side != part)
    def _():
        pltpu.make_async_copy(source, sent.at[pl.ds(at, count)], semaphore).start()

    return pltpu.make_async_copy(source, kept.at[pl.ds(at, count)], semaphore)


def forward_kernel(
    ready, done, numbers, own, side, middle, middle_far, side_far, last_memory,
    segments, vectors, ck, cv, canvas, blended, wo, cq, co, we, wr, ws, cotangent,
    slots_out, last_out, first_state, normal_out, scaling_out, low_out, query_out, fetched_out,
    lse, second_out, sums, gathered, sent, kept,
    tails, memory, columns, keys, values_t, summit, total,
    blend_t, q_sides, hidden, slope, second, low2, early, semaphores,
):
    T, D = canvas.shape
    M = memory.shape[0]
    FF = we.shape[1]
    place, length, memory_length = numbers[0], numbers[1], numbers[2]
    edges = [
        pltpu.make_async_copy(side.at[pl.ds(T, TAIL)], tails.at[0], semaphores.at[0]),
        pltpu.make_async_copy(middle.at[pl.ds(T, TAIL)], tails.at[1], semaphores.at[1]),
    ]
    bring = memory_moves(
        place, (own, side, middle, middle_far, side_far), last_memory, gathered, semaphores, 2
    )
    bring(start)
    for copy in edges:
        copy.start()
    leaving = []

    half_side = numbers[3]

    def leave(block, index):
        early[pl.ds(index * D, D), :] = block

    def go(*indices):
        for index in indices:
            leaving.append(ship(early, index * D, D, sent, kept, half_side, semaphores.at[6 + index]))

    def vector(index):
        return vectors[index : index + 1, :]

    sums[...] = jnp.zeros_like(sums)
    ready(2)
    code_row = segments[...].astype(f32)

    bring(wait)
    memory_rows(gathered, memory, columns, memory_length)
    done(11)
    ready(2)
    k = bfloat(matmul(memory[...], ck[...]))
    for pair in range(PAIRS):
        keys[pair] = k[:, 128 * pair : 128 * pair + 128]
    bias_t = as_column(vector(BV2))[:, 0:1]
    v_t = bfloat(times_transposed(jnp.transpose(cv[...]), memory[...]) + bias_t)
    for head in range(H):
        values_t[head, 0:HD, :] = v_t[HD * head : HD * head + HD]
        values_t[head, HD:VROWS, :] = jnp.ones((VROWS - HD, M), bf16)

    ready(3)
    first_in = widen(canvas[...]) + matmul(blended[...], wo[...]) + vector(BO1)
    normal, scaling = norm_forward(first_in)
    normal_out[...] = normal
    scaling_out[...] = jnp.broadcast_to(scaling, (T, 128))
    done(3, 4)
    first = normal * vector(G1) + vector(B1)
    low = bfloat(first)
    low_out[...] = low
    ready(1)
    query_out[...] = bfloat((matmul(low, cq[...]) + vector(BQ2)) * 0.125)
    done(5, 6)

    ones_of_heads = head_rows(bf16)
    q_all = query_out[...]
    reach = jnp.max(
        jnp.max(times_transposed(ones_of_heads, q_all * q_all), axis=1, keepdims=True)
        * jnp.max(times_transposed(ones_of_heads, k * k), axis=1, keepdims=True)
    )
    wide = reach > safe_square
    summit[...] = jnp.zeros_like(summit)
    total[...] = jnp.zeros_like(total)
    split_heads(q_all, q_sides)
    tiles = [slice(t, t + TILE) for t in range(0, M, TILE)]

    @pl.when(wide)
    def _():
        summit[...] = jnp.full(summit.shape, masked_score, f32)
        for at in tiles:
            look_at(at, keys, q_sides, columns, code_row, summit)

    for at in tiles:
        blend_at(at, keys, values_t, q_sides, columns, code_row, summit, total)
    fetched = normalise(total, summit, lse, blend_t)
    fetched_out[...] = fetched
    done(7, 8)

    ready(1)
    second_in = first + matmul(fetched, co[...]) + vector(BO2)
    normal2, scaling2 = norm_forward(second_in)
    second[...] = normal2 * vector(G2) + vector(B2)
    low2[...] = bfloat(second[...])
    ready(2)
    third_in = second[...] + vector(BR)
    for c in range(FF // D):
        lanes = slice(c * D, (c + 1) * D)
        before = matmul(low2[...], we[:, lanes]) + vector(BE + c)
        gate, bend = smooth_gate(before)
        gate = bfloat(gate)
        hidden[:, lanes] = gate
        slope[:, lanes] = bend
        third_in += matmul(gate, wr[lanes, :])
    normal3, scaling3 = norm_forward(third_in)
    states = bfloat(normal3 * vector(G3) + vector(B3))
    first_state[...] = states[0:TAIL]

    for copy in edges:
        copy.wait()
    ready()
    inner = jnp.logical_or(place == 1, place == 2)
    beside_tail, across_tail = widen(tails[0]), widen(tails[1])
    after_code = jnp.where(place == 1, across_tail[0:1, 0:1], beside_tail[0:1, 0:1])
    before_code = jnp.where(place == 2, across_tail[0:1, T - 1 : T], beside_tail[0:1, T - 1 : T])
    before_row = jnp.where(place == 2, across_tail[1:2, :], beside_tail[1:2, :])
    lane = lax.broadcasted_iota(jnp.int32, (8, T), 1)
    codes8 = jnp.broadcast_to(code_row, (8, T))
    live = jnp.where(place * T + lane < length, codes8, -1.0)
    next_code = jnp.where(lane == T - 1, after_code, pltpu.roll(live, T - 1, 1))
    valid8 = jnp.where(
        jnp.logical_and(next_code == codes8, place * T + lane + 1 < length), 1.0, 0.0
    )
    valid = as_column(valid8[0:1, :])[:, 0:1]
    last_valid = jnp.where(
        jnp.logical_and(before_code == code_row[:, 0:1], jnp.logical_and(place > 0, place * T < length)),
        1.0, 0.0,
    )
    row = lax.broadcasted_iota(jnp.int32, (T, D), 0)
    following = bfloat(jnp.where(row == T - 1, 0.0, pltpu.roll(widen(states), T - 1, 0)))
    raw = matmul(states, ws[0:D, :]) + vector(BS) + matmul(following, ws[D : 2 * D, :])
    slots_out[...] = bfloat(raw * valid)
    last_out[...] = jnp.concatenate(
        [raw[T - 1 : T], jnp.broadcast_to(valid[T - 1 : T], (1, D)), jnp.zeros((6, D), f32)], axis=0
    )
    done(0, 1, 2)
    masked = widen(cotangent[...]) * valid
    shifted = jnp.where(row == 0, before_row * last_valid, pltpu.roll(masked, 1, 0))
    masked_low, shifted_low = bfloat(masked), bfloat(shifted)
    upstream = times_transposed(masked_low, ws[0:D, :]) + widen(
        bfloat(times_transposed(shifted_low, ws[D : 2 * D, :]))
    )
    states_t = jnp.transpose(states)
    leave(bfloat(matmul(states_t, masked_low)), 0)
    leave(bfloat(matmul(states_t, shifted_low)), 1)
    sums[0:1, :] = summed(masked)

    third_grad = norm_backward(upstream, vector(G3), normal3, scaling3)
    sums[1:2, :] = summed(upstream * normal3)
    sums[2:3, :] = summed(upstream)
    third_low = bfloat(third_grad)
    sums[3:4, :] = summed(third_low)
    low2_t = jnp.transpose(low2[...])
    second_up = third_grad
    for c in range(FF // D):
        lanes = slice(c * D, (c + 1) * D)
        leave(bfloat(matmul(jnp.transpose(hidden[:, lanes]), third_low)), 2 + FF // D + c)
        hidden_grad = bfloat(times_transposed(third_low, wr[lanes, :]))
        before_grad = bfloat(widen(hidden_grad) * slope[:, lanes])
        leave(bfloat(matmul(low2_t, before_grad)), 2 + c)
        sums[4 + c : 5 + c, :] = summed(before_grad)
        second_up += times_transposed(before_grad, we[:, lanes])
        if c == FF // D // 2:
            go(0, 1, *[2 + n for n in range(c)], *[2 + FF // D + n for n in range(c)])
    second_out[...] = norm_backward(second_up, vector(G2), normal2, scaling2)
    sums[8:9, :] = summed(second_up * normal2)
    sums[9:10, :] = summed(second_up)
    rest = range(FF // D // 2, FF // D)
    go(*[2 + n for n in rest], *[2 + FF // D + n for n in rest])
    for copy in leaving:
        copy.wait()


def backward_kernel(
    ready, done, numbers,
    second_grad, co, segments, vectors, gathered, query, ck, cv, fetched, lse, cq, normal, scaling, wo, low,
    blended, first_state, wv, self_lse,
    first_grad_out, upstream_out, sums, sent, kept, memory_goes, memory_stays,
    memory, columns, keys, keys_t, values, grad_keys, grad_values, query_t, upstream2, q_sides, u_sides, fixes, late, memory_out, semaphores,
):
    T, D = low.shape
    M = memory.shape[0]
    half_side = numbers[3]
    sums[...] = jnp.zeros_like(sums)
    ready(2)
    low_grad = bfloat(second_grad[...])
    upstream2[...] = bfloat(times_transposed(low_grad, co[...]))
    ready(4)
    code_row = segments[...].astype(f32)
    gain = vectors[G1 : G1 + 1, :]
    memory_rows(gathered, memory, columns, numbers[2])
    split_heads(query[...], q_sides)
    ready(2)
    k = bfloat(matmul(memory[...], ck[...]))
    v = bfloat(matmul(memory[...], cv[...]) + vectors[BV2 : BV2 + 1, :])
    for pair in range(PAIRS):
        keys[pair] = k[:, 128 * pair : 128 * pair + 128]
        values[pair] = v[:, 128 * pair : 128 * pair + 128]
    keys_t[...] = jnp.transpose(k)
    ready(2)
    fixes[...] = row_corrections(upstream2[...], fetched[...])
    split_heads(upstream2[...], u_sides)
    query_t[...] = jnp.zeros_like(query_t)
    for tile in range(M // TILE):
        step_back(
            slice(tile * TILE, (tile + 1) * TILE), keys, keys_t, values, q_sides, u_sides, columns,
            code_row, lse, fixes, query_t, grad_keys, grad_values,
        )
    query_rows = bfloat(jnp.transpose(query_t[...])) * 0.125
    ready()
    first_up = second_grad[...] + times_transposed(query_rows, cq[...])
    first_grad = norm_backward(first_up, gain, normal[...], scaling[:, 0:1])
    first_grad_out[...] = first_grad
    first_low = bfloat(first_grad)
    upstream_out[...] = bfloat(times_transposed(first_low, wo[...]))
    done(0, 1)
    gk, gv = tile_grads(slice(0, M), grad_keys, grad_values)
    part = bfloat(times_transposed(gk, ck[...]) + times_transposed(gv, cv[...]))
    count, size, _ = memory_out.shape
    here = size - TAIL
    place = numbers[0]
    tail = lax.broadcasted_iota(jnp.int32, (TAIL, D), 0)
    terms = jnp.broadcast_to(masked_terms(self_lse[...], upstream_out[...]), (TAIL, D))
    opposite_row = times_transposed(bfloat(terms), wv[...])
    for b in range(count):
        memory_out[b, 0:here, :] = part[b * here : (b + 1) * here]
        rows = jnp.where(jnp.logical_and(tail == 0, place == b + 1), widen(first_state[...]), 0.0)
        rows += jnp.where(
            jnp.logical_and(tail == 1, jnp.logical_and(is_outer(place), place == 3 - b)), opposite_row, 0.0
        )
        memory_out[b, here:size, :] = bfloat(rows)
    leaving = []
    for b in range(count):
        copies = [
            pltpu.make_async_copy(memory_out.at[b], half_out.at[b // 2], semaphores.at[2 + b])
            for half_out in (memory_stays, memory_goes)
        ]

        @pl.when(lax.rem(place, 2) == b % 2)
        def _():
            copies[0].start()

        @pl.when(lax.rem(place, 2) != b % 2)
        def _():
            copies[1].start()

        leaving.append(copies[0])
    memory_t = jnp.transpose(memory[...])
    late[0:D, :] = bfloat(matmul(jnp.transpose(low[...]), query_rows))
    late[D : 2 * D, :] = bfloat(matmul(memory_t, gk))
    late[2 * D : 3 * D, :] = bfloat(matmul(memory_t, gv))
    late[3 * D : 4 * D, :] = bfloat(matmul(jnp.transpose(fetched[...]), low_grad))
    late[4 * D : 5 * D, :] = bfloat(matmul(jnp.transpose(blended[...]), first_low))
    half = 5 * D // 2
    leaving += [ship(late, n * half, half, sent, kept, half_side, semaphores.at[n]) for n in range(2)]
    sums[0:1, :] = summed(low_grad)
    sums[1:2, :] = summed(query_rows)
    sums[2:3, :] = summed(gv)
    sums[3:4, :] = summed(first_up * normal[...])
    sums[4:5, :] = summed(first_up)
    sums[5:6, :] = summed(first_low)
    done(2)
    for copy in leaving:
        copy.wait()


def middle_forward(numbers, segments, canvas, blended, cotangent, vectors, blocks, last_memory, weights, ties=()):
    T, D = canvas.shape
    wo, ck, cv, cq, co, we, wr, ws = weights
    FF = we.shape[1]
    here = last_memory.shape[0] - TAIL
    M = 4 * here
    rows = 2 * D + 2 * FF
    return run_kernel(
        forward_kernel, "middle_forward", 24,
        [
            ((T, D), bf16), ((8, D), f32), ((TAIL, D), bf16), ((T, D), f32), ((T, 128), f32), ((T, D), bf16),
            ((T, D), bf16), ((T, D), bf16), ((H, T), f32), ((T, D), f32),
            ((16, D), f32), ((4, here + TAIL, D), bf16), ((rows // 2, D), bf16), ((rows // 2, D), bf16),
        ],
        numbers, [*blocks, last_memory],
        [segments, vectors, ck, cv, canvas, blended, wo, cq, co, we, wr, ws, cotangent],
        [
            pltpu.VMEM((2, TAIL, D), bf16),
            pltpu.VMEM((M, D), bf16),
            pltpu.VMEM((M, 128), f32),
            pltpu.VMEM((PAIRS, M, 128), bf16),
            pltpu.VMEM((H, VROWS, M), bf16),
            pltpu.VMEM((H, T), f32),
            pltpu.VMEM((H, VROWS, T), f32),
            pltpu.VMEM((D, T), f32),
            pltpu.VMEM((H, T, 128), bf16),
            pltpu.VMEM((T, FF), bf16),
            pltpu.VMEM((T, FF), f32),
            pltpu.VMEM((T, D), f32),
            pltpu.VMEM((T, D), bf16),
            pltpu.VMEM((rows, D), bf16),
            pltpu.SemaphoreType.DMA((6 + rows // D,)),
        ],
        ties, 2,
    )


def middle_backward(numbers, segments, blended, gathered, vectors, saved, weights, ties=()):
    T, D = blended.shape
    M = gathered.shape[0] * (gathered.shape[1] - TAIL)
    rows = 5 * D // 2
    part = (gathered.shape[0] // 2, *gathered.shape[1:])
    normal, scaling, low, query, fetched, lse, second_grad, first_state, self_lse = saved
    wo, cq, ck, cv, co, wv = weights
    return run_kernel(
        backward_kernel, "middle_backward", 16,
        [
            ((T, D), f32), ((T, D), bf16), ((8, D), f32), ((rows, D), bf16), ((rows, D), bf16),
            (part, bf16), (part, bf16),
        ],
        numbers, [],
        [
            second_grad, co, segments, vectors, gathered, query, ck, cv, fetched, lse,
            cq, normal, scaling, wo, low, blended, first_state, wv, self_lse,
        ],
        [
            pltpu.VMEM((M, D), bf16),
            pltpu.VMEM((M, 128), f32),
            pltpu.VMEM((PAIRS, M, 128), bf16),
            pltpu.VMEM((D, M), bf16),
            pltpu.VMEM((PAIRS, M, 128), bf16),
            pltpu.VMEM((PAIRS, M, 128), f32),
            pltpu.VMEM((PAIRS, M, 128), f32),
            pltpu.VMEM((D, T), f32),
            pltpu.VMEM((T, D), bf16),
            pltpu.VMEM((H, T, 128), bf16),
            pltpu.VMEM((H, T, 128), bf16),
            pltpu.VMEM((H, T), f32),
            pltpu.VMEM((2 * rows, D), bf16),
            pltpu.VMEM(gathered.shape, bf16),
            pltpu.SemaphoreType.DMA((6,)),
        ],
        ties, 4,
    )


def pieces(start, count, half):
    found = []
    for part in range(2):
        low, high = max(start, part * half), min(start + count, (part + 1) * half)
        if low < high:
            found.append((part, low - part * half, low - start, high - low))
    return found


def unpack_kernel(layout, ready, done, numbers, mine, came, *outs):
    half, D = mine.shape
    half_side = numbers[3]
    ready()
    for number, (out, starts) in enumerate(zip(outs, layout)):
        count = out.shape[0]
        for column, start_row in enumerate(starts):
            lanes = slice(column * D, (column + 1) * D)
            for part, there, here, rows in pieces(start_row, count, half):
                step = min(rows, 512)
                for at in range(0, rows, step):
                    size = min(step, rows - at)
                    source = slice(there + at, there + at + size)
                    target = slice(here + at, here + at + size)

                    @pl.when(half_side == part)
                    def _():
                        out[target, lanes] = widen(mine[source, :])

                    @pl.when(half_side != part)
                    def _():
                        out[target, lanes] = widen(came[source, :])

        done(number)


def unpack(numbers, name, mine, came, layout, ties=()):
    D = mine.shape[1]
    return run_kernel(
        functools.partial(unpack_kernel, [starts for _, starts in layout]), name, 4,
        [((count, D * len(starts)), f32) for count, starts in layout],
        numbers, [], [mine, came], [], ties, 0, True,
    )


def finish_kernel(
    ready, done, numbers, memory_stays, memory_came, last_slot, slots, bottom, base, onward, outward,
    memory_grad, slots_out, canvas_grad,
):
    T, D = slots.shape
    here = memory_grad.shape[0]
    ready(4)
    summed_rows = widen(memory_stays[...]) + widen(memory_came[...])
    memory_grad[...] = summed_rows[0:here]
    done(0)
    next_state = bfloat(summed_rows[here : here + TAIL])
    ready(1)
    last_row = (last_slot[0:1, :] + matmul(next_state, bottom[...])[0:1]) * last_slot[1:2, :]
    row = lax.broadcasted_iota(jnp.int32, (TAIL, D), 0)
    slots_out[0 : T - TAIL, :] = slots[0 : T - TAIL, :]
    slots_out[T - TAIL : T, :] = bfloat(
        jnp.where(row == TAIL - 1, last_row, widen(slots[T - TAIL : T, :]))
    )
    done(1)
    ready()
    canvas_grad[...] = base[...] + summed_rows[here + 1 : here + 2] + widen(onward[...]) + widen(outward[...])


def finish(numbers, memory_stays, memory_came, last_slot, slots, bottom, base, onward, outward, ties=()):
    T, D = slots.shape
    return run_kernel(
        finish_kernel, "finish", 3,
        [((memory_stays.shape[0] - TAIL, D), f32), ((T, D), bf16), ((T, D), f32)],
        numbers, [], [memory_stays, memory_came, last_slot, slots, bottom, base, onward, outward], [], ties,
    )


SIDE = [(0, 1), (1, 0), (2, 3), (3, 2)]
MIDDLE = [(1, 2), (2, 1)]
OUTWARD = [(1, 0), (2, 3)]
INWARD = [(0, 1), (3, 2)]


def routes():
    bits = [("rows", 1 << b) for b in range((lax.axis_size("rows") - 1).bit_length())]
    along = [("seq", 1 << b) for b in range((lax.axis_size("seq") - 1).bit_length())]
    return bits[0], bits[1:], bits[:0:-1], along


def swap(block, step):
    axis, bit = step
    return lax.ppermute(block, axis, [(i, i ^ bit) for i in range(lax.axis_size(axis))])


def side_of(step):
    axis, bit = step
    return jnp.where((lax.axis_index(axis) & bit) != 0, 1, 0)


def halves(terms, step):
    side = side_of(step)
    half = terms[0].shape[0] // 2

    def part(which):
        pieces = [widen(lax.dynamic_slice_in_dim(t, which * half, half)) for t in terms]
        return bfloat(sum(pieces[1:], pieces[0]))

    return part(1 - side), part(side)


def ordered(block, came, step):
    side = side_of(step) == 1
    return jnp.where(side, came, block), jnp.where(side, block, came)


class Order:
    def __init__(self):
        self.last = []

    def made(self, *values):
        self.last = list(values)

    def after(self, *values):
        if not self.last:
            return values
        values, _ = lax.optimization_barrier((values, tuple(self.last)))
        return values


class Summing:
    def __init__(self, order, sent, kept, split):
        self.order = order
        self.split = split
        self.steps = self.run(sent, kept)
        self.whole = None
        next(self.steps)

    def step(self):
        if self.whole is not None:
            return
        try:
            self.order.made(*next(self.steps))
        except StopIteration as end:
            self.whole = end.value

    def finish(self):
        while self.whole is None:
            self.step()
        return self.whole

    def take(self, blocks):
        return self.order.after(*blocks)

    def run(self, sent, kept):
        first, up, down, along = routes()
        came = swap(sent, first)
        yield [sent]
        (came,) = self.take([came])
        size = kept.shape[0]
        if self.split == 2:
            ways = [(up, 0, size // 2), (down, size // 2, size // 2)]
        else:
            ways = [(down if self.split else up, 0, size)]
        lanes = [[kept[at : at + n], came[at : at + n]] for _, at, n in ways]
        for number in range(len(up)):
            parts = [halves(terms, way[number]) for terms, (way, _, _) in zip(lanes, ways)]
            came = [swap(goes, way[number]) for (goes, _), (way, _, _) in zip(parts, ways)]
            yield [goes for goes, _ in parts]
            came = self.take(came)
            lanes = [[stays, block] for (_, stays), block in zip(parts, came)]
        parts = [halves(terms, along[0]) for terms in lanes]
        cut = parts[0][0].shape[0]
        goes = jnp.concatenate([p[0] for p in parts], axis=0)
        stays = jnp.concatenate([p[1] for p in parts], axis=0)
        came = swap(goes, along[0])
        yield [goes]
        (came,) = self.take([came])
        mine = bfloat(widen(stays) + widen(came))
        for step in along[1:]:
            came = swap(mine, step)
            yield [mine]
            (came,) = self.take([came])
            mine = bfloat(widen(mine) + widen(came))
        came = swap(mine, along[0])
        yield [mine]
        (came,) = self.take([came])
        low, high = ordered(mine, came, along[0])
        lanes = [
            jnp.concatenate([low[n * cut : n * cut + cut], high[n * cut : n * cut + cut]], axis=0)
            for n in range(len(ways))
        ]
        for number in range(len(up) - 1, -1, -1):
            came = [swap(block, way[number]) for block, (way, _, _) in zip(lanes, ways)]
            yield lanes
            came = self.take(came)
            lanes = [
                jnp.concatenate(ordered(block, other, way[number]), axis=0)
                for block, other, (way, _, _) in zip(lanes, came, ways)
            ]
        block = lanes[0] if len(lanes) == 1 else jnp.concatenate(lanes, axis=0)
        came = swap(block, first)
        yield [block]
        return block, came


def entry_halves(block, step, bit):
    count = block.shape[0]
    grouped = block.reshape(count // (2 * bit), 2, bit, *block.shape[1:])
    side = side_of(step)
    take = lambda which: lax.dynamic_index_in_dim(grouped, which, 1, False).reshape(
        count // 2, *block.shape[1:]
    )
    return take(1 - side), take(side)


def shards(
    canvas,
    memory,
    cotangent,
    canvas_lengths,
    canvas_segments,
    memory_segments,
    memory_lengths,
    self_query,
    self_key,
    self_value,
    self_output,
    self_query_bias,
    self_value_bias,
    self_output_bias,
    first_gain,
    first_bias,
    cross_query,
    cross_key,
    cross_value,
    cross_output,
    cross_query_bias,
    cross_value_bias,
    cross_output_bias,
    second_gain,
    second_bias,
    expand_weight,
    expand_bias,
    reduce_weight,
    reduce_bias,
    third_gain,
    third_bias,
    slot_weight,
    slot_bias,
):
    place = lax.axis_index("seq")
    tokens_here = canvas.shape[1]
    width = canvas.shape[2]
    wide = expand_weight.shape[1]
    row = canvas[0]
    numbers = [
        jnp.stack([place, side_of(routes()[0])]).astype(jnp.int32),
        canvas_lengths, memory_lengths, canvas_segments,
    ]
    vectors, payload = pack(
        numbers,
        (
            self_query_bias, self_value_bias, self_output_bias, first_gain, first_bias,
            cross_query_bias, cross_value_bias, cross_output_bias, second_gain, second_bias,
            reduce_bias, third_gain, third_bias, slot_bias,
        ),
        expand_bias, canvas_segments, memory_segments, memory[0], row, cotangent[0],
    )
    side, middle = lax.ppermute(payload, "seq", SIDE), lax.ppermute(payload, "seq", MIDDLE)
    opposite = lax.ppermute(payload[tokens_here : tokens_here + TAIL], "seq", [(0, 3), (3, 0)])
    blocks = (
        payload, side, middle, lax.ppermute(side, "seq", MIDDLE), lax.ppermute(middle, "seq", OUTWARD)
    )
    last_memory = lax.ppermute(blocks[3][tokens_here + TAIL :], "seq", OUTWARD)
    projections = (self_query, self_key, self_value)

    queries, total, reach = self_near(numbers, canvas_segments, blocks, projections, vectors)
    blended, masses = self_far(
        numbers, canvas_segments, blocks, projections, vectors, queries, total, reach, opposite
    )
    (
        slots, last_slot, first_state, normal, scaling, low, cross_rows, fetched, cross_masses,
        second_grad, early_sums, gathered, early_sent, early_kept,
    ) = middle_forward(
        numbers, canvas_segments, row, blended, cotangent[0], vectors, blocks, last_memory,
        (self_output, cross_key, cross_value, cross_query, cross_output, expand_weight, reduce_weight, slot_weight),
    )
    order = Order()
    early = Summing(order, early_sent, early_kept, 2)
    early.step()
    first_grad, blended_grad, later_sums, later_sent, later_kept, memory_goes, memory_stays = middle_backward(
        numbers, canvas_segments, blended, gathered, vectors,
        (normal, scaling, low, cross_rows, fetched, cross_masses, second_grad, first_state, masses),
        (self_output, cross_query, cross_key, cross_value, cross_output, self_value), order.last,
    )
    order.made(later_sums)
    early.step()
    later = Summing(order, later_sent, later_kept, LATER_SPLIT)
    far_part, *far = back_far(
        numbers, canvas_segments, blocks, projections, vectors, queries, blended, blended_grad, masses,
        opposite, order.last,
    )
    order.made(far[2])
    from_side = lax.ppermute(far_part, "seq", INWARD)
    from_middle = lax.ppermute(far_part, "seq", MIDDLE)
    near_step, far_step = routes()[3]
    memory_came = swap(memory_goes, near_step)
    early.step()
    (memory_came,) = order.after(memory_came)
    half_sum = bfloat(widen(memory_stays) + widen(memory_came))
    memory_goes, memory_stays = entry_halves(half_sum, far_step, 1)
    memory_came = swap(memory_goes, far_step)
    order.made(*order.last, memory_goes)
    later.step()
    canvas_base, middle_part, side_part, last_sent, last_kept = back_near(
        numbers, canvas_segments, blocks, projections, vectors, queries, blended, blended_grad, masses,
        first_grad, (early_sums, later_sums), far, order.last,
    )
    order.made(last_sent)
    last = Summing(order, last_sent, last_kept, LAST_SPLIT)
    finals = {}
    turns = {"E": early, "M": later, "S": last}
    for turn in TURNS:
        if turn in turns:
            turns[turn].step()
        elif turn == "1":
            from_side, from_middle = order.after(from_side, from_middle)
            middle_part = bfloat(widen(middle_part) + widen(from_side))
            side_part = bfloat(widen(side_part) + widen(from_middle))
            onward = lax.ppermute(middle_part, "seq", MIDDLE)
            outward = lax.ppermute(side_part, "seq", SIDE)
            order.made(middle_part, side_part)
        elif turn == "s":
            *self_grads, sums = unpack(
                numbers, "last_out", *last.finish(),
                [(width, [c * width]) for c in range(3)] + [(32, [3 * width])], order.last,
            )
            order.made(sums)
        elif turn == "e":
            count = 2 * width
            grad_slot, grad_expand, grad_reduce = unpack(
                numbers, "early_out", *early.finish(),
                [
                    (count, [0]),
                    (width, list(range(count, count + wide, width))),
                    (wide, [count + wide]),
                ],
                order.last,
            )
            order.made(grad_slot)
        elif turn == "m":
            cross_grads = unpack(
                numbers, "later_out", *later.finish(),
                [(width, [c * width]) for c in range(5)], order.last,
            )
            order.made(cross_grads[0])
        elif turn == "c":
            memory_grad, slots, canvas_grad = finish(
                numbers, memory_stays[0], memory_came[0], last_slot, slots, slot_weight[width:],
                canvas_base, onward, outward, order.last,
            )
            order.made(memory_grad)
    return (
        slots[None],
        canvas_grad[None],
        memory_grad[None],
        self_grads[0],
        self_grads[1],
        self_grads[2],
        cross_grads[4],
        sums[24],
        sums[25],
        sums[21],
        sums[19],
        sums[20],
        cross_grads[0],
        cross_grads[1],
        cross_grads[2],
        cross_grads[3],
        sums[17],
        sums[18],
        sums[16],
        sums[8],
        sums[9],
        grad_expand,
        sums[4:8].reshape(-1),
        grad_reduce,
        sums[3],
        sums[1],
        sums[2],
        grad_slot,
        sums[0],
    )


def solution(mesh):
    placed = (
        P("rows", "seq", None),
        P("rows", "seq", None),
        P("rows", "seq", None),
        P("rows"),
        P("rows", "seq"),
        P("rows", "seq"),
        P("rows"),
        P(),
        P(),
        P(),
        P(),
        P(),
        P(),
        P(),
        P(),
        P(),
        P(),
        P(),
        P(),
        P(),
        P(),
        P(),
        P(),
        P(),
        P(),
        P(),
        P(),
        P(),
        P(),
        P(),
        P(),
        P(),
        P(),
    )
    return jax.shard_map(
        shards,
        mesh=mesh,
        in_specs=placed,
        out_specs=(
            P("rows", "seq", None),
            P("rows", "seq", None),
            P("rows", "seq", None),
            P(),
            P(),
            P(),
            P(),
            P(),
            P(),
            P(),
            P(),
            P(),
            P(),
            P(),
            P(),
            P(),
            P(),
            P(),
            P(),
            P(),
            P(),
            P(),
            P(),
            P(),
            P(),
            P(),
            P(),
            P(),
            P(),
        ),
        check_vma=False,
    )
```

```python
import functools

import jax
import jax.numpy as jnp
from jax import lax
from jax.experimental import pallas as pl
from jax.experimental.pallas import tpu as pltpu
from jax.sharding import PartitionSpec as P

H = 8
HD = 64
PAIRS = H // 2
TILE = 256
TAIL = 16
LAST_SPLIT = 2
LATER_SPLIT = 0
TURNS = "EM1SMSEMSESMEMSSESMceSMsm"
VROWS = 80
ROOM = 58 * 1024 * 1024

masked_score = -30000.0
epsilon = 1e-05
gelu_scale = 0.7978845608028654
gelu_cubic = 0.044715
safe_square = 3600.0
bf16 = jnp.bfloat16
f32 = jnp.float32


def cost(microseconds):
    return pl.CostEstimate(flops=int(microseconds * 1.1e9), bytes_accessed=0, transcendentals=0)


def matmul(left, right):
    return jnp.dot(left, right, preferred_element_type=f32)


def times_transposed(left, right):
    return lax.dot_general(left, right, (((1,), (1,)), ((), ())), preferred_element_type=f32)


def bfloat(values):
    return values.astype(bf16)


def widen(values):
    return values.astype(f32)


def head_rows(dtype):
    row = lax.broadcasted_iota(jnp.int32, (16, H * HD), 0)
    column = lax.broadcasted_iota(jnp.int32, (16, H * HD), 1)
    return jnp.where(column // HD == row, 1.0, 0.0).astype(dtype)


def one_head(pair_columns, side):
    lane = lax.broadcasted_iota(jnp.int32, pair_columns.shape, 1)
    wanted = lane < HD if side == 0 else lane >= HD
    return jnp.where(wanted, widen(pair_columns), 0.0).astype(bf16)


def neighbours(place):
    inner = jnp.logical_or(place == 1, place == 2)
    beside = place + 1 - 2 * lax.rem(place, 2)
    across = 3 - place
    far = jnp.where(inner, across + 1 - 2 * lax.rem(across, 2), 3 - beside)
    return inner, beside, across, far


def window_moves(place, blocks, window, tails, semaphores):
    own, side, middle, middle_far, side_far = blocks
    inner, beside, across, far = neighbours(place)
    outer = jnp.logical_not(inner)
    T = window.shape[1]

    def move(block, slot, index):
        return (
            pltpu.make_async_copy(block.at[pl.ds(0, T)], window.at[slot], semaphores.at[2 * index]),
            pltpu.make_async_copy(
                block.at[pl.ds(T, TAIL)], tails.at[slot], semaphores.at[2 * index + 1]
            ),
        )

    def near(act):
        for copy in move(own, place, 0) + move(side, beside, 1):
            act(copy)

        @pl.when(inner)
        def _():
            for copy in move(middle, across, 2):
                act(copy)

    def distant(act):
        @pl.when(inner)
        def _():
            for copy in move(middle_far, far, 3):
                act(copy)

        @pl.when(outer)
        def _():
            for copy in move(side_far, far, 3):
                act(copy)

    return near, distant


def is_outer(place):
    return jnp.logical_or(place == 0, place == 3)


def present_tiles(place, per, with_far):
    reach = 2 if with_far else 1
    return jnp.maximum(place - reach, 0) * per, jnp.minimum(place + reach + 1, 4) * per


def masked_chances(lse):
    return jnp.exp(masked_score - lse)


def masked_terms(lse, upstream):
    chances = jnp.concatenate([masked_chances(lse), jnp.zeros((8, lse.shape[1]), f32)], axis=0)
    terms = matmul(bfloat(chances), upstream)
    return jnp.sum(jnp.where(head_rows(f32) > 0.0, terms, 0.0), axis=0, keepdims=True)


def start(copy):
    copy.start()


def wait(copy):
    copy.wait()


def no_codes(codes, keycodes, pivot):
    T = codes.shape[1]
    for slot in range(4):
        codes[slot : slot + 1, :] = jnp.full((1, T), 1.0, f32) * jnp.where(slot < pivot, -8.0, 8.0)
        keycodes[slot : slot + 1, :] = jnp.full((1, T), -9.0, f32)


def read_codes(codes, keycodes, tails, slot, length):
    T = codes.shape[1]
    lane = lax.broadcasted_iota(jnp.int32, (1, T), 1)
    code = widen(tails[slot, 0:1, 0:T])
    codes[pl.ds(slot, 1), :] = code
    keycodes[pl.ds(slot, 1), :] = jnp.where(slot * T + lane < length, code, -1.0)


def near_codes(codes, keycodes, tails, place, length):
    inner, beside, across, _ = neighbours(place)
    read_codes(codes, keycodes, tails, place, length)
    read_codes(codes, keycodes, tails, beside, length)

    @pl.when(inner)
    def _():
        read_codes(codes, keycodes, tails, across, length)


def tile_range(codes, first_code, last_code):
    below = jnp.sum(jnp.where(codes[...] < first_code, 1, 0))
    through = jnp.sum(jnp.where(codes[...] <= last_code, 1, 0))
    return below // TILE, (through + TILE - 1) // TILE


def as_column(row):
    return jnp.transpose(jnp.broadcast_to(row, (128, row.shape[1])))


def column_codes(keycodes, columns, tile, T):
    per = T // TILE
    row = keycodes[pl.ds(tile // per, 1), pl.ds(pl.multiple_of(lax.rem(tile, per) * TILE, TILE), TILE)]
    columns[pl.ds(pl.multiple_of(tile * TILE, TILE), TILE), :] = as_column(row)


def tile_rows(window, tile):
    per = window.shape[1] // TILE
    return window[tile // per, pl.ds(pl.multiple_of(lax.rem(tile, per) * TILE, TILE), TILE), :]


def split_heads(rows, sides):
    for head in range(H):
        sides[head] = one_head(rows[:, 128 * (head // 2) : 128 * (head // 2) + 128], head % 2)


def visible_in(columns, at, code_row):
    column = columns[at, :]
    return jnp.concatenate([column] * (code_row.shape[1] // 128), axis=1) == code_row


def look_at(at, keys, q_sides, columns, code_row, summit):
    visible = visible_in(columns, at, code_row)
    for head in range(H):
        scores = times_transposed(keys[head // 2, at, :], q_sides[head])
        scores = jnp.where(visible, scores, masked_score)
        summit[head : head + 1, :] = jnp.maximum(
            summit[head : head + 1, :], jnp.max(scores, axis=0, keepdims=True)
        )


def blend_at(at, keys, values_t, q_sides, columns, code_row, summit, total):
    visible = visible_in(columns, at, code_row)
    for head in range(H):
        scores = jnp.where(visible, times_transposed(keys[head // 2, at, :], q_sides[head]), masked_score)
        powers = bfloat(jnp.exp(scores - summit[head : head + 1, :]))
        total[head] += matmul(values_t[head, :, at], powers)


def normalise(total, summit, lse, blend_t):
    for head in range(H):
        mass = total[head, HD : HD + 1, :]
        blend_t[HD * head : HD * head + HD, :] = total[head, 0:HD, :] / mass
        lse[head : head + 1, :] = summit[head : head + 1, :] + jnp.log(mass)
    return bfloat(jnp.transpose(blend_t[...]))


def row_corrections(upstream, blended):
    products = widen(upstream) * widen(blended)
    coarse = bfloat(products)
    fine = bfloat(products - widen(coarse))
    ones_of_heads = head_rows(bf16)
    both = times_transposed(ones_of_heads, coarse) + times_transposed(ones_of_heads, fine)
    return both[0:H]


def step_back(at, keys, keys_t, values, q_sides, u_sides, columns, code_row, lse, fixes, query_t, grad_keys, grad_values):
    visible = visible_in(columns, at, code_row)
    for pair in range(PAIRS):
        k = keys[pair, at, :]
        v = values[pair, at, :]
        key_add = value_add = None
        for head in (2 * pair, 2 * pair + 1):
            q_side, u_side = q_sides[head], u_sides[head]
            scores = jnp.where(visible, times_transposed(k, q_side), masked_score)
            chances = jnp.exp(scores - lse[head : head + 1, :])
            chance_grad = times_transposed(v, u_side) - fixes[head : head + 1, :]
            score_grad = bfloat(jnp.where(visible, chances * chance_grad, 0.0))
            to_values = matmul(bfloat(chances), u_side)
            to_keys = matmul(score_grad, q_side)
            value_add = to_values if value_add is None else value_add + to_values
            key_add = to_keys if key_add is None else key_add + to_keys
            rows = slice(HD * head, HD * head + HD)
            query_t[rows, :] += matmul(keys_t[rows, at], score_grad)
        grad_keys[pair, at, :] = key_add
        grad_values[pair, at, :] = value_add


def tile_at(tile):
    return pl.ds(pl.multiple_of(tile * TILE, TILE), TILE)


def project_forward(tile, window, keycodes, columns, keys, values_t, wk, weights_t, bias_t):
    x = tile_rows(window, tile)
    at = tile_at(tile)
    k = bfloat(matmul(x, wk[...]))
    for pair in range(PAIRS):
        keys[pair, at, :] = k[:, 128 * pair : 128 * pair + 128]
    v_t = bfloat(times_transposed(weights_t, x) + bias_t)
    for head in range(H):
        values_t[head, 0:HD, at] = v_t[HD * head : HD * head + HD]
        values_t[head, HD:VROWS, at] = jnp.ones((VROWS - HD, TILE), bf16)
    column_codes(keycodes, columns, tile, window.shape[1])
    return times_transposed(head_rows(bf16), k * k)


def self_near_kernel(
    ready, done, numbers, own, side, middle, segments, vectors, wv, wq, wk,
    queries, total, reach_out,
    window, tails, codes, keycodes, columns, keys, values_t, zeros, q_sides, semaphores,
):
    T, D = queries.shape
    place, length = numbers[0], numbers[1]
    near, _ = window_moves(place, (own, side, middle, middle, side), window, tails, semaphores)
    near(start)
    no_codes(codes, keycodes, place)
    ready()
    weights_t = jnp.transpose(wv[...])
    bias_t = as_column(vectors[BV1 : BV1 + 1, :])[:, 0:1]
    near(wait)
    near_codes(codes, keycodes, tails, place, length)
    low, high = tile_range(codes, numbers[4].astype(f32), numbers[5].astype(f32))
    rows_q = bfloat((matmul(window[place], wq[...]) + vectors[BQ1 : BQ1 + 1, :]) * 0.125)
    queries[...] = rows_q
    done(0)
    split_heads(rows_q, q_sides)

    def project(tile, reach):
        return jnp.maximum(
            reach, project_forward(tile, window, keycodes, columns, keys, values_t, wk, weights_t, bias_t)
        )

    key_reach = lax.fori_loop(low, high, project, jnp.zeros((16, TILE), f32))
    reach_out[...] = jnp.broadcast_to(jnp.max(key_reach, axis=1, keepdims=True), (16, 128))
    zeros[...] = jnp.zeros_like(zeros)
    total[...] = jnp.zeros_like(total)
    code_row = segments[...].astype(f32)

    def blend(tile, _):
        blend_at(tile_at(tile), keys, values_t, q_sides, columns, code_row, zeros, total)
        return 0

    lax.fori_loop(low, high, blend, 0)


def self_far_kernel(
    ready, done, numbers, own, side, middle, middle_far, side_far,
    wk, wv, segments, vectors, queries, near_reach, opposite, near_total,
    out, lse,
    window, tails, codes, keycodes, columns, keys, values_t, summit, total, blend_t, q_sides, semaphores,
):
    T, D = out.shape
    place, length = numbers[0], numbers[1]
    _, _, _, far = neighbours(place)
    near, distant = window_moves(
        place, (own, side, middle, middle_far, side_far), window, tails, semaphores
    )
    distant(start)
    no_codes(codes, keycodes, far)
    ready()
    weights_t = jnp.transpose(wv[...])
    bias_t = as_column(vectors[BV1 : BV1 + 1, :])[:, 0:1]
    ones_of_heads = head_rows(bf16)
    rows_q = queries[...]
    split_heads(rows_q, q_sides)
    query_reach = jnp.max(times_transposed(ones_of_heads, rows_q * rows_q), axis=1, keepdims=True)
    first, last = numbers[4].astype(f32), numbers[5].astype(f32)
    distant(wait)
    read_codes(codes, keycodes, tails, far, length)
    low, high = tile_range(codes, first, last)

    def project(tile, reach):
        return jnp.maximum(
            reach, project_forward(tile, window, keycodes, columns, keys, values_t, wk, weights_t, bias_t)
        )

    key_reach = lax.fori_loop(low, high, project, jnp.zeros((16, TILE), f32))
    key_reach = jnp.maximum(jnp.max(key_reach, axis=1, keepdims=True), near_reach[:, 0:1])
    wide = jnp.max(query_reach * key_reach) > safe_square
    summit[...] = jnp.zeros_like(summit)
    total[...] = near_total[...]
    code_row = segments[...].astype(f32)

    per = T // TILE
    low_here, high_here = present_tiles(place, per, True)

    @pl.when(wide)
    def _():
        near(start)
        near(wait)
        near_codes(codes, keycodes, tails, place, length)
        lax.fori_loop(low_here, high_here, project, jnp.zeros((16, TILE), f32))
        total[...] = jnp.zeros_like(total)
        summit[...] = jnp.full(summit.shape, masked_score, f32)

        def look(tile, _):
            look_at(tile_at(tile), keys, q_sides, columns, code_row, summit)
            return 0

        lax.fori_loop(low_here, high_here, look, 0)

        @pl.when(is_outer(place))
        def _():
            sums = times_transposed(weights_t, opposite[...])
            column = sums[:, 2:3] + sums[:, 3:4] + T * bias_t
            for head in range(H):
                part = jnp.concatenate(
                    [column[HD * head : HD * head + HD], jnp.full((VROWS - HD, 1), T, f32)], axis=0
                )
                total[head] = part * jnp.exp(masked_score - summit[head : head + 1, :])

    def blend(tile, _):
        blend_at(tile_at(tile), keys, values_t, q_sides, columns, code_row, summit, total)
        return 0

    lax.fori_loop(
        jnp.where(wide, low_here, low), jnp.where(wide, high_here, high), blend, 0
    )
    out[...] = normalise(total, summit, lse, blend_t)


def project_backward(tile, window, keycodes, columns, keys, keys_t, values, wk, wv, bias, weights_t):
    x = tile_rows(window, tile)
    at = tile_at(tile)
    k = bfloat(matmul(x, wk[...]))
    v = bfloat(matmul(x, wv[...]) + bias)
    for pair in range(PAIRS):
        keys[pair, at, :] = k[:, 128 * pair : 128 * pair + 128]
        values[pair, at, :] = v[:, 128 * pair : 128 * pair + 128]
    keys_t[:, at] = bfloat(times_transposed(weights_t, x))
    column_codes(keycodes, columns, tile, window.shape[1])


def tile_grads(at, grad_keys, grad_values):
    gk = jnp.concatenate([bfloat(grad_keys[pair, at, :]) for pair in range(PAIRS)], axis=1)
    gv = jnp.concatenate([bfloat(grad_values[pair, at, :]) for pair in range(PAIRS)], axis=1)
    return gk, gv


def back_far_kernel(
    ready, done, numbers, middle_far, side_far,
    segments, vectors, wk, wv, queries, upstream, blended, lse, opposite,
    part_out, grad_k, grad_v, value_sum, query_t,
    window, tails, codes, keycodes, columns, keys, keys_t, values, grad_keys, grad_values,
    q_sides, u_sides, fixes, semaphores,
):
    T, D = queries.shape
    place, length = numbers[0], numbers[1]
    _, _, _, far = neighbours(place)
    _, distant = window_moves(
        place, (side_far, side_far, side_far, middle_far, side_far), window, tails, semaphores
    )
    distant(start)
    ready()
    no_codes(codes, keycodes, far)
    part_out[...] = jnp.zeros_like(part_out)
    query_t[...] = jnp.zeros_like(query_t)
    grad_k[...] = jnp.zeros_like(grad_k)
    grad_v[...] = jnp.zeros_like(grad_v)
    value_sum[...] = jnp.zeros_like(value_sum)
    distant(wait)
    read_codes(codes, keycodes, tails, far, length)
    low, high = tile_range(codes, numbers[4].astype(f32), numbers[5].astype(f32))
    code_row = segments[...].astype(f32)
    per = T // TILE
    deep = jnp.max(masked_chances(lse[...])) > 0.0
    low = jnp.where(deep, far * per, low)
    high = jnp.where(deep, far * per + per, high)

    @pl.when(jnp.logical_and(deep, is_outer(place)))
    def _():
        terms = masked_terms(lse[...], upstream[...])
        terms_8 = jnp.broadcast_to(terms, (TAIL, D))
        row = lax.broadcasted_iota(jnp.int32, (TAIL, D), 0)
        rows = jnp.where(jnp.logical_or(row == 2, row == 3), widen(opposite[...]), 0.0)
        grad_v[...] += matmul(jnp.transpose(rows), jnp.where(row < 4, terms_8, 0.0))
        value_sum[0:1, :] += T * terms

    @pl.when(high > low)
    def _():
        weights_t = jnp.transpose(wk[...])
        split_heads(queries[...], q_sides)
        split_heads(upstream[...], u_sides)
        fixes[...] = row_corrections(upstream[...], blended[...])

        def step(tile, _):
            project_backward(
                tile, window, keycodes, columns, keys, keys_t, values, wk, wv,
                vectors[BV1 : BV1 + 1, :], weights_t,
            )
            at = tile_at(tile)
            step_back(
                at, keys, keys_t, values, q_sides, u_sides, columns, code_row, lse, fixes, query_t,
                grad_keys, grad_values,
            )
            gk, gv = tile_grads(at, grad_keys, grad_values)
            x_t = jnp.transpose(tile_rows(window, tile))
            grad_k[...] += matmul(x_t, gk)
            grad_v[...] += matmul(x_t, gv)
            value_sum[0:1, :] += summed(gv)
            inside = pl.ds(pl.multiple_of(lax.rem(tile, T // TILE) * TILE, TILE), TILE)
            part_out[inside, :] = bfloat(times_transposed(gk, wk[...]) + times_transposed(gv, wv[...]))
            return 0

        lax.fori_loop(low, high, step, 0)


def back_near_kernel(
    ready, done, numbers, own, side, middle,
    segments, vectors, wk, wv, queries, upstream, blended, lse, far_query_t,
    wq, entering, far_k, far_v, far_sum, sums_one, sums_two,
    canvas_out, middle_out, side_out, sent, kept,
    window, tails, codes, keycodes, columns, keys, keys_t, values, grad_keys, grad_values,
    q_sides, u_sides, fixes, query_t, grad_k, grad_v, late, semaphores,
):
    T, D = queries.shape
    place, length = numbers[0], numbers[1]
    per = T // TILE
    near, _ = window_moves(place, (own, side, middle, middle, side), window, tails, semaphores)
    near(start)
    no_codes(codes, keycodes, place)
    ready(9)
    weights_t = jnp.transpose(wk[...])
    split_heads(queries[...], q_sides)
    split_heads(upstream[...], u_sides)
    fixes[...] = row_corrections(upstream[...], blended[...])
    query_t[...] = far_query_t[...]
    middle_out[...] = jnp.zeros_like(middle_out)
    side_out[...] = jnp.zeros_like(side_out)
    near(wait)
    near_codes(codes, keycodes, tails, place, length)
    low, high = tile_range(codes, numbers[4].astype(f32), numbers[5].astype(f32))
    code_row = segments[...].astype(f32)
    deep = jnp.max(masked_chances(lse[...])) > 0.0
    low_here, high_here = present_tiles(place, per, False)
    low, high = jnp.where(deep, low_here, low), jnp.where(deep, high_here, high)

    def step(tile, _):
        project_backward(
            tile, window, keycodes, columns, keys, keys_t, values, wk, wv,
            vectors[BV1 : BV1 + 1, :], weights_t,
        )
        step_back(
            tile_at(tile), keys, keys_t, values, q_sides, u_sides, columns, code_row, lse, fixes, query_t,
            grad_keys, grad_values,
        )
        return 0

    lax.fori_loop(low, high, step, 0)
    ready()
    grad_k[...] = far_k[...]
    grad_v[...] = far_v[...]
    query_rows = bfloat(jnp.transpose(query_t[...])) * 0.125
    canvas_out[...] = entering[...] + times_transposed(query_rows, wq[...])
    half = kept.shape[0]
    half_side = numbers[3]
    late[0:D, :] = bfloat(matmul(jnp.transpose(window[place]), query_rows))
    inner, beside, across, _ = neighbours(place)

    def fold(tile, value_sum):
        block = tile // per
        inside = pl.ds(pl.multiple_of(lax.rem(tile, per) * TILE, TILE), TILE)
        gk, gv = tile_grads(tile_at(tile), grad_keys, grad_values)
        x_t = jnp.transpose(tile_rows(window, tile))
        grad_k[...] += matmul(x_t, gk)
        grad_v[...] += matmul(x_t, gv)
        part = times_transposed(gk, wk[...]) + times_transposed(gv, wv[...])

        @pl.when(block == place)
        def _():
            canvas_out[inside, :] += part

        @pl.when(jnp.logical_and(inner, block == across))
        def _():
            middle_out[inside, :] = bfloat(part)

        @pl.when(block == beside)
        def _():
            side_out[inside, :] = bfloat(part)

        return value_sum + summed(gv)

    value_sum = lax.fori_loop(low, high, fold, far_sum[0:1, :])
    done(0, 1, 2)
    late[D : 2 * D, :] = bfloat(grad_k[...])
    late[2 * D : 3 * D, :] = bfloat(grad_v[...])
    vector_sums = jnp.concatenate(
        [sums_one[...], sums_two[...], summed(query_rows), value_sum, jnp.zeros((6, D), f32)], axis=0
    )
    late[3 * D : 3 * D + 32, :] = bfloat(vector_sums)
    late[3 * D + 32 : 2 * half, :] = jnp.zeros((2 * half - 3 * D - 32, D), bf16)
    for copy in [ship(late, n * half, half, sent, kept, half_side, semaphores.at[8 + n]) for n in range(2)]:
        copy.wait()


VMEM_BLOCK = pl.BlockSpec(memory_space=pltpu.VMEM)
SMEM_BLOCK = pl.BlockSpec(memory_space=pltpu.SMEM)
ANY_BLOCK = pl.BlockSpec(memory_space=pl.ANY)
HBM_BLOCK = pl.BlockSpec(memory_space=pltpu.HBM)


class Numbers:
    def __init__(self, numbers, length, memory_length, segments):
        T = segments.shape[1]
        self.refs = [
            (numbers, (0,)), (length, (0,)), (memory_length, (0,)), (numbers, (1,)),
            (segments, (0, 0)), (segments, (0, T - 1)),
        ]

    def __getitem__(self, index):
        ref, at = self.refs[index]
        return ref[at]


def run_kernel(kernel, name, microseconds, out_shapes, small, far, near, scratch, ties=(), out_far=0, anywhere=False):
    kept = out_shapes[: len(out_shapes) - out_far]
    counts = [len(small), len(far), len(near), len(ties), len(kept), out_far, len(scratch), len(near), len(kept), 1]

    def body(*refs):
        parts, at = [], 0
        for count in counts:
            parts.append(refs[at : at + count])
            at += count
        small_refs, far_refs, held, _, outs, own_outs, scratch_refs, copies, results, (semaphores,) = parts
        loads = [
            pltpu.make_async_copy(a, b, semaphores.at[n]) for n, (a, b) in enumerate(zip(held, copies))
        ]
        leaving = {
            n: pltpu.make_async_copy(a, b, semaphores.at[len(loads) + n])
            for n, (a, b) in enumerate(zip(results, outs))
        }
        left = []
        for load in loads:
            load.start()
        waiting = list(loads)

        def ready(count=len(loads)):
            for load in waiting[:count]:
                load.wait()
            del waiting[:count]

        def done(*numbers):
            for n in numbers:
                copy = leaving.pop(n)
                copy.start()
                left.append(copy)

        kernel(ready, done, Numbers(*small_refs), *far_refs, *copies, *results, *own_outs, *scratch_refs)
        ready()
        done(*list(leaving))
        for copy in left:
            copy.wait()

    return pl.pallas_call(
        body,
        out_shape=[jax.ShapeDtypeStruct(shape, kind) for shape, kind in out_shapes],
        in_specs=[SMEM_BLOCK] * len(small)
        + [ANY_BLOCK if anywhere else HBM_BLOCK] * len(far)
        + [ANY_BLOCK if anywhere else HBM_BLOCK] * len(near)
        + [ANY_BLOCK] * len(ties),
        out_specs=[HBM_BLOCK] * len(out_shapes),
        scratch_shapes=[
            *scratch,
            *[pltpu.VMEM(w.shape, w.dtype) for w in near],
            *[pltpu.VMEM(shape, kind) for shape, kind in kept],
            pltpu.SemaphoreType.DMA((len(near) + len(kept),)),
        ],
        compiler_params=pltpu.CompilerParams(vmem_limit_bytes=ROOM),
        cost_estimate=cost(microseconds),
        name=name,
    )(*small, *far, *near, *ties)


def window_scratch(T, D):
    return [
        pltpu.VMEM((4, T, D), bf16),
        pltpu.VMEM((4, TAIL, D), bf16),
        pltpu.VMEM((4, T), f32),
        pltpu.VMEM((4, T), f32),
        pltpu.VMEM((4 * T, 128), f32),
    ]


def self_near(numbers, segments, blocks, weights, vectors, ties=()):
    T, D = segments.shape[1], vectors.shape[1]
    wq, wk, wv = weights
    return run_kernel(
        self_near_kernel, "self_near", 13,
        [((T, D), bf16), ((H, VROWS, T), f32), ((16, 128), f32)],
        numbers, blocks[:3], [segments, vectors, wv, wq, wk],
        window_scratch(T, D)
        + [
            pltpu.VMEM((PAIRS, 4 * T, 128), bf16),
            pltpu.VMEM((H, VROWS, 4 * T), bf16),
            pltpu.VMEM((H, T), f32),
            pltpu.VMEM((H, T, 128), bf16),
            pltpu.SemaphoreType.DMA((8,)),
        ],
        ties,
    )


def self_far(numbers, segments, blocks, weights, vectors, queries, total, reach, opposite, ties=()):
    T, D = queries.shape
    return run_kernel(
        self_far_kernel, "self_far", 7,
        [((T, D), bf16), ((H, T), f32)],
        numbers, blocks, [*weights[1:], segments, vectors, queries, reach, opposite, total],
        window_scratch(T, D)
        + [
            pltpu.VMEM((PAIRS, 4 * T, 128), bf16),
            pltpu.VMEM((H, VROWS, 4 * T), bf16),
            pltpu.VMEM((H, T), f32),
            pltpu.VMEM((H, VROWS, T), f32),
            pltpu.VMEM((D, T), f32),
            pltpu.VMEM((H, T, 128), bf16),
            pltpu.SemaphoreType.DMA((8,)),
        ],
        ties,
    )


def backward_scratch(T, D):
    return window_scratch(T, D) + [
        pltpu.VMEM((PAIRS, 4 * T, 128), bf16),
        pltpu.VMEM((D, 4 * T), bf16),
        pltpu.VMEM((PAIRS, 4 * T, 128), bf16),
        pltpu.VMEM((PAIRS, 4 * T, 128), f32),
        pltpu.VMEM((PAIRS, 4 * T, 128), f32),
        pltpu.VMEM((H, T, 128), bf16),
        pltpu.VMEM((H, T, 128), bf16),
        pltpu.VMEM((H, T), f32),
    ]


def back_far(numbers, segments, blocks, weights, vectors, queries, blended, upstream, lse, opposite, ties=()):
    T, D = queries.shape
    return run_kernel(
        back_far_kernel, "back_far", 8,
        [((T, D), bf16), ((D, D), f32), ((D, D), f32), ((8, D), f32), ((D, T), f32)],
        numbers, blocks[3:],
        [segments, vectors, *weights[1:], queries, upstream, blended, lse, opposite],
        backward_scratch(T, D) + [pltpu.SemaphoreType.DMA((8,))],
        ties,
    )


def back_near(numbers, segments, blocks, weights, vectors, queries, blended, upstream, lse, entering, sums, far, ties=()):
    T, D = queries.shape
    wq, wk, wv = weights
    far_k, far_v, far_sum, far_query_t = far
    rows = 3 * D // 2 + D // 4
    return run_kernel(
        back_near_kernel, "back_near", 22,
        [((T, D), f32), ((T, D), bf16), ((T, D), bf16), ((rows, D), bf16), ((rows, D), bf16)],
        numbers, blocks[:3],
        [
            segments, vectors, wk, wv, queries, upstream, blended, lse, far_query_t,
            wq, entering, far_k, far_v, far_sum, *sums,
        ],
        backward_scratch(T, D)
        + [
            pltpu.VMEM((D, T), f32),
            pltpu.VMEM((D, D), f32),
            pltpu.VMEM((D, D), f32),
            pltpu.VMEM((2 * rows, D), bf16),
            pltpu.SemaphoreType.DMA((10,)),
        ],
        ties, 2,
    )


def pack_kernel(ready, done, numbers, canvas, cotangent, *refs):
    *small, wide, segments, memory_segments, memory, vectors, payload, last, extras, held, semaphores = refs
    T, D = canvas.shape
    here = memory.shape[0]
    arrive = pltpu.make_async_copy(canvas, held, semaphores.at[0])
    arrive.start()
    rows = pltpu.make_async_copy(held, payload.at[pl.ds(0, T)], semaphores.at[3])
    copy = pltpu.make_async_copy(cotangent.at[pl.ds(T - TAIL, TAIL)], last, semaphores.at[1])
    copy.start()
    arrive.wait()
    rows.start()
    ready()

    def padded(row):
        if row.shape[1] == D:
            return row
        return jnp.concatenate([row, jnp.zeros((1, D - row.shape[1]), f32)], axis=1)

    row = lax.broadcasted_iota(jnp.int32, (TAIL, D), 0)
    copy.wait()
    codes = jnp.broadcast_to(padded(segments[...].astype(f32)), (TAIL, D))
    carried = jnp.broadcast_to(widen(last[...])[TAIL - 1 : TAIL], (TAIL, D))
    row_sum = jnp.broadcast_to(summed(held[...]), (TAIL, D))
    rest_of_sum = row_sum - widen(bfloat(row_sum))
    extras[0:TAIL, :] = bfloat(
        jnp.where(
            row == 0, codes,
            jnp.where(row == 1, carried, jnp.where(row == 2, row_sum, jnp.where(row == 3, rest_of_sum, 0.0))),
        )
    )
    extras[TAIL : TAIL + here, :] = memory[...]
    codes = jnp.broadcast_to(padded(memory_segments[...].astype(f32)), (TAIL, D))
    extras[TAIL + here : 2 * TAIL + here, :] = bfloat(jnp.where(row == 0, codes, 0.0))
    rest = pltpu.make_async_copy(extras, payload.at[pl.ds(T, 2 * TAIL + here)], semaphores.at[2])
    rest.start()
    for index, vector in enumerate(small):
        vectors[index : index + 1, :] = widen(vector[...])[None, :]
    values = widen(wide[...])
    for c in range(values.shape[0] // D):
        vectors[len(small) + c : len(small) + c + 1, :] = values[c * D : c * D + D][None, :]
    rows.wait()
    rest.wait()


def pack(numbers, small, wide, segments, memory_segments, memory, canvas, cotangent):
    T, D = canvas.shape
    size = 2 * TAIL + memory.shape[0]
    return run_kernel(
        pack_kernel, "pack", 2,
        [((len(small) + wide.shape[0] // D, D), f32), ((T + size, D), bf16)],
        numbers, [canvas, cotangent], [*small, wide, segments, memory_segments, memory],
        [pltpu.VMEM((TAIL, D), bf16), pltpu.VMEM((size, D), bf16), pltpu.VMEM((T, D), bf16), pltpu.SemaphoreType.DMA((4,))],
        (), 1,
    )


BQ1, BV1, BO1, G1, B1, BQ2, BV2, BO2, G2, B2, BR, G3, B3, BS, BE = range(15)


def smooth_gate(inputs):
    square = inputs * inputs
    bent = jnp.tanh(gelu_scale * inputs * (1.0 + gelu_cubic * square))
    half = 0.5 * (1.0 + bent)
    slope = half + 0.5 * inputs * (1.0 - bent * bent) * (
        gelu_scale * (1.0 + 3.0 * gelu_cubic * square)
    )
    return inputs * half, slope


def norm_forward(inputs):
    average = jnp.mean(inputs, axis=-1, keepdims=True)
    centred = inputs - average
    scaling = lax.rsqrt(jnp.mean(centred * centred, axis=-1, keepdims=True) + epsilon)
    return centred * scaling, scaling


def norm_backward(upstream, gain, normal, scaling):
    scaled = upstream * gain
    return scaling * (
        scaled
        - jnp.mean(scaled, axis=-1, keepdims=True)
        - normal * jnp.mean(scaled * normal, axis=-1, keepdims=True)
    )


def summed(values):
    return jnp.sum(widen(values), axis=0, keepdims=True)


def memory_moves(place, blocks, last_memory, gathered, semaphores, first):
    own, side, middle, middle_far, side_far = blocks
    size = gathered.shape[1]
    begin = own.shape[0] - size
    inner, beside, across, far = neighbours(place)

    def move(block, slot, index):
        return pltpu.make_async_copy(
            block.at[pl.ds(begin, size)], gathered.at[slot], semaphores.at[first + index]
        )

    def run(act):
        for copy in (move(own, place, 0), move(side, beside, 1)):
            act(copy)

        @pl.when(inner)
        def _():
            for copy in (move(middle, across, 2), move(middle_far, far, 3)):
                act(copy)

        @pl.when(jnp.logical_not(inner))
        def _():
            last = pltpu.make_async_copy(last_memory, gathered.at[3 - place], semaphores.at[first + 3])
            for copy in (move(side_far, far, 2), last):
                act(copy)

    return run


def memory_rows(gathered, memory, columns, memory_length):
    count, size, width = gathered.shape
    here = size - TAIL
    lane = lax.broadcasted_iota(jnp.int32, (1, here), 1)
    for b in range(count):
        span = slice(b * here, (b + 1) * here)
        memory[span, :] = gathered[b, 0:here, :]
        code = widen(gathered[b, here : here + 1, 0:here])
        columns[span, :] = as_column(jnp.where(b * here + lane < memory_length, code, -1.0))


def ship(buffer, first, count, sent, kept, side, semaphore):
    half = kept.shape[0]
    part, at = divmod(first, half)
    source = buffer.at[pl.ds(first, count)]

    @pl.when(side == part)
    def _():
        pltpu.make_async_copy(source, kept.at[pl.ds(at, count)], semaphore).start()

    @pl.when(side != part)
    def _():
        pltpu.make_async_copy(source, sent.at[pl.ds(at, count)], semaphore).start()

    return pltpu.make_async_copy(source, kept.at[pl.ds(at, count)], semaphore)


def forward_kernel(
    ready, done, numbers, own, side, middle, middle_far, side_far, last_memory,
    segments, vectors, ck, cv, canvas, blended, wo, cq, co, we, wr, ws, cotangent,
    slots_out, last_out, first_state, normal_out, scaling_out, low_out, query_out, fetched_out,
    lse, second_out, sums, gathered, sent, kept,
    tails, memory, columns, keys, values_t, summit, total,
    blend_t, q_sides, hidden, slope, second, low2, early, semaphores,
):
    T, D = canvas.shape
    M = memory.shape[0]
    FF = we.shape[1]
    place, length, memory_length = numbers[0], numbers[1], numbers[2]
    edges = [
        pltpu.make_async_copy(side.at[pl.ds(T, TAIL)], tails.at[0], semaphores.at[0]),
        pltpu.make_async_copy(middle.at[pl.ds(T, TAIL)], tails.at[1], semaphores.at[1]),
    ]
    bring = memory_moves(
        place, (own, side, middle, middle_far, side_far), last_memory, gathered, semaphores, 2
    )
    bring(start)
    for copy in edges:
        copy.start()
    leaving = []

    half_side = numbers[3]

    def leave(block, index):
        early[pl.ds(index * D, D), :] = block

    def go(*indices):
        for index in indices:
            leaving.append(ship(early, index * D, D, sent, kept, half_side, semaphores.at[6 + index]))

    def vector(index):
        return vectors[index : index + 1, :]

    sums[...] = jnp.zeros_like(sums)
    ready(2)
    code_row = segments[...].astype(f32)

    bring(wait)
    memory_rows(gathered, memory, columns, memory_length)
    done(11)
    ready(2)
    k = bfloat(matmul(memory[...], ck[...]))
    for pair in range(PAIRS):
        keys[pair] = k[:, 128 * pair : 128 * pair + 128]
    bias_t = as_column(vector(BV2))[:, 0:1]
    v_t = bfloat(times_transposed(jnp.transpose(cv[...]), memory[...]) + bias_t)
    for head in range(H):
        values_t[head, 0:HD, :] = v_t[HD * head : HD * head + HD]
        values_t[head, HD:VROWS, :] = jnp.ones((VROWS - HD, M), bf16)

    ready(3)
    first_in = widen(canvas[...]) + matmul(blended[...], wo[...]) + vector(BO1)
    normal, scaling = norm_forward(first_in)
    normal_out[...] = normal
    scaling_out[...] = jnp.broadcast_to(scaling, (T, 128))
    done(3, 4)
    first = normal * vector(G1) + vector(B1)
    low = bfloat(first)
    low_out[...] = low
    ready(1)
    query_out[...] = bfloat((matmul(low, cq[...]) + vector(BQ2)) * 0.125)
    done(5, 6)

    ones_of_heads = head_rows(bf16)
    q_all = query_out[...]
    reach = jnp.max(
        jnp.max(times_transposed(ones_of_heads, q_all * q_all), axis=1, keepdims=True)
        * jnp.max(times_transposed(ones_of_heads, k * k), axis=1, keepdims=True)
    )
    wide = reach > safe_square
    summit[...] = jnp.zeros_like(summit)
    total[...] = jnp.zeros_like(total)
    split_heads(q_all, q_sides)
    tiles = [slice(t, t + TILE) for t in range(0, M, TILE)]

    @pl.when(wide)
    def _():
        summit[...] = jnp.full(summit.shape, masked_score, f32)
        for at in tiles:
            look_at(at, keys, q_sides, columns, code_row, summit)

    for at in tiles:
        blend_at(at, keys, values_t, q_sides, columns, code_row, summit, total)
    fetched = normalise(total, summit, lse, blend_t)
    fetched_out[...] = fetched
    done(7, 8)

    ready(1)
    second_in = first + matmul(fetched, co[...]) + vector(BO2)
    normal2, scaling2 = norm_forward(second_in)
    second[...] = normal2 * vector(G2) + vector(B2)
    low2[...] = bfloat(second[...])
    ready(2)
    third_in = second[...] + vector(BR)
    for c in range(FF // D):
        lanes = slice(c * D, (c + 1) * D)
        before = matmul(low2[...], we[:, lanes]) + vector(BE + c)
        gate, bend = smooth_gate(before)
        gate = bfloat(gate)
        hidden[:, lanes] = gate
        slope[:, lanes] = bend
        third_in += matmul(gate, wr[lanes, :])
    normal3, scaling3 = norm_forward(third_in)
    states = bfloat(normal3 * vector(G3) + vector(B3))
    first_state[...] = states[0:TAIL]

    for copy in edges:
        copy.wait()
    ready()
    inner = jnp.logical_or(place == 1, place == 2)
    beside_tail, across_tail = widen(tails[0]), widen(tails[1])
    after_code = jnp.where(place == 1, across_tail[0:1, 0:1], beside_tail[0:1, 0:1])
    before_code = jnp.where(place == 2, across_tail[0:1, T - 1 : T], beside_tail[0:1, T - 1 : T])
    before_row = jnp.where(place == 2, across_tail[1:2, :], beside_tail[1:2, :])
    lane = lax.broadcasted_iota(jnp.int32, (8, T), 1)
    codes8 = jnp.broadcast_to(code_row, (8, T))
    live = jnp.where(place * T + lane < length, codes8, -1.0)
    next_code = jnp.where(lane == T - 1, after_code, pltpu.roll(live, T - 1, 1))
    valid8 = jnp.where(
        jnp.logical_and(next_code == codes8, place * T + lane + 1 < length), 1.0, 0.0
    )
    valid = as_column(valid8[0:1, :])[:, 0:1]
    last_valid = jnp.where(
        jnp.logical_and(before_code == code_row[:, 0:1], jnp.logical_and(place > 0, place * T < length)),
        1.0, 0.0,
    )
    row = lax.broadcasted_iota(jnp.int32, (T, D), 0)
    following = bfloat(jnp.where(row == T - 1, 0.0, pltpu.roll(widen(states), T - 1, 0)))
    raw = matmul(states, ws[0:D, :]) + vector(BS) + matmul(following, ws[D : 2 * D, :])
    slots_out[...] = bfloat(raw * valid)
    last_out[...] = jnp.concatenate(
        [raw[T - 1 : T], jnp.broadcast_to(valid[T - 1 : T], (1, D)), jnp.zeros((6, D), f32)], axis=0
    )
    done(0, 1, 2)
    masked = widen(cotangent[...]) * valid
    shifted = jnp.where(row == 0, before_row * last_valid, pltpu.roll(masked, 1, 0))
    masked_low, shifted_low = bfloat(masked), bfloat(shifted)
    upstream = times_transposed(masked_low, ws[0:D, :]) + widen(
        bfloat(times_transposed(shifted_low, ws[D : 2 * D, :]))
    )
    states_t = jnp.transpose(states)
    leave(bfloat(matmul(states_t, masked_low)), 0)
    leave(bfloat(matmul(states_t, shifted_low)), 1)
    sums[0:1, :] = summed(masked)

    third_grad = norm_backward(upstream, vector(G3), normal3, scaling3)
    sums[1:2, :] = summed(upstream * normal3)
    sums[2:3, :] = summed(upstream)
    third_low = bfloat(third_grad)
    sums[3:4, :] = summed(third_low)
    low2_t = jnp.transpose(low2[...])
    second_up = third_grad
    for c in range(FF // D):
        lanes = slice(c * D, (c + 1) * D)
        leave(bfloat(matmul(jnp.transpose(hidden[:, lanes]), third_low)), 2 + FF // D + c)
        hidden_grad = bfloat(times_transposed(third_low, wr[lanes, :]))
        before_grad = bfloat(widen(hidden_grad) * slope[:, lanes])
        leave(bfloat(matmul(low2_t, before_grad)), 2 + c)
        sums[4 + c : 5 + c, :] = summed(before_grad)
        second_up += times_transposed(before_grad, we[:, lanes])
        if c == FF // D // 2:
            go(0, 1, *[2 + n for n in range(c)], *[2 + FF // D + n for n in range(c)])
    second_out[...] = norm_backward(second_up, vector(G2), normal2, scaling2)
    sums[8:9, :] = summed(second_up * normal2)
    sums[9:10, :] = summed(second_up)
    rest = range(FF // D // 2, FF // D)
    go(*[2 + n for n in rest], *[2 + FF // D + n for n in rest])
    for copy in leaving:
        copy.wait()


def backward_kernel(
    ready, done, numbers,
    second_grad, co, segments, vectors, gathered, query, ck, cv, fetched, lse, cq, normal, scaling, wo, low,
    blended, first_state, wv, self_lse,
    first_grad_out, upstream_out, sums, sent, kept, memory_goes, memory_stays,
    memory, columns, keys, keys_t, values, grad_keys, grad_values, query_t, upstream2, q_sides, u_sides, fixes, late, memory_out, semaphores,
):
    T, D = low.shape
    M = memory.shape[0]
    half_side = numbers[3]
    sums[...] = jnp.zeros_like(sums)
    ready(2)
    low_grad = bfloat(second_grad[...])
    upstream2[...] = bfloat(times_transposed(low_grad, co[...]))
    ready(4)
    code_row = segments[...].astype(f32)
    gain = vectors[G1 : G1 + 1, :]
    memory_rows(gathered, memory, columns, numbers[2])
    split_heads(query[...], q_sides)
    ready(2)
    k = bfloat(matmul(memory[...], ck[...]))
    v = bfloat(matmul(memory[...], cv[...]) + vectors[BV2 : BV2 + 1, :])
    for pair in range(PAIRS):
        keys[pair] = k[:, 128 * pair : 128 * pair + 128]
        values[pair] = v[:, 128 * pair : 128 * pair + 128]
    keys_t[...] = jnp.transpose(k)
    ready(2)
    fixes[...] = row_corrections(upstream2[...], fetched[...])
    split_heads(upstream2[...], u_sides)
    query_t[...] = jnp.zeros_like(query_t)
    for tile in range(M // TILE):
        step_back(
            slice(tile * TILE, (tile + 1) * TILE), keys, keys_t, values, q_sides, u_sides, columns,
            code_row, lse, fixes, query_t, grad_keys, grad_values,
        )
    query_rows = bfloat(jnp.transpose(query_t[...])) * 0.125
    ready()
    first_up = second_grad[...] + times_transposed(query_rows, cq[...])
    first_grad = norm_backward(first_up, gain, normal[...], scaling[:, 0:1])
    first_grad_out[...] = first_grad
    first_low = bfloat(first_grad)
    upstream_out[...] = bfloat(times_transposed(first_low, wo[...]))
    done(0, 1)
    gk, gv = tile_grads(slice(0, M), grad_keys, grad_values)
    part = bfloat(times_transposed(gk, ck[...]) + times_transposed(gv, cv[...]))
    count, size, _ = memory_out.shape
    here = size - TAIL
    place = numbers[0]
    tail = lax.broadcasted_iota(jnp.int32, (TAIL, D), 0)
    terms = jnp.broadcast_to(masked_terms(self_lse[...], upstream_out[...]), (TAIL, D))
    opposite_row = times_transposed(bfloat(terms), wv[...])
    for b in range(count):
        memory_out[b, 0:here, :] = part[b * here : (b + 1) * here]
        rows = jnp.where(jnp.logical_and(tail == 0, place == b + 1), widen(first_state[...]), 0.0)
        rows += jnp.where(
            jnp.logical_and(tail == 1, jnp.logical_and(is_outer(place), place == 3 - b)), opposite_row, 0.0
        )
        memory_out[b, here:size, :] = bfloat(rows)
    leaving = []
    for b in range(count):
        copies = [
            pltpu.make_async_copy(memory_out.at[b], half_out.at[b // 2], semaphores.at[2 + b])
            for half_out in (memory_stays, memory_goes)
        ]

        @pl.when(lax.rem(place, 2) == b % 2)
        def _():
            copies[0].start()

        @pl.when(lax.rem(place, 2) != b % 2)
        def _():
            copies[1].start()

        leaving.append(copies[0])
    memory_t = jnp.transpose(memory[...])
    late[0:D, :] = bfloat(matmul(jnp.transpose(low[...]), query_rows))
    late[D : 2 * D, :] = bfloat(matmul(memory_t, gk))
    late[2 * D : 3 * D, :] = bfloat(matmul(memory_t, gv))
    late[3 * D : 4 * D, :] = bfloat(matmul(jnp.transpose(fetched[...]), low_grad))
    late[4 * D : 5 * D, :] = bfloat(matmul(jnp.transpose(blended[...]), first_low))
    half = 5 * D // 2
    leaving += [ship(late, n * half, half, sent, kept, half_side, semaphores.at[n]) for n in range(2)]
    sums[0:1, :] = summed(low_grad)
    sums[1:2, :] = summed(query_rows)
    sums[2:3, :] = summed(gv)
    sums[3:4, :] = summed(first_up * normal[...])
    sums[4:5, :] = summed(first_up)
    sums[5:6, :] = summed(first_low)
    done(2)
    for copy in leaving:
        copy.wait()


def middle_forward(numbers, segments, canvas, blended, cotangent, vectors, blocks, last_memory, weights, ties=()):
    T, D = canvas.shape
    wo, ck, cv, cq, co, we, wr, ws = weights
    FF = we.shape[1]
    here = last_memory.shape[0] - TAIL
    M = 4 * here
    rows = 2 * D + 2 * FF
    return run_kernel(
        forward_kernel, "middle_forward", 24,
        [
            ((T, D), bf16), ((8, D), f32), ((TAIL, D), bf16), ((T, D), f32), ((T, 128), f32), ((T, D), bf16),
            ((T, D), bf16), ((T, D), bf16), ((H, T), f32), ((T, D), f32),
            ((16, D), f32), ((4, here + TAIL, D), bf16), ((rows // 2, D), bf16), ((rows // 2, D), bf16),
        ],
        numbers, [*blocks, last_memory],
        [segments, vectors, ck, cv, canvas, blended, wo, cq, co, we, wr, ws, cotangent],
        [
            pltpu.VMEM((2, TAIL, D), bf16),
            pltpu.VMEM((M, D), bf16),
            pltpu.VMEM((M, 128), f32),
            pltpu.VMEM((PAIRS, M, 128), bf16),
            pltpu.VMEM((H, VROWS, M), bf16),
            pltpu.VMEM((H, T), f32),
            pltpu.VMEM((H, VROWS, T), f32),
            pltpu.VMEM((D, T), f32),
            pltpu.VMEM((H, T, 128), bf16),
            pltpu.VMEM((T, FF), bf16),
            pltpu.VMEM((T, FF), f32),
            pltpu.VMEM((T, D), f32),
            pltpu.VMEM((T, D), bf16),
            pltpu.VMEM((rows, D), bf16),
            pltpu.SemaphoreType.DMA((6 + rows // D,)),
        ],
        ties, 2,
    )


def middle_backward(numbers, segments, blended, gathered, vectors, saved, weights, ties=()):
    T, D = blended.shape
    M = gathered.shape[0] * (gathered.shape[1] - TAIL)
    rows = 5 * D // 2
    part = (gathered.shape[0] // 2, *gathered.shape[1:])
    normal, scaling, low, query, fetched, lse, second_grad, first_state, self_lse = saved
    wo, cq, ck, cv, co, wv = weights
    return run_kernel(
        backward_kernel, "middle_backward", 16,
        [
            ((T, D), f32), ((T, D), bf16), ((8, D), f32), ((rows, D), bf16), ((rows, D), bf16),
            (part, bf16), (part, bf16),
        ],
        numbers, [],
        [
            second_grad, co, segments, vectors, gathered, query, ck, cv, fetched, lse,
            cq, normal, scaling, wo, low, blended, first_state, wv, self_lse,
        ],
        [
            pltpu.VMEM((M, D), bf16),
            pltpu.VMEM((M, 128), f32),
            pltpu.VMEM((PAIRS, M, 128), bf16),
            pltpu.VMEM((D, M), bf16),
            pltpu.VMEM((PAIRS, M, 128), bf16),
            pltpu.VMEM((PAIRS, M, 128), f32),
            pltpu.VMEM((PAIRS, M, 128), f32),
            pltpu.VMEM((D, T), f32),
            pltpu.VMEM((T, D), bf16),
            pltpu.VMEM((H, T, 128), bf16),
            pltpu.VMEM((H, T, 128), bf16),
            pltpu.VMEM((H, T), f32),
            pltpu.VMEM((2 * rows, D), bf16),
            pltpu.VMEM(gathered.shape, bf16),
            pltpu.SemaphoreType.DMA((6,)),
        ],
        ties, 4,
    )


def pieces(start, count, half):
    found = []
    for part in range(2):
        low, high = max(start, part * half), min(start + count, (part + 1) * half)
        if low < high:
            found.append((part, low - part * half, low - start, high - low))
    return found


def unpack_chunks(layout, counts, half):
    chunks, held = [], 0
    for number, (starts, count) in enumerate(zip(layout, counts)):
        for column, start_row in enumerate(starts):
            for part, there, here, rows in pieces(start_row, count, half):
                for at in range(0, rows, 512):
                    size = min(512, rows - at)
                    chunks.append((number, column, here + at, part, there + at, held, size))
                    held += size
    return chunks, held


def unpack_kernel(layout, ready, done, numbers, mine, came, *refs):
    *outs, held, semaphores = refs
    half, D = mine.shape
    half_side = numbers[3]
    chunks, _ = unpack_chunks(layout, [out.shape[0] for out in outs], half)
    moves = []
    for n, (_, _, _, part, there, at, size) in enumerate(chunks):
        sources = [
            pltpu.make_async_copy(block.at[pl.ds(there, size)], held.at[pl.ds(at, size)], semaphores.at[n])
            for block in (mine, came)
        ]

        @pl.when(half_side == part)
        def _():
            sources[0].start()

        @pl.when(half_side != part)
        def _():
            sources[1].start()

        moves.append(sources[0])
    for n, (number, column, here, _, _, at, size) in enumerate(chunks):
        moves[n].wait()
        outs[number][here : here + size, column * D : column * D + D] = widen(held[at : at + size, :])
        if n + 1 == len(chunks) or chunks[n + 1][0] != number:
            done(number)


def unpack(numbers, name, mine, came, layout, ties=()):
    half, D = mine.shape
    starts = [first for _, first in layout]
    chunks, held = unpack_chunks(starts, [count for count, _ in layout], half)
    return run_kernel(
        functools.partial(unpack_kernel, starts), name, 4,
        [((count, D * len(first)), f32) for count, first in layout],
        numbers, [mine, came], [],
        [pltpu.VMEM((held, D), bf16), pltpu.SemaphoreType.DMA((len(chunks),))], ties, 0, True,
    )


def finish_kernel(
    ready, done, numbers, memory_stays, memory_came, last_slot, slots, bottom, base, onward, outward,
    memory_grad, slots_out, canvas_grad,
):
    T, D = slots.shape
    here = memory_grad.shape[0]
    ready(4)
    summed_rows = widen(memory_stays[...]) + widen(memory_came[...])
    memory_grad[...] = summed_rows[0:here]
    done(0)
    next_state = bfloat(summed_rows[here : here + TAIL])
    ready(1)
    last_row = (last_slot[0:1, :] + matmul(next_state, bottom[...])[0:1]) * last_slot[1:2, :]
    row = lax.broadcasted_iota(jnp.int32, (TAIL, D), 0)
    slots_out[0 : T - TAIL, :] = slots[0 : T - TAIL, :]
    slots_out[T - TAIL : T, :] = bfloat(
        jnp.where(row == TAIL - 1, last_row, widen(slots[T - TAIL : T, :]))
    )
    done(1)
    ready()
    canvas_grad[...] = base[...] + summed_rows[here + 1 : here + 2] + widen(onward[...]) + widen(outward[...])


def finish(numbers, memory_stays, memory_came, last_slot, slots, bottom, base, onward, outward, ties=()):
    T, D = slots.shape
    return run_kernel(
        finish_kernel, "finish", 3,
        [((memory_stays.shape[0] - TAIL, D), f32), ((T, D), bf16), ((T, D), f32)],
        numbers, [], [memory_stays, memory_came, last_slot, slots, bottom, base, onward, outward], [], ties,
    )


SIDE = [(0, 1), (1, 0), (2, 3), (3, 2)]
MIDDLE = [(1, 2), (2, 1)]
OUTWARD = [(1, 0), (2, 3)]
INWARD = [(0, 1), (3, 2)]


def routes():
    bits = [("rows", 1 << b) for b in range((lax.axis_size("rows") - 1).bit_length())]
    along = [("seq", 1 << b) for b in range((lax.axis_size("seq") - 1).bit_length())]
    return bits[0], bits[1:], bits[:0:-1], along


def swap(block, step):
    axis, bit = step
    return lax.ppermute(block, axis, [(i, i ^ bit) for i in range(lax.axis_size(axis))])


def side_of(step):
    axis, bit = step
    return jnp.where((lax.axis_index(axis) & bit) != 0, 1, 0)


def halves(terms, step):
    side = side_of(step)
    half = terms[0].shape[0] // 2

    def part(which):
        pieces = [widen(lax.dynamic_slice_in_dim(t, which * half, half)) for t in terms]
        return bfloat(sum(pieces[1:], pieces[0]))

    return part(1 - side), part(side)


def ordered(block, came, step):
    side = side_of(step) == 1
    return jnp.where(side, came, block), jnp.where(side, block, came)


class Order:
    def __init__(self):
        self.last = []

    def made(self, *values):
        self.last = list(values)

    def after(self, *values):
        if not self.last:
            return values
        values, _ = lax.optimization_barrier((values, tuple(self.last)))
        return values


class Summing:
    def __init__(self, order, sent, kept, split):
        self.order = order
        self.split = split
        self.steps = self.run(sent, kept)
        self.whole = None
        next(self.steps)

    def step(self):
        if self.whole is not None:
            return
        try:
            self.order.made(*next(self.steps))
        except StopIteration as end:
            self.whole = end.value

    def finish(self):
        while self.whole is None:
            self.step()
        return self.whole

    def take(self, blocks):
        return self.order.after(*blocks)

    def run(self, sent, kept):
        first, up, down, along = routes()
        came = swap(sent, first)
        yield [sent]
        (came,) = self.take([came])
        size = kept.shape[0]
        if self.split == 2:
            ways = [(up, 0, size // 2), (down, size // 2, size // 2)]
        else:
            ways = [(down if self.split else up, 0, size)]
        lanes = [[kept[at : at + n], came[at : at + n]] for _, at, n in ways]
        for number in range(len(up)):
            parts = [halves(terms, way[number]) for terms, (way, _, _) in zip(lanes, ways)]
            came = [swap(goes, way[number]) for (goes, _), (way, _, _) in zip(parts, ways)]
            yield [goes for goes, _ in parts]
            came = self.take(came)
            lanes = [[stays, block] for (_, stays), block in zip(parts, came)]
        parts = [halves(terms, along[0]) for terms in lanes]
        cut = parts[0][0].shape[0]
        goes = jnp.concatenate([p[0] for p in parts], axis=0)
        stays = jnp.concatenate([p[1] for p in parts], axis=0)
        came = swap(goes, along[0])
        yield [goes]
        (came,) = self.take([came])
        mine = bfloat(widen(stays) + widen(came))
        for step in along[1:]:
            came = swap(mine, step)
            yield [mine]
            (came,) = self.take([came])
            mine = bfloat(widen(mine) + widen(came))
        came = swap(mine, along[0])
        yield [mine]
        (came,) = self.take([came])
        low, high = ordered(mine, came, along[0])
        lanes = [
            jnp.concatenate([low[n * cut : n * cut + cut], high[n * cut : n * cut + cut]], axis=0)
            for n in range(len(ways))
        ]
        for number in range(len(up) - 1, -1, -1):
            came = [swap(block, way[number]) for block, (way, _, _) in zip(lanes, ways)]
            yield lanes
            came = self.take(came)
            lanes = [
                jnp.concatenate(ordered(block, other, way[number]), axis=0)
                for block, other, (way, _, _) in zip(lanes, came, ways)
            ]
        block = lanes[0] if len(lanes) == 1 else jnp.concatenate(lanes, axis=0)
        came = swap(block, first)
        yield [block]
        return block, came


def entry_halves(block, step, bit):
    count = block.shape[0]
    grouped = block.reshape(count // (2 * bit), 2, bit, *block.shape[1:])
    side = side_of(step)
    take = lambda which: lax.dynamic_index_in_dim(grouped, which, 1, False).reshape(
        count // 2, *block.shape[1:]
    )
    return take(1 - side), take(side)


def shards(
    canvas,
    memory,
    cotangent,
    canvas_lengths,
    canvas_segments,
    memory_segments,
    memory_lengths,
    self_query,
    self_key,
    self_value,
    self_output,
    self_query_bias,
    self_value_bias,
    self_output_bias,
    first_gain,
    first_bias,
    cross_query,
    cross_key,
    cross_value,
    cross_output,
    cross_query_bias,
    cross_value_bias,
    cross_output_bias,
    second_gain,
    second_bias,
    expand_weight,
    expand_bias,
    reduce_weight,
    reduce_bias,
    third_gain,
    third_bias,
    slot_weight,
    slot_bias,
):
    place = lax.axis_index("seq")
    tokens_here = canvas.shape[1]
    width = canvas.shape[2]
    wide = expand_weight.shape[1]
    row = canvas[0]
    numbers = [
        jnp.stack([place, side_of(routes()[0])]).astype(jnp.int32),
        canvas_lengths, memory_lengths, canvas_segments,
    ]
    vectors, payload = pack(
        numbers,
        (
            self_query_bias, self_value_bias, self_output_bias, first_gain, first_bias,
            cross_query_bias, cross_value_bias, cross_output_bias, second_gain, second_bias,
            reduce_bias, third_gain, third_bias, slot_bias,
        ),
        expand_bias, canvas_segments, memory_segments, memory[0], row, cotangent[0],
    )
    side, middle = lax.ppermute(payload, "seq", SIDE), lax.ppermute(payload, "seq", MIDDLE)
    opposite = lax.ppermute(payload[tokens_here : tokens_here + TAIL], "seq", [(0, 3), (3, 0)])
    blocks = (
        payload, side, middle, lax.ppermute(side, "seq", MIDDLE), lax.ppermute(middle, "seq", OUTWARD)
    )
    last_memory = lax.ppermute(blocks[3][tokens_here + TAIL :], "seq", OUTWARD)
    projections = (self_query, self_key, self_value)

    queries, total, reach = self_near(numbers, canvas_segments, blocks, projections, vectors)
    blended, masses = self_far(
        numbers, canvas_segments, blocks, projections, vectors, queries, total, reach, opposite
    )
    (
        slots, last_slot, first_state, normal, scaling, low, cross_rows, fetched, cross_masses,
        second_grad, early_sums, gathered, early_sent, early_kept,
    ) = middle_forward(
        numbers, canvas_segments, row, blended, cotangent[0], vectors, blocks, last_memory,
        (self_output, cross_key, cross_value, cross_query, cross_output, expand_weight, reduce_weight, slot_weight),
    )
    order = Order()
    early = Summing(order, early_sent, early_kept, 2)
    early.step()
    first_grad, blended_grad, later_sums, later_sent, later_kept, memory_goes, memory_stays = middle_backward(
        numbers, canvas_segments, blended, gathered, vectors,
        (normal, scaling, low, cross_rows, fetched, cross_masses, second_grad, first_state, masses),
        (self_output, cross_query, cross_key, cross_value, cross_output, self_value), order.last,
    )
    order.made(later_sums)
    early.step()
    later = Summing(order, later_sent, later_kept, LATER_SPLIT)
    far_part, *far = back_far(
        numbers, canvas_segments, blocks, projections, vectors, queries, blended, blended_grad, masses,
        opposite, order.last,
    )
    order.made(far[2])
    from_side = lax.ppermute(far_part, "seq", INWARD)
    from_middle = lax.ppermute(far_part, "seq", MIDDLE)
    near_step, far_step = routes()[3]
    memory_came = swap(memory_goes, near_step)
    early.step()
    (memory_came,) = order.after(memory_came)
    half_sum = bfloat(widen(memory_stays) + widen(memory_came))
    memory_goes, memory_stays = entry_halves(half_sum, far_step, 1)
    memory_came = swap(memory_goes, far_step)
    order.made(*order.last, memory_goes)
    later.step()
    canvas_base, middle_part, side_part, last_sent, last_kept = back_near(
        numbers, canvas_segments, blocks, projections, vectors, queries, blended, blended_grad, masses,
        first_grad, (early_sums, later_sums), far, order.last,
    )
    order.made(last_sent)
    last = Summing(order, last_sent, last_kept, LAST_SPLIT)
    finals = {}
    turns = {"E": early, "M": later, "S": last}
    for turn in TURNS:
        if turn in turns:
            turns[turn].step()
        elif turn == "1":
            from_side, from_middle = order.after(from_side, from_middle)
            middle_part = bfloat(widen(middle_part) + widen(from_side))
            side_part = bfloat(widen(side_part) + widen(from_middle))
            onward = lax.ppermute(middle_part, "seq", MIDDLE)
            outward = lax.ppermute(side_part, "seq", SIDE)
            order.made(middle_part, side_part)
        elif turn == "s":
            *self_grads, sums = unpack(
                numbers, "last_out", *last.finish(),
                [(width, [c * width]) for c in range(3)] + [(32, [3 * width])], order.last,
            )
            order.made(sums)
        elif turn == "e":
            count = 2 * width
            grad_slot, grad_expand, grad_reduce = unpack(
                numbers, "early_out", *early.finish(),
                [
                    (count, [0]),
                    (width, list(range(count, count + wide, width))),
                    (wide, [count + wide]),
                ],
                order.last,
            )
            order.made(grad_slot)
        elif turn == "m":
            cross_grads = unpack(
                numbers, "later_out", *later.finish(),
                [(width, [c * width]) for c in range(5)], order.last,
            )
            order.made(cross_grads[0])
        elif turn == "c":
            memory_grad, slots, canvas_grad = finish(
                numbers, memory_stays[0], memory_came[0], last_slot, slots, slot_weight[width:],
                canvas_base, onward, outward, order.last,
            )
            order.made(memory_grad)
    return (
        slots[None],
        canvas_grad[None],
        memory_grad[None],
        self_grads[0],
        self_grads[1],
        self_grads[2],
        cross_grads[4],
        sums[24],
        sums[25],
        sums[21],
        sums[19],
        sums[20],
        cross_grads[0],
        cross_grads[1],
        cross_grads[2],
        cross_grads[3],
        sums[17],
        sums[18],
        sums[16],
        sums[8],
        sums[9],
        grad_expand,
        sums[4:8].reshape(-1),
        grad_reduce,
        sums[3],
        sums[1],
        sums[2],
        grad_slot,
        sums[0],
    )


def solution(mesh):
    placed = (
        P("rows", "seq", None),
        P("rows", "seq", None),
        P("rows", "seq", None),
        P("rows"),
        P("rows", "seq"),
        P("rows", "seq"),
        P("rows"),
        P(),
        P(),
        P(),
        P(),
        P(),
        P(),
        P(),
        P(),
        P(),
        P(),
        P(),
        P(),
        P(),
        P(),
        P(),
        P(),
        P(),
        P(),
        P(),
        P(),
        P(),
        P(),
        P(),
        P(),
        P(),
        P(),
    )
    return jax.shard_map(
        shards,
        mesh=mesh,
        in_specs=placed,
        out_specs=(
            P("rows", "seq", None),
            P("rows", "seq", None),
            P("rows", "seq", None),
            P(),
            P(),
            P(),
            P(),
            P(),
            P(),
            P(),
            P(),
            P(),
            P(),
            P(),
            P(),
            P(),
            P(),
            P(),
            P(),
            P(),
            P(),
            P(),
            P(),
            P(),
            P(),
            P(),
            P(),
            P(),
            P(),
        ),
        check_vma=False,
    )
```
